512 devices in a mesh: wide: 64 (over y, x, core), narrow: 8 (over z).
Axes of the slice: x: 4, y: 8, z: 8, core: 2. Of those that a mesh axis runs over, the one named last changes fastest.
Arguments:
- source: float32 [256, 128, 128], P('wide', 'narrow'), may hold values from -120 to 120
- row_scale: float32 [256, 128, 128], P('wide', 'narrow'), may hold values from 0.5 to 2
- shift_field: float32 [256, 128, 128], P('wide', 'narrow'), may hold values from 0.03 to 1
Outputs:
- correction: float32 [256, 128, 128], P('wide', 'narrow')
The draws below stay inside these ranges and needn't reach their ends.
All inputs are finite; a program needn't handle non-finite values.
Results may differ from the reference program's by a relative error of at most 0.0001.
Values sent between devices are 32-bit elements; how exact they have to be, the bound alone decides.
No kernel may reach another device: no remote copies, remote signals or barrier semaphores. Data moves between devices by JAX's collectives and lax.ppermute only.
A program may use at most 64 MiB of HBM per device.

```python
import math
import jax
import jax.numpy as jnp

PRE = 2
POST = 2
COARSE = 4
NX = 256
NY = 128
NZ = 128


def draw_shift_field(key, part):
    key = jax.random.fold_in(key, 7)
    cell_key, block_key = jax.random.split(key)
    rough = jnp.exp(jax.random.uniform(cell_key, (NX, NY, NZ), jnp.float32, jnp.log(0.3), 0.0))
    blocks = jnp.exp(jax.random.uniform(block_key, (NX // 4, NY // 4, NZ // 4), jnp.float32, jnp.log(0.1), 0.0))
    blocks = jnp.repeat(jnp.repeat(jnp.repeat(blocks, 4, axis=0), 4, axis=1), 4, axis=2)
    return jnp.clip(rough * blocks, 0.03, 1.0).astype(jnp.float32)


def block_scale(stream_key, shape, shards, low, largest):
    loudness = 1.0
    for dim, blocks in shards:
        steps = jax.random.uniform(jax.random.fold_in(jax.random.fold_in(stream_key, 6), dim), (blocks,), jnp.float32, low / len(shards), largest / len(shards))
        loudness = loudness * jnp.repeat(jnp.exp(steps), shape[dim] // blocks).reshape((-1,) + (1,) * (len(shape) - 1 - dim))
    return loudness


def centred(key, shape, scale, reach, shards=(), kind=jnp.bfloat16):
    result = jax.random.normal(key, shape, jnp.float32) * scale
    if len(shards) > 0:
        result = block_scale(key, shape, shards, -0.22, 0.18) * result
    return jnp.clip(result, min=-reach, max=reach).astype(kind)


def setup_inputs(seed: int = 0) -> dict:
    arg_keys = jax.random.split(jax.random.key(seed), 4)
    source = centred(arg_keys[0], (NX, NY, NZ), 20.0, 120.0, ((0, 64), (1, 8)), jnp.float32)
    row_scale = jnp.clip(jnp.exp(math.log(2.0) - 1.3862944 * jax.random.uniform(arg_keys[1], (NX, NY, NZ), jnp.float32) ** block_scale(arg_keys[1], (NX, NY, NZ), ((0, 64), (1, 8)), -0.2, 0.2)), 0.5, 2.0)
    shift_field = draw_shift_field(jax.random.fold_in(arg_keys[3], 71), 0)
    return dict(source=source, row_scale=row_scale, shift_field=shift_field)


DAMPING = 0.8


def box_sum(padded):
    total = padded[:-2] + padded[1:-1] + padded[2:]
    total = total[:, :-2] + total[:, 1:-1] + total[:, 2:]
    return total[:, :, :-2] + total[:, :, 1:-1] + total[:, :, 2:]


def operate(field, padded, row_scale, shift_field, level_scale):
    return level_scale * row_scale * (27.0 * field - box_sum(padded)) + shift_field * field


def coarsen(field):
    sx, sy, sz = field.shape
    return field.reshape(sx // 2, 2, sy // 2, 2, sz // 2, 2).mean(axis=(1, 3, 5))


def refine(field):
    sx, sy, sz = field.shape
    spread = jnp.broadcast_to(field[:, None, :, None, :, None], (sx, 2, sy, 2, sz, 2))
    return spread.reshape(2 * sx, 2 * sy, 2 * sz)


def smooth(field, rhs, row_scale, shift_field, level_scale, count):
    diagonal = 26.0 * level_scale * row_scale + shift_field
    for repeat in range(count):
        image = operate(field, jnp.pad(field, 1), row_scale, shift_field, level_scale)
        field = field + DAMPING * (rhs - image) / diagonal
    return field


def min_residual(rhs, row_scale, shift_field, level_scale, count):
    diagonal = 26.0 * level_scale * row_scale + shift_field
    field = jnp.zeros_like(rhs)
    remain = rhs
    for repeat in range(count):
        search = remain / diagonal
        image = operate(search, jnp.pad(search, 1), row_scale, shift_field, level_scale)
        alpha = jnp.sum(image * remain) / jnp.sum(image * image)
        field = field + alpha * search
        remain = remain - alpha * image
    return field


def residual_of(field, rhs, row_scale, shift_field, level_scale):
    return rhs - operate(field, jnp.pad(field, 1), row_scale, shift_field, level_scale)


def reference(source, row_scale, shift_field):
    scale_one = coarsen(row_scale)
    shift_one = coarsen(shift_field)
    scale_two = coarsen(scale_one)
    shift_two = coarsen(shift_one)
    fine_iter = smooth(jnp.zeros_like(source), source, row_scale, shift_field, 1.0, PRE)
    rhs_one = coarsen(residual_of(fine_iter, source, row_scale, shift_field, 1.0))
    middle_iter = smooth(jnp.zeros_like(rhs_one), rhs_one, scale_one, shift_one, 0.25, PRE)
    rhs_two = coarsen(residual_of(middle_iter, rhs_one, scale_one, shift_one, 0.25))
    coarse_iter = min_residual(rhs_two, scale_two, shift_two, 0.0625, COARSE)
    middle_iter = smooth(middle_iter + refine(coarse_iter), rhs_one, scale_one, shift_one, 0.25, POST)
    return smooth(fine_iter + refine(middle_iter), source, row_scale, shift_field, 1.0, POST)
```

```python
import functools

import jax
import jax.numpy as jnp
from jax import lax
from jax.experimental import pallas as pl
from jax.experimental.pallas import tpu as pltpu
from jax.sharding import Mesh, PartitionSpec as P

COARSE = 4
DAMPING = 0.8
F32 = jnp.float32


def dot(a, b):
    high = a.astype(jnp.bfloat16)
    rest = a - high.astype(F32)
    middle = rest.astype(jnp.bfloat16)
    low = (rest - middle.astype(F32)).astype(jnp.bfloat16)
    parts = lax.dot_general(
        jnp.concatenate([high, middle, low], axis=0),
        b.astype(jnp.bfloat16),
        (((1,), (0,)), ((), ())),
        preferred_element_type=F32,
    )
    n = a.shape[0]
    return parts[:n] + parts[n : 2 * n] + parts[2 * n :]


def iota(shape, dim):
    return lax.broadcasted_iota(jnp.int32, shape, dim)


def ones_where(cond, value=1.0):
    return jnp.where(cond, jnp.float32(value), jnp.float32(0.0))


def lane_box(v, period):
    axis = v.ndim - 1
    lane = iota(v.shape[-2:], 1) % period
    below = jnp.where(lane > 0, pltpu.roll(v, 1, axis), 0.0)
    above = jnp.where(lane < period - 1, pltpu.roll(v, 127, axis), 0.0)
    return v + below + above


def relax_weight(scale, shift, level_scale):
    inside = scale > 0.25
    diag = jnp.where(inside, 26.0 * level_scale * scale + shift, 1.0)
    return jnp.where(inside, DAMPING / diag, 0.0)


def fine_apply(v, scale, shift):
    rows = v.shape[1]
    box = v[:-2] + v[1:-1] + v[2:]
    box = box + pltpu.roll(box, 1, 1) + pltpu.roll(box, rows - 1, 1)
    box = lane_box(box, 128)
    mid = v[1:-1]
    return scale * (27.0 * mid - box) + shift * mid


def pair_planes(quads, rows_ref):
    parts = []
    for k, t in enumerate(quads):
        halves = []
        for i in (0, 2):
            at = 40 * (2 * k + i // 2)
            rows_ref[at : at + 40] = t[i] + t[i + 1]
            halves.append(
                rows_ref[pl.ds(at + 4, 16, stride=2)] + rows_ref[pl.ds(at + 5, 16, stride=2)]
            )
        parts.append(jnp.concatenate(halves, axis=1))
    lane, out = iota((256, 128), 0), iota((256, 128), 1)
    pack = ones_where(lane // 2 == out, 0.125)
    return dot(jnp.concatenate(parts, axis=0), pack).reshape(len(quads), 16, 128)


def fine_kernel(
    own_ref, mate_ref, face_ref, iter_ref, field_ref, piece_ref, one_ref, coef_rows, rows_ref
):
    left = lax.axis_index("c") == 0
    blocks = []
    for k in range(3):
        face, mate = face_ref[k], mate_ref[k]
        before, after = jnp.where(left, face, mate), jnp.where(left, mate, face)
        blocks.append(jnp.concatenate([before, own_ref[k], after], axis=0))
    f, a, s = blocks
    coefs = pair_planes([t[4 * p : 4 * p + 4] for t in (a, s) for p in range(3)], coef_rows)
    w = relax_weight(a[1:11], s[1:11], 1.0)
    u = w * f[1:11]
    u = u[1:-1] + w[1:-1] * (f[2:10] - fine_apply(u, a[2:10], s[2:10]))
    iter_ref[...] = u[:, 8:32]
    for k, t in enumerate((f[2:10], a[2:10], s[2:10], w[1:9])):
        field_ref[k] = t[:, 8:32]
    resid = f[4:8] - fine_apply(u[1:7], a[4:8], s[4:8])
    f = pair_planes([resid], rows_ref)
    a, s = coefs[:3], coefs[3:]
    for k, t in enumerate((f[0], a[1], s[1])):
        one_ref[k] = t

    row = iota((16, 128), 0)
    f = jnp.where((row >= 4) & (row < 12), f, 0.0)
    none = jnp.zeros_like(f)
    f = jnp.concatenate([none, f, none], axis=0)
    w = relax_weight(a, s, 0.25)
    v = w * f
    v = v + w * (f - middle_apply(v, a, s))
    resid = f - middle_apply(v, a, s)
    spread = ones_where(iota((128, 128), 1) % 32 == (iota((128, 128), 0) % 64) // 2, 0.125)
    two = row // 2
    group = iota((16, 128), 1) // 32
    own = ones_where(two == group + 2)
    over = ones_where(((two == 1) & (group == 3)) | ((two == 6) & (group == 0)))
    mixed = dot(resid.reshape(48, 128), spread).reshape(3, 16, 128)
    rows = []
    for k in range(3):
        rows += [mixed[k] * own, mixed[k] * over]
    mixed = dot(jnp.concatenate([a[1], s[1]], axis=0), spread).reshape(2, 16, 128)
    rows += [mixed[0] * own, mixed[1] * own]
    piece = jnp.concatenate([jnp.sum(t, axis=0, keepdims=True) for t in rows], axis=0)
    piece_ref[...] = jnp.broadcast_to(piece[None], piece_ref.shape)


def middle_apply(v, scale, shift):
    rows = v.shape[1]
    lane = iota((rows, 128), 1)
    row = iota((rows, 128), 0)
    swap = pltpu.roll(v, 64, 2)
    edge = jnp.zeros_like(swap[:1])
    prev = jnp.concatenate([edge, swap[:-1]], axis=0)
    later = jnp.concatenate([swap[1:], edge], axis=0)
    box = v + swap + jnp.where(lane < 64, prev, later)
    box = (
        box
        + jnp.where(row > 0, pltpu.roll(box, 1, 1), 0.0)
        + jnp.where(row < rows - 1, pltpu.roll(box, rows - 1, 1), 0.0)
    )
    box = lane_box(box, 64)
    return 0.25 * scale * (27.0 * v - box) + shift * v


def quarter_row(shape, dim):
    i = iota(shape, dim)
    return 4 * (i % 8) + i // 8


def quarter_mask():
    return ones_where(iota((4, 8, 128), 2) // 32 == iota((4, 8, 128), 0))


def gather_kernel(got_ref, piece_ref, rows_ref):
    left = lax.axis_index("c") == 0
    half = got_ref.shape[0] // 2
    ranks = half // 8
    rows_ref[: 2 * half] = got_ref[...]

    def column(core, k):
        return rows_ref[pl.ds(core * half + k, ranks, stride=8)]

    lane, row = iota((ranks, 128), 1), iota((ranks, 128), 0)

    def plane(core, p):
        over = column(core, 2 * p + 1)
        down = jnp.where((lane >= 96) & (row < ranks - 1), pltpu.roll(over, ranks - 1, 0), 0.0)
        up = jnp.where((lane < 32) & (row > 0), pltpu.roll(over, 1, 0), 0.0)
        return column(core, 2 * p) + down + up

    fields = [
        jnp.where(left, plane(0, 0), plane(0, 2) + plane(1, 1)),
        jnp.where(left, plane(0, 1) + plane(1, 0), plane(1, 2)),
    ]
    fields += [jnp.where(left, column(0, k), column(1, k)) for k in (6, 7)]
    piece = jnp.concatenate(fields, axis=0)
    piece_ref[...] = jnp.broadcast_to(piece[None], piece_ref.shape)


def smooth_kernel(own_ref, mate_ref, outer_ref, swap_ref, field_ref, iter_ref):
    left = lax.axis_index("c") == 0
    for k in range(3):
        mate, outer, swapped = mate_ref[k], outer_ref[:, k], swap_ref[:, k]
        field_ref[k, 0] = jnp.where(left, outer[0], swapped[1])
        field_ref[k, 1] = jnp.where(left, outer[1], mate)
        field_ref[k, 2] = own_ref[k]
        field_ref[k, 3] = jnp.where(left, mate, outer[0])
        field_ref[k, 4] = jnp.where(left, swapped[0], outer[1])
    f, a, s = (field_ref[k] for k in range(3))
    w = relax_weight(a, s, 0.25)
    field_ref[3] = w
    v = w * f
    iter_ref[...] = v + w * (f - middle_apply(v, a, s))


def coarse_box(v):
    edge = jnp.zeros_like(v[:1])
    box = v + jnp.concatenate([edge, v[:-1]], axis=0) + jnp.concatenate([v[1:], edge], axis=0)
    lane, row = iota((8, 128), 1), iota((8, 128), 0)
    up = pltpu.roll(box, 32, 2)
    up = jnp.where(lane >= 32, up, jnp.where(row > 0, pltpu.roll(up, 1, 1), 0.0))
    down = pltpu.roll(box, 96, 2)
    down = jnp.where(lane < 96, down, jnp.where(row < 7, pltpu.roll(down, 7, 1), 0.0))
    return lane_box(box + up + down, 32)


def total(v):
    plane = jnp.sum(v, axis=0)
    return jnp.sum(jnp.sum(plane, axis=0, keepdims=True), axis=1, keepdims=True)


def last_kernel(
    got_ref, mate_ref, field_ref, middle_ref, fine_ref, iter_ref, out_ref,
    coarse_ref, middle_rows, fine_rows,
):
    nx = lax.axis_size("x")
    chip = lax.axis_index("y") * nx + lax.axis_index("x")
    core = lax.axis_index("c")
    rank = lax.axis_index("z")
    planes = 2 * got_ref.shape[0]

    got, mate = got_ref[...], mate_ref[...]
    halves = jnp.where(core == 0, got, mate), jnp.where(core == 0, mate, got)

    def part(half, k):
        return halves[half][:, 8 * k : 8 * k + 8]

    def pairs(first, second):
        return jnp.concatenate([first[:, None], second[:, None]], axis=1).reshape(planes, 8, 128)

    edge = jnp.zeros_like(part(0, 0)[:1])
    q = pairs(
        part(0, 1) + jnp.concatenate([edge, part(1, 1)[:-1]], axis=0),
        part(1, 0) + jnp.concatenate([part(0, 0)[1:], edge], axis=0),
    )
    a, s = pairs(part(0, 2), part(1, 2)), pairs(part(0, 3), part(1, 3))
    a = 0.0625 * a
    inverse = 1.0 / (26.0 * a + s)
    e = jnp.zeros_like(q)
    for _ in range(COARSE):
        z = q * inverse
        image = a * (27.0 * z - coarse_box(z)) + s * z
        alpha = (total(image * q) / total(image * image))[None]
        e = e + alpha * z
        q = q - alpha * image
    coarse_ref[...] = jnp.zeros_like(coarse_ref)
    coarse_ref[2 : planes + 2] = e
    near = coarse_ref[pl.ds(chip * 2 + core, 5)]

    mask = quarter_mask()
    stack = jnp.concatenate([(near[p][None] * mask).reshape(32, 128) for p in range(5)], axis=0)
    spread = ones_where(iota((128, 128), 0) % 32 == (iota((128, 128), 1) % 64) // 2)
    mixed = dot(stack, spread)
    size = (middle_rows.shape[0] - 16) // 5
    edge = jnp.zeros((4, 128), F32)
    window = []
    for p in range(5):
        at = size * p
        middle_rows[at : at + 4] = edge
        middle_rows[at + size - 4 : at + size] = edge
        for k in range(4):
            t = mixed[32 * p + 8 * k : 32 * p + 8 * k + 8]
            for i in (4, 5):
                middle_rows[pl.ds(at + 2 * k + i, 8, stride=8)] = t
        window.append(middle_rows[pl.ds(pl.multiple_of(at + rank * 8, 8), 16)][None])
    v = middle_ref[...] + jnp.concatenate(window, axis=0)
    f, a, s, w = (field_ref[k] for k in range(4))
    for _ in range(2):
        v = v + w * (f - middle_apply(v, a, s))

    lane, out = iota((128, 256), 0), iota((128, 256), 1)
    mixed = dot(v[1:4].reshape(48, 128), ones_where(lane == out // 2))
    halves = [mixed[:16, 128:], mixed[16:32, :128], mixed[16:32, 128:], mixed[32:, :128]]
    refined = []
    for p, t in enumerate(halves):
        for i in range(2):
            fine_rows[pl.ds(24 * p + i, 12, stride=2)] = t[2:14]
        refined += [fine_rows[24 * p : 24 * p + 24][None]] * 2
    refined = jnp.concatenate(refined, axis=0)

    f, a, s, w = (fine_ref[k] for k in range(4))
    u = iter_ref[...] + jnp.where(a > 0.25, refined, 0.0)
    for i in (1, 2):
        j = 8 - i
        u = u[1:-1] + w[i:j] * (f[i:j] - fine_apply(u, a[i:j], s[i:j]))
    out_ref[...] = u[:, 4:20]


def call(kernel, outs, *args, scratch=()):
    return pl.pallas_call(
        kernel,
        out_shape=[jax.ShapeDtypeStruct(shape, F32) for shape in outs],
        in_specs=[pl.BlockSpec(memory_space=pltpu.VMEM)] * len(args),
        out_specs=[pl.BlockSpec(memory_space=pltpu.VMEM)] * len(outs),
        scratch_shapes=[pltpu.VMEM(shape, F32) for shape in scratch],
        compiler_params=pltpu.CompilerParams(vmem_limit_bytes=24 * 2**20),
    )(*args)


def shards(source, row_scale, shift_field):
    ny, nx, nz = lax.axis_size("y"), lax.axis_size("x"), lax.axis_size("z")
    chips = ny * nx
    first = lax.axis_index("c") == 0

    own = jnp.stack([source, row_scale, shift_field])
    up = [(i, i + 1) for i in range(nz - 1)]
    down = [(i + 1, i) for i in range(nz - 1)]
    before = lax.ppermute(own[:, :, 6:], "z", up)
    after = lax.ppermute(own[:, :, :10], "z", down)
    fill = jnp.zeros((3, 4, 2, 128), F32)
    own = jnp.concatenate([fill, before, own, after, fill], axis=2)
    facing = []
    for i in range(chips - 1):
        facing += [(2 * i + 1, 2 * i + 2), (2 * i + 2, 2 * i + 1)]
    swap = [(0, 1), (1, 0)]
    face = lax.ppermute(own, ("y", "x", "c"), facing)
    mate = lax.ppermute(own, "c", swap)
    fine_iter, fine_fields, sent, one = call(
        fine_kernel,
        [(8, 24, 128), (4, 8, 24, 128), (2 * nz, 8, 128), (3, 16, 128)],
        own, mate, face,
        scratch=[(12 * 40 + 16, 128), (2 * 40 + 16, 128)],
    )

    got = lax.all_to_all(sent, ("c", "z"), 0, 0).reshape(16 * nz, 128)
    (sent,) = call(
        gather_kernel, [(chips, 32, 128)], got, scratch=[(16 * nz + 16, 128)]
    )
    half = lax.all_to_all(sent, ("y", "x"), 0, 0)

    mate = lax.ppermute(one, "c", swap)
    pairs = jnp.stack([jnp.where(first, one, mate), jnp.where(first, mate, one)])
    ring = []
    for i in range(chips - 1):
        ring += [(2 * i, 2 * i + 2), (2 * i + 3, 2 * i + 1)]
    outer = lax.ppermute(pairs, ("y", "x", "c"), ring)
    swapped = lax.ppermute(outer, "c", swap)
    fields, middle_iter = call(
        smooth_kernel, [(4, 5, 16, 128), (5, 16, 128)], one, mate, outer, swapped
    )
    half, fields, middle_iter = lax.optimization_barrier((half, fields, middle_iter))
    half_mate = lax.ppermute(half, "c", swap)
    (result,) = call(
        last_kernel, [source.shape],
        half, half_mate, fields, middle_iter, fine_fields, fine_iter,
        scratch=[(2 * chips + 4, 8, 128), (5 * (8 * nz + 8) + 16, 128), (4 * 24 + 16, 128)],
    )
    return result


def solution(mesh):
    ny, nx = (8, 4) if mesh.devices.shape[0] == 64 else (mesh.devices.shape[0] // 2, 1)
    nz = mesh.devices.shape[1]
    split = Mesh(mesh.devices.reshape(ny, nx, 2, nz), ("y", "x", "c", "z"))
    spec = P(("y", "x", "c"), "z", None)
    return jax.shard_map(
        shards, mesh=split, in_specs=(spec, spec, spec), out_specs=spec, check_vma=False
    )
```

```python
import functools

import jax
import jax.numpy as jnp
from jax import lax
from jax.experimental import pallas as pl
from jax.experimental.pallas import tpu as pltpu
from jax.sharding import Mesh, PartitionSpec as P

COARSE = 4
DAMPING = 0.8
F32 = jnp.float32


def dot(a, b):
    high = a.astype(jnp.bfloat16)
    rest = a - high.astype(F32)
    middle = rest.astype(jnp.bfloat16)
    low = (rest - middle.astype(F32)).astype(jnp.bfloat16)
    parts = lax.dot_general(
        jnp.concatenate([high, middle, low], axis=0),
        b.astype(jnp.bfloat16),
        (((1,), (0,)), ((), ())),
        preferred_element_type=F32,
    )
    n = a.shape[0]
    return parts[:n] + parts[n : 2 * n] + parts[2 * n :]


def iota(shape, dim):
    return lax.broadcasted_iota(jnp.int32, shape, dim)


def ones_where(cond, value=1.0):
    return jnp.where(cond, jnp.float32(value), jnp.float32(0.0))


def lane_box(v, period):
    axis = v.ndim - 1
    lane = iota(v.shape[-2:], 1) % period
    below = jnp.where(lane > 0, pltpu.roll(v, 1, axis), 0.0)
    above = jnp.where(lane < period - 1, pltpu.roll(v, 127, axis), 0.0)
    return v + below + above


def relax_weight(scale, shift, level_scale):
    inside = scale > 0.25
    diag = jnp.where(inside, 26.0 * level_scale * scale + shift, 1.0)
    return jnp.where(inside, DAMPING / diag, 0.0)


def fine_apply(v, scale, shift):
    rows = v.shape[1]
    box = v[:-2] + v[1:-1] + v[2:]
    box = box + pltpu.roll(box, 1, 1) + pltpu.roll(box, rows - 1, 1)
    box = lane_box(box, 128)
    mid = v[1:-1]
    return scale * (27.0 * mid - box) + shift * mid


def pair_planes(quads, rows_ref):
    parts = []
    for k, t in enumerate(quads):
        halves = []
        for i in (0, 2):
            at = 40 * (2 * k + i // 2)
            rows_ref[at : at + 40] = t[i] + t[i + 1]
            halves.append(
                rows_ref[pl.ds(at + 4, 16, stride=2)] + rows_ref[pl.ds(at + 5, 16, stride=2)]
            )
        parts.append(jnp.concatenate(halves, axis=1))
    lane, out = iota((256, 128), 0), iota((256, 128), 1)
    pack = ones_where(lane // 2 == out, 0.125)
    return dot(jnp.concatenate(parts, axis=0), pack).reshape(len(quads), 16, 128)


def fine_kernel(
    own_ref, mate_ref, face_ref, iter_ref, field_ref, piece_ref, one_ref, coef_rows, rows_ref
):
    left = lax.axis_index("c") == 0
    blocks = []
    for k in range(3):
        face, mate = face_ref[k], mate_ref[k]
        before, after = jnp.where(left, face, mate), jnp.where(left, mate, face)
        blocks.append(jnp.concatenate([before, own_ref[k], after], axis=0))
    f, a, s = blocks
    coefs = pair_planes([t[4 * p : 4 * p + 4] for t in (a, s) for p in range(3)], coef_rows)
    w = relax_weight(a[1:11], s[1:11], 1.0)
    u = w * f[1:11]
    u = u[1:-1] + w[1:-1] * (f[2:10] - fine_apply(u, a[2:10], s[2:10]))
    iter_ref[...] = u[:, 8:32]
    for k, t in enumerate((f[2:10], a[2:10], s[2:10], w[1:9])):
        field_ref[k] = t[:, 8:32]
    resid = f[4:8] - fine_apply(u[1:7], a[4:8], s[4:8])
    f = pair_planes([resid], rows_ref)
    a, s = coefs[:3], coefs[3:]
    for k, t in enumerate((f[0], a[1], s[1])):
        one_ref[k] = t

    none = jnp.zeros_like(f)
    f = jnp.concatenate([none, f, none], axis=0)
    w = relax_weight(a, s, 0.25)
    v = w * f
    v = v + w * (f - middle_apply(v, a, s))
    resid = f - middle_apply(v, a, s)
    spread = ones_where(iota((128, 128), 1) % 32 == (iota((128, 128), 0) % 64) // 2, 0.125)
    own = ones_where(iota((16, 128), 0) // 2 == iota((16, 128), 1) // 32 + 2)
    mixed = dot(resid.reshape(48, 128), spread).reshape(3, 16, 128)
    rows = [mixed[k] * own for k in range(3)]
    mixed = dot(jnp.concatenate([a[1], s[1]], axis=0), spread).reshape(2, 16, 128)
    rows += [mixed[k] * own for k in range(2)] + [jnp.zeros((1, 128), F32)] * 3
    piece = jnp.concatenate([jnp.sum(t, axis=0, keepdims=True) for t in rows], axis=0)
    piece_ref[...] = jnp.broadcast_to(piece[None], piece_ref.shape)


def middle_apply(v, scale, shift):
    rows = v.shape[1]
    lane = iota((rows, 128), 1)
    row = iota((rows, 128), 0)
    swap = pltpu.roll(v, 64, 2)
    edge = jnp.zeros_like(swap[:1])
    prev = jnp.concatenate([edge, swap[:-1]], axis=0)
    later = jnp.concatenate([swap[1:], edge], axis=0)
    box = v + swap + jnp.where(lane < 64, prev, later)
    box = (
        box
        + jnp.where(row > 0, pltpu.roll(box, 1, 1), 0.0)
        + jnp.where(row < rows - 1, pltpu.roll(box, rows - 1, 1), 0.0)
    )
    box = lane_box(box, 64)
    return 0.25 * scale * (27.0 * v - box) + shift * v


def quarter_row(shape, dim):
    i = iota(shape, dim)
    return 4 * (i % 8) + i // 8


def quarter_mask():
    return ones_where(iota((4, 8, 128), 2) // 32 == iota((4, 8, 128), 0))


def gather_kernel(got_ref, piece_ref, rows_ref):
    core = lax.axis_index("c")
    half = got_ref.shape[0] // 2
    rows_ref[: 2 * half] = got_ref[...]

    def column(at, k):
        return rows_ref[pl.ds(at * half + k, half // 8, stride=8)]

    outward = 2 * core
    piece = jnp.concatenate(
        [
            column(core, outward),
            column(core, 1) + column(1 - core, outward),
            column(core, 3),
            column(core, 4),
        ],
        axis=0,
    )
    piece_ref[...] = jnp.broadcast_to(piece[None], piece_ref.shape)


def smooth_kernel(own_ref, mate_ref, outer_ref, inner_ref, field_ref, iter_ref):
    left = lax.axis_index("c") == 0
    for k in range(3):
        mate, outer, inner = mate_ref[k], outer_ref[:, k], inner_ref[k]
        field_ref[k, 0] = jnp.where(left, outer[0], inner)
        field_ref[k, 1] = jnp.where(left, outer[1], mate)
        field_ref[k, 2] = own_ref[k]
        field_ref[k, 3] = jnp.where(left, mate, outer[0])
        field_ref[k, 4] = jnp.where(left, inner, outer[1])
    f, a, s = (field_ref[k] for k in range(3))
    w = relax_weight(a, s, 0.25)
    field_ref[3] = w
    v = w * f
    iter_ref[...] = v + w * (f - middle_apply(v, a, s))


def coarse_box(v):
    box = v[:-2] + v[1:-1] + v[2:]
    lane, row = iota((8, 128), 1), iota((8, 128), 0)
    up = pltpu.roll(box, 32, 2)
    up = jnp.where(lane >= 32, up, jnp.where(row > 0, pltpu.roll(up, 1, 1), 0.0))
    down = pltpu.roll(box, 96, 2)
    down = jnp.where(lane < 96, down, jnp.where(row < 7, pltpu.roll(down, 7, 1), 0.0))
    return lane_box(box + up + down, 32)


def total(plane):
    return jnp.sum(jnp.sum(plane, axis=0, keepdims=True), axis=1, keepdims=True)


def solve_coarse(q_ref, a_ref, d_ref, inverse_ref, z_ref, image_ref, e_ref):
    planes = q_ref.shape[0]
    chunk = 8 if planes % 8 == 0 else 2
    starts = range(0, planes, chunk)
    none = jnp.zeros((1, 8, 128), F32)
    z_ref[:1] = none
    z_ref[planes + 1 :] = none
    for i in (0, 1, planes + 2, planes + 3):
        e_ref[i : i + 1] = none
    for i in starts:
        own = slice(i, i + chunk)
        inverse = 1.0 / (d_ref[own] - a_ref[own])
        inverse_ref[own] = inverse
        z_ref[i + 1 : i + chunk + 1] = q_ref[own] * inverse
    for step in range(COARSE):
        upper = lower = jnp.zeros((8, 128), F32)
        for i in starts:
            own = slice(i, i + chunk)
            z = z_ref[i : i + chunk + 2]
            image = d_ref[own] * z[1:-1] - a_ref[own] * coarse_box(z)
            image_ref[own] = image
            upper = upper + jnp.sum(image * q_ref[own], axis=0)
            lower = lower + jnp.sum(image * image, axis=0)
        alpha = (total(upper) / total(lower))[None]
        for i in starts:
            own = slice(i, i + chunk)
            inner = slice(i + 1, i + chunk + 1)
            outer = slice(i + 2, i + chunk + 2)
            gain = alpha * z_ref[inner]
            e_ref[outer] = gain if step == 0 else e_ref[outer] + gain
            if step < COARSE - 1:
                q = q_ref[own] - alpha * image_ref[own]
                q_ref[own] = q
                z_ref[inner] = q * inverse_ref[own]


def last_kernel(
    got_ref, mate_ref, field_ref, middle_ref, fine_ref, iter_ref, out_ref,
    q_ref, a_ref, d_ref, inverse_ref, z_ref, image_ref, coarse_ref, middle_rows, fine_rows,
):
    nx = lax.axis_size("x")
    chip = lax.axis_index("y") * nx + lax.axis_index("x")
    core = lax.axis_index("c")
    rank = lax.axis_index("z")
    planes = 2 * got_ref.shape[0]

    got, mate = got_ref[...], mate_ref[...]
    halves = jnp.where(core == 0, got, mate), jnp.where(core == 0, mate, got)

    def part(half, k):
        return halves[half][:, 8 * k : 8 * k + 8]

    def pairs(first, second):
        return jnp.concatenate([first[:, None], second[:, None]], axis=1).reshape(planes, 8, 128)

    edge = jnp.zeros_like(part(0, 0)[:1])
    q_ref[...] = pairs(
        part(0, 1) + jnp.concatenate([edge, part(1, 0)[:-1]], axis=0),
        part(1, 1) + jnp.concatenate([part(0, 0)[1:], edge], axis=0),
    )
    a = 0.0625 * pairs(part(0, 2), part(1, 2))
    a_ref[...] = a
    d_ref[...] = 27.0 * a + pairs(part(0, 3), part(1, 3))
    solve_coarse(q_ref, a_ref, d_ref, inverse_ref, z_ref, image_ref, coarse_ref)
    near = coarse_ref[pl.ds(chip * 2 + core, 5)]

    mask = quarter_mask()
    stack = jnp.concatenate([(near[p][None] * mask).reshape(32, 128) for p in range(5)], axis=0)
    spread = ones_where(iota((128, 128), 0) % 32 == (iota((128, 128), 1) % 64) // 2)
    mixed = dot(stack, spread)
    size = (middle_rows.shape[0] - 16) // 5
    edge = jnp.zeros((4, 128), F32)
    window = []
    for p in range(5):
        at = size * p
        middle_rows[at : at + 4] = edge
        middle_rows[at + size - 4 : at + size] = edge
        for k in range(4):
            t = mixed[32 * p + 8 * k : 32 * p + 8 * k + 8]
            for i in (4, 5):
                middle_rows[pl.ds(at + 2 * k + i, 8, stride=8)] = t
        window.append(middle_rows[pl.ds(pl.multiple_of(at + rank * 8, 8), 16)][None])
    v = middle_ref[...] + jnp.concatenate(window, axis=0)
    f, a, s, w = (field_ref[k] for k in range(4))
    for _ in range(2):
        v = v + w * (f - middle_apply(v, a, s))

    lane, out = iota((128, 256), 0), iota((128, 256), 1)
    mixed = dot(v[1:4].reshape(48, 128), ones_where(lane == out // 2))
    halves = [mixed[:16, 128:], mixed[16:32, :128], mixed[16:32, 128:], mixed[32:, :128]]
    refined = []
    for p, t in enumerate(halves):
        for i in range(2):
            fine_rows[pl.ds(24 * p + i, 12, stride=2)] = t[2:14]
        refined += [fine_rows[24 * p : 24 * p + 24][None]] * 2
    refined = jnp.concatenate(refined, axis=0)

    f, a, s, w = (fine_ref[k] for k in range(4))
    u = iter_ref[...] + jnp.where(a > 0.25, refined, 0.0)
    for i in (1, 2):
        j = 8 - i
        u = u[1:-1] + w[i:j] * (f[i:j] - fine_apply(u, a[i:j], s[i:j]))
    out_ref[...] = u[:, 4:20]


def call(kernel, outs, *args, scratch=()):
    return pl.pallas_call(
        kernel,
        out_shape=[jax.ShapeDtypeStruct(shape, F32) for shape in outs],
        in_specs=[pl.BlockSpec(memory_space=pltpu.VMEM)] * len(args),
        out_specs=[pl.BlockSpec(memory_space=pltpu.VMEM)] * len(outs),
        scratch_shapes=[pltpu.VMEM(shape, F32) for shape in scratch],
        compiler_params=pltpu.CompilerParams(vmem_limit_bytes=24 * 2**20),
    )(*args)


def shards(source, row_scale, shift_field):
    ny, nx, nz = lax.axis_size("y"), lax.axis_size("x"), lax.axis_size("z")
    chips = ny * nx
    first = lax.axis_index("c") == 0

    own = jnp.stack([source, row_scale, shift_field])
    up = [(i, i + 1) for i in range(nz - 1)]
    down = [(i + 1, i) for i in range(nz - 1)]
    before = lax.ppermute(own[:, :, 6:], "z", up)
    after = lax.ppermute(own[:, :, :10], "z", down)
    fill = jnp.zeros((3, 4, 2, 128), F32)
    own = jnp.concatenate([fill, before, own, after, fill], axis=2)
    facing = []
    for i in range(chips - 1):
        facing += [(2 * i + 1, 2 * i + 2), (2 * i + 2, 2 * i + 1)]
    swap = [(0, 1), (1, 0)]
    face = lax.ppermute(own, ("y", "x", "c"), facing)
    mate = lax.ppermute(own, "c", swap)
    fine_iter, fine_fields, sent, one = call(
        fine_kernel,
        [(8, 24, 128), (4, 8, 24, 128), (2 * nz, 8, 128), (3, 16, 128)],
        own, mate, face,
        scratch=[(12 * 40 + 16, 128), (2 * 40 + 16, 128)],
    )

    got = lax.all_to_all(sent, ("c", "z"), 0, 0).reshape(16 * nz, 128)
    (sent,) = call(
        gather_kernel, [(chips, 32, 128)], got, scratch=[(16 * nz + 16, 128)]
    )
    one, sent = lax.optimization_barrier((one, sent))
    half = lax.all_to_all(sent, ("y", "x"), 0, 0)

    mate = lax.ppermute(one, "c", swap)
    pairs = jnp.stack([jnp.where(first, one, mate), jnp.where(first, mate, one)])
    ring = []
    for i in range(chips - 1):
        ring += [(2 * i, 2 * i + 2), (2 * i + 3, 2 * i + 1)]
    outer = lax.ppermute(pairs, ("y", "x", "c"), ring)
    inner = lax.ppermute(one, ("y", "x", "c"), [(j, i) for i, j in ring])
    fields, middle_iter = call(
        smooth_kernel, [(4, 5, 16, 128), (5, 16, 128)], one, mate, outer, inner
    )
    half, fields, middle_iter = lax.optimization_barrier((half, fields, middle_iter))
    half_mate = lax.ppermute(half, "c", swap)
    (result,) = call(
        last_kernel, [source.shape],
        half, half_mate, fields, middle_iter, fine_fields, fine_iter,
        scratch=[(2 * chips, 8, 128)] * 4
        + [(2 * chips + 2, 8, 128), (2 * chips, 8, 128), (2 * chips + 4, 8, 128)]
        + [(5 * (8 * nz + 8) + 16, 128), (4 * 24 + 16, 128)],
    )
    return result


def solution(mesh):
    ny, nx = (8, 4) if mesh.devices.shape[0] == 64 else (mesh.devices.shape[0] // 2, 1)
    nz = mesh.devices.shape[1]
    split = Mesh(mesh.devices.reshape(ny, nx, 2, nz), ("y", "x", "c", "z"))
    spec = P(("y", "x", "c"), "z", None)
    return jax.shard_map(
        shards, mesh=split, in_specs=(spec, spec, spec), out_specs=spec, check_vma=False
    )
```

```python
import jax
import jax.numpy as jnp
from jax import lax
from jax.experimental import pallas as pl
from jax.experimental.pallas import tpu as pltpu
from jax.sharding import Mesh, PartitionSpec as P

COARSE = 4
DAMPING = 0.8
F32 = jnp.float32


def iota(shape, dim):
    return lax.broadcasted_iota(jnp.int32, shape, dim)


def ones_where(cond, value=1.0):
    return jnp.where(cond, jnp.float32(value), jnp.float32(0.0))


def lane_box(v, period):
    axis = v.ndim - 1
    lane = iota(v.shape[-2:], 1) % period
    below = jnp.where(lane > 0, pltpu.roll(v, 1, axis), 0.0)
    above = jnp.where(lane < period - 1, pltpu.roll(v, 127, axis), 0.0)
    return v + below + above


def gather_lanes(v, index):
    return jnp.take_along_axis(v, index, axis=1, mode="promise_in_bounds")


def relax_weight(scale, shift, level_scale):
    inside = scale > 0.25
    diag = jnp.where(inside, 26.0 * level_scale * scale + shift, 1.0)
    return jnp.where(inside, DAMPING / diag, 0.0)


def fine_apply(v, scale, shift):
    rows = v.shape[1]
    box = v[:-2] + v[1:-1] + v[2:]
    box = box + pltpu.roll(box, 1, 1) + pltpu.roll(box, rows - 1, 1)
    box = lane_box(box, 128)
    mid = v[1:-1]
    return scale * (27.0 * mid - box) + shift * mid


def pair_planes(quads, rows_ref):
    parts = []
    for i in (0, 2):
        for k, t in enumerate(quads):
            at = 40 * (2 * k + i // 2)
            rows_ref[at : at + 40] = t[i] + t[i + 1]
            parts.append(
                rows_ref[pl.ds(at + 4, 16, stride=2)] + rows_ref[pl.ds(at + 5, 16, stride=2)]
            )
    both = jnp.concatenate(parts, axis=0)
    lane = iota(both.shape, 1)
    both = gather_lanes(both + pltpu.roll(both, 127, 1), 2 * (lane % 64))
    n = 16 * len(quads)
    pair = 0.125 * jnp.where(lane[:n] < 64, both[:n], both[n:])
    return pair.reshape(len(quads), 16, 128)


def plane_groups(v):
    v = v + pltpu.roll(v, 127, 1)
    v = v + pltpu.roll(v, 64, 1)
    return 0.125 * gather_lanes(v, 2 * (iota(v.shape, 1) % 32))


def fine_kernel(
    own_ref, mate_ref, face_ref, iter_ref, field_ref, piece_ref, one_ref, coef_rows, rows_ref
):
    left = lax.axis_index("c") == 0
    blocks = []
    for k in range(3):
        face, mate = face_ref[k], mate_ref[k]
        before, after = jnp.where(left, face, mate), jnp.where(left, mate, face)
        blocks.append(jnp.concatenate([before, own_ref[k], after], axis=0))
    f, a, s = blocks
    coefs = pair_planes([t[4 * p : 4 * p + 4] for t in (a, s) for p in range(3)], coef_rows)
    w = relax_weight(a[1:11], s[1:11], 1.0)
    u = w * f[1:11]
    u = u[1:-1] + w[1:-1] * (f[2:10] - fine_apply(u, a[2:10], s[2:10]))
    iter_ref[...] = u[:, 8:32]
    for k, t in enumerate((f[2:10], a[2:10], s[2:10], w[1:9])):
        field_ref[k] = t[:, 8:32]
    resid = f[4:8] - fine_apply(u[1:7], a[4:8], s[4:8])
    f = pair_planes([resid], rows_ref)
    a, s = coefs[:3], coefs[3:]
    for k, t in enumerate((f[0], a[1], s[1])):
        one_ref[k] = t

    none = jnp.zeros_like(f)
    f = jnp.concatenate([none, f, none], axis=0)
    w = relax_weight(a, s, 0.25)
    v = w * f
    v = v + w * (f - middle_apply(v, a, s))
    resid = f - middle_apply(v, a, s)
    own = ones_where(iota((16, 128), 0) // 2 == iota((16, 128), 1) // 32 + 2)
    mixed = plane_groups(resid.reshape(48, 128)).reshape(3, 16, 128)
    rows = [mixed[k] * own for k in range(3)]
    mixed = plane_groups(jnp.concatenate([a[1], s[1]], axis=0)).reshape(2, 16, 128)
    rows += [mixed[k] * own for k in range(2)] + [jnp.zeros((1, 128), F32)] * 3
    piece = jnp.concatenate([jnp.sum(t, axis=0, keepdims=True) for t in rows], axis=0)
    piece_ref[...] = jnp.broadcast_to(piece[None], piece_ref.shape)


def middle_apply(v, scale, shift):
    rows = v.shape[1]
    lane = iota((rows, 128), 1)
    row = iota((rows, 128), 0)
    swap = pltpu.roll(v, 64, 2)
    edge = jnp.zeros_like(swap[:1])
    prev = jnp.concatenate([edge, swap[:-1]], axis=0)
    later = jnp.concatenate([swap[1:], edge], axis=0)
    box = v + swap + jnp.where(lane < 64, prev, later)
    box = (
        box
        + jnp.where(row > 0, pltpu.roll(box, 1, 1), 0.0)
        + jnp.where(row < rows - 1, pltpu.roll(box, rows - 1, 1), 0.0)
    )
    box = lane_box(box, 64)
    return 0.25 * scale * (27.0 * v - box) + shift * v


def gather_kernel(got_ref, piece_ref, rows_ref):
    core = lax.axis_index("c")
    half = got_ref.shape[0] // 2
    rows_ref[: 2 * half] = got_ref[...]

    def column(at, k):
        return rows_ref[pl.ds(at * half + k, half // 8, stride=8)]

    outward = 2 * core
    piece = jnp.concatenate(
        [
            column(core, outward),
            column(core, 1) + column(1 - core, outward),
            column(core, 3),
            column(core, 4),
        ],
        axis=0,
    )
    piece_ref[...] = jnp.broadcast_to(piece[None], piece_ref.shape)


def smooth_kernel(own_ref, mate_ref, outer_ref, inner_ref, field_ref, iter_ref):
    left = lax.axis_index("c") == 0
    for k in range(3):
        mate, outer, inner = mate_ref[k], outer_ref[:, k], inner_ref[k]
        field_ref[k, 0] = jnp.where(left, outer[0], inner)
        field_ref[k, 1] = jnp.where(left, outer[1], mate)
        field_ref[k, 2] = own_ref[k]
        field_ref[k, 3] = jnp.where(left, mate, outer[0])
        field_ref[k, 4] = jnp.where(left, inner, outer[1])
    f, a, s = (field_ref[k] for k in range(3))
    w = relax_weight(a, s, 0.25)
    field_ref[3] = w
    v = w * f
    iter_ref[...] = v + w * (f - middle_apply(v, a, s))


def coarse_box(v):
    box = v[:-2] + v[1:-1] + v[2:]
    lane, row = iota((8, 128), 1), iota((8, 128), 0)
    up = pltpu.roll(box, 32, 2)
    up = jnp.where(lane >= 32, up, jnp.where(row > 0, pltpu.roll(up, 1, 1), 0.0))
    down = pltpu.roll(box, 96, 2)
    down = jnp.where(lane < 96, down, jnp.where(row < 7, pltpu.roll(down, 7, 1), 0.0))
    return lane_box(box + up + down, 32)


def total(plane):
    return jnp.sum(jnp.sum(plane, axis=0, keepdims=True), axis=1, keepdims=True)


def solve_coarse(q_ref, a_ref, d_ref, inverse_ref, w_ref, y_ref, at):
    planes = a_ref.shape[0]
    chunk = 8 if planes % 8 == 0 else 2
    starts = range(0, planes, chunk)
    none = jnp.zeros((2, 8, 128), F32)
    for ref in (q_ref, inverse_ref, w_ref):
        ref[:2] = none
        ref[planes + 2 :] = none
    for i in starts:
        own, padded = slice(i, i + chunk), slice(i + 2, i + chunk + 2)
        inverse_ref[padded] = 1.0 / (d_ref[own] - a_ref[own])

    def product(ref):
        for i in starts:
            own, wide = slice(i, i + chunk), slice(i + 1, i + chunk + 3)
            z = ref[wide] * inverse_ref[wide]
            y_ref[own] = d_ref[own] * z[1:-1] - a_ref[own] * coarse_box(z)

    product(q_ref)
    solution = jnp.zeros((5, 8, 128), F32)
    for step in range(COARSE):
        upper = lower = jnp.zeros((8, 128), F32)
        for i in starts:
            own, padded = slice(i, i + chunk), slice(i + 2, i + chunk + 2)
            w, q = y_ref[own], q_ref[padded]
            if step > 0:
                old = w_ref[padded]
                w, q = old - alpha * w, q - alpha * old
                q_ref[padded] = q
            w_ref[padded] = w
            upper = upper + jnp.sum(w * q, axis=0)
            lower = lower + jnp.sum(w * w, axis=0)
        alpha = (total(upper) / total(lower))[None]
        if step < COARSE - 1:
            product(w_ref)
        solution = solution + alpha * q_ref[pl.ds(at, 5)]
    return solution * inverse_ref[pl.ds(at, 5)]


def last_kernel(
    got_ref, mate_ref, field_ref, middle_ref, fine_ref, iter_ref, out_ref,
    q_ref, a_ref, d_ref, inverse_ref, w_ref, y_ref, middle_rows, fine_rows,
):
    nx = lax.axis_size("x")
    chip = lax.axis_index("y") * nx + lax.axis_index("x")
    core = lax.axis_index("c")
    rank = lax.axis_index("z")
    planes = 2 * got_ref.shape[0]

    got, mate = got_ref[...], mate_ref[...]
    halves = jnp.where(core == 0, got, mate), jnp.where(core == 0, mate, got)

    def part(half, k):
        return halves[half][:, 8 * k : 8 * k + 8]

    def pairs(first, second):
        return jnp.concatenate([first[:, None], second[:, None]], axis=1).reshape(planes, 8, 128)

    edge = jnp.zeros_like(part(0, 0)[:1])
    q_ref[2 : planes + 2] = pairs(
        part(0, 1) + jnp.concatenate([edge, part(1, 0)[:-1]], axis=0),
        part(1, 1) + jnp.concatenate([part(0, 0)[1:], edge], axis=0),
    )
    a = 0.0625 * pairs(part(0, 2), part(1, 2))
    a_ref[...] = a
    d_ref[...] = 27.0 * a + pairs(part(0, 3), part(1, 3))
    near = solve_coarse(q_ref, a_ref, d_ref, inverse_ref, w_ref, y_ref, chip * 2 + core)

    lane = iota((8, 128), 1) % 64 // 2
    size = (middle_rows.shape[0] - 16) // 5
    edge = jnp.zeros((4, 128), F32)
    window = []
    for p in range(5):
        at = size * p
        middle_rows[at : at + 4] = edge
        middle_rows[at + size - 4 : at + size] = edge
        for k in range(4):
            t = gather_lanes(near[p], 32 * k + lane)
            for i in (4, 5):
                middle_rows[pl.ds(at + 2 * k + i, 8, stride=8)] = t
        window.append(middle_rows[pl.ds(pl.multiple_of(at + rank * 8, 8), 16)][None])
    v = middle_ref[...] + jnp.concatenate(window, axis=0)
    f, a, s, w = (field_ref[k] for k in range(4))
    for _ in range(2):
        v = v + w * (f - middle_apply(v, a, s))

    lane = iota((32, 128), 1) // 2
    low = gather_lanes(v[2:4].reshape(32, 128), lane)
    high = gather_lanes(v[1:3].reshape(32, 128), 64 + lane)
    halves = [high[:16], low[:16], high[16:], low[16:]]
    refined = []
    for p, t in enumerate(halves):
        for i in range(2):
            fine_rows[pl.ds(24 * p + i, 12, stride=2)] = t[2:14]
        refined += [fine_rows[24 * p : 24 * p + 24][None]] * 2
    refined = jnp.concatenate(refined, axis=0)

    f, a, s, w = (fine_ref[k] for k in range(4))
    u = iter_ref[...] + jnp.where(a > 0.25, refined, 0.0)
    for i in (1, 2):
        j = 8 - i
        u = u[1:-1] + w[i:j] * (f[i:j] - fine_apply(u, a[i:j], s[i:j]))
    out_ref[...] = u[:, 4:20]


def call(kernel, outs, *args, scratch=()):
    return pl.pallas_call(
        kernel,
        out_shape=[jax.ShapeDtypeStruct(shape, F32) for shape in outs],
        in_specs=[pl.BlockSpec(memory_space=pltpu.VMEM)] * len(args),
        out_specs=[pl.BlockSpec(memory_space=pltpu.VMEM)] * len(outs),
        scratch_shapes=[pltpu.VMEM(shape, F32) for shape in scratch],
        compiler_params=pltpu.CompilerParams(vmem_limit_bytes=24 * 2**20),
    )(*args)


def shards(source, row_scale, shift_field):
    ny, nx, nz = lax.axis_size("y"), lax.axis_size("x"), lax.axis_size("z")
    chips = ny * nx
    first = lax.axis_index("c") == 0

    own = jnp.stack([source, row_scale, shift_field])
    up = [(i, i + 1) for i in range(nz - 1)]
    down = [(i + 1, i) for i in range(nz - 1)]
    before = lax.ppermute(own[:, :, 6:], "z", up)
    after = lax.ppermute(own[:, :, :10], "z", down)
    fill = jnp.zeros((3, 4, 2, 128), F32)
    own = jnp.concatenate([fill, before, own, after, fill], axis=2)
    facing = []
    for i in range(chips - 1):
        facing += [(2 * i + 1, 2 * i + 2), (2 * i + 2, 2 * i + 1)]
    swap = [(0, 1), (1, 0)]
    face = lax.ppermute(own, ("y", "x", "c"), facing)
    mate = lax.ppermute(own, "c", swap)
    fine_iter, fine_fields, sent, one = call(
        fine_kernel,
        [(8, 24, 128), (4, 8, 24, 128), (2 * nz, 8, 128), (3, 16, 128)],
        own, mate, face,
        scratch=[(12 * 40 + 16, 128), (2 * 40 + 16, 128)],
    )

    got = lax.all_to_all(sent, ("c", "z"), 0, 0).reshape(16 * nz, 128)
    (sent,) = call(
        gather_kernel, [(chips, 32, 128)], got, scratch=[(16 * nz + 16, 128)]
    )
    one, sent = lax.optimization_barrier((one, sent))
    half = lax.all_to_all(sent, ("y", "x"), 0, 0)

    mate = lax.ppermute(one, "c", swap)
    pairs = jnp.stack([jnp.where(first, one, mate), jnp.where(first, mate, one)])
    ring = []
    for i in range(chips - 1):
        ring += [(2 * i, 2 * i + 2), (2 * i + 3, 2 * i + 1)]
    outer = lax.ppermute(pairs, ("y", "x", "c"), ring)
    inner = lax.ppermute(one, ("y", "x", "c"), [(j, i) for i, j in ring])
    fields, middle_iter = call(
        smooth_kernel, [(4, 5, 16, 128), (5, 16, 128)], one, mate, outer, inner
    )
    half, fields, middle_iter = lax.optimization_barrier((half, fields, middle_iter))
    half_mate = lax.ppermute(half, "c", swap)
    (result,) = call(
        last_kernel, [source.shape],
        half, half_mate, fields, middle_iter, fine_fields, fine_iter,
        scratch=[(2 * chips + 4, 8, 128)] + [(2 * chips, 8, 128)] * 2
        + [(2 * chips + 4, 8, 128)] * 2 + [(2 * chips, 8, 128)]
        + [(5 * (8 * nz + 8) + 16, 128), (4 * 24 + 16, 128)],
    )
    return result


def solution(mesh):
    ny, nx = (8, 4) if mesh.devices.shape[0] == 64 else (mesh.devices.shape[0] // 2, 1)
    nz = mesh.devices.shape[1]
    split = Mesh(mesh.devices.reshape(ny, nx, 2, nz), ("y", "x", "c", "z"))
    spec = P(("y", "x", "c"), "z", None)
    return jax.shard_map(
        shards, mesh=split, in_specs=(spec, spec, spec), out_specs=spec, check_vma=False
    )
```

```python
import jax
import jax.numpy as jnp
from jax import lax
from jax.experimental import pallas as pl
from jax.experimental.pallas import tpu as pltpu
from jax.sharding import Mesh, PartitionSpec as P

COARSE = 4
DAMPING = 0.8
F32 = jnp.float32


def dot(a, b):
    high = a.astype(jnp.bfloat16)
    rest = a - high.astype(F32)
    middle = rest.astype(jnp.bfloat16)
    low = (rest - middle.astype(F32)).astype(jnp.bfloat16)
    parts = lax.dot_general(
        jnp.concatenate([high, middle, low], axis=0),
        b.astype(jnp.bfloat16),
        (((1,), (0,)), ((), ())),
        preferred_element_type=F32,
    )
    n = a.shape[0]
    return parts[:n] + parts[n : 2 * n] + parts[2 * n :]


def iota(shape, dim):
    return lax.broadcasted_iota(jnp.int32, shape, dim)


def ones_where(cond, value=1.0):
    return jnp.where(cond, jnp.float32(value), jnp.float32(0.0))


def lane_box(v, period):
    axis = v.ndim - 1
    lane = iota(v.shape[-2:], 1) % period
    below = jnp.where(lane > 0, pltpu.roll(v, 1, axis), 0.0)
    above = jnp.where(lane < period - 1, pltpu.roll(v, 127, axis), 0.0)
    return v + below + above


def relax_weight(scale, shift, level_scale):
    inside = scale > 0.25
    diag = jnp.where(inside, 26.0 * level_scale * scale + shift, 1.0)
    return jnp.where(inside, DAMPING / diag, 0.0)


def fine_apply(v, scale, shift):
    rows = v.shape[1]
    box = v[:-2] + v[1:-1] + v[2:]
    box = box + pltpu.roll(box, 1, 1) + pltpu.roll(box, rows - 1, 1)
    box = lane_box(box, 128)
    mid = v[1:-1]
    return scale * (27.0 * mid - box) + shift * mid


def pair_planes(quads, rows_ref):
    parts = []
    for k, t in enumerate(quads):
        halves = []
        for i in (0, 2):
            at = 40 * (2 * k + i // 2)
            rows_ref[at : at + 40] = t[i] + t[i + 1]
            halves.append(
                rows_ref[pl.ds(at + 4, 16, stride=2)] + rows_ref[pl.ds(at + 5, 16, stride=2)]
            )
        parts.append(jnp.concatenate(halves, axis=1))
    lane, out = iota((256, 128), 0), iota((256, 128), 1)
    pack = ones_where(lane // 2 == out, 0.125)
    return dot(jnp.concatenate(parts, axis=0), pack).reshape(len(quads), 16, 128)


def edge_kernel(own_ref, first_ref, last_ref):
    for k in range(3):
        for p in range(4):
            at = 10 * (4 * k + p)
            first_ref[at : at + 10] = own_ref[k, p, :10]
            last_ref[at : at + 10] = own_ref[k, p, 6:]


def block_kernel(own_ref, before_ref, after_ref, block_ref, face_ref):
    left = lax.axis_index("c") == 0
    none = jnp.zeros((2, 128), F32)
    for k in range(3):
        for p in range(4):
            at = 10 * (4 * k + p)
            block_ref[k, p, 12:28] = own_ref[k, p]
            block_ref[k, p, 2:12] = before_ref[at : at + 10]
            block_ref[k, p, 28:38] = after_ref[at : at + 10]
            block_ref[k, p, :2] = none
            block_ref[k, p, 38:] = none
    for k in range(3):
        for p in range(2):
            at = 40 * (2 * k + p)
            face_ref[at : at + 40] = jnp.where(left, block_ref[k, p], block_ref[k, p + 2])
        at = 240 + 24 * k
        rows = slice(8, 32)
        face_ref[at : at + 24] = jnp.where(left, block_ref[k, 2, rows], block_ref[k, 1, rows])
    face_ref[312:] = jnp.where(left, block_ref[1, 3, rows], block_ref[1, 0, rows])


def fine_kernel(
    own_ref, mate_ref, face_ref, iter_ref, field_ref, piece_ref, one_ref, coef_rows, rows_ref
):
    left = lax.axis_index("c") == 0
    blocks = []
    for k in range(3):
        mate = mate_ref[k]
        near = face_ref[80 * k : 80 * k + 80].reshape(2, 40, 128)
        pad = jnp.zeros((1, 8, 128), F32)
        third = face_ref[240 + 24 * k : 264 + 24 * k][None]
        fourth = face_ref[312:][None] if k == 1 else jnp.zeros_like(third)
        third, fourth = (
            jnp.concatenate([pad, t, pad], axis=1) for t in (third, fourth)
        )
        before = jnp.where(left, jnp.concatenate([fourth, third, near], axis=0), mate)
        after = jnp.where(left, mate, jnp.concatenate([near, third, fourth], axis=0))
        blocks.append(jnp.concatenate([before, own_ref[k], after], axis=0))
    f, a, s = blocks
    coefs = pair_planes([t[4 * p : 4 * p + 4] for t in (a, s) for p in range(3)], coef_rows)
    w = relax_weight(a[1:11], s[1:11], 1.0)
    u = w * f[1:11]
    u = u[1:-1] + w[1:-1] * (f[2:10] - fine_apply(u, a[2:10], s[2:10]))
    iter_ref[...] = u[:, 8:32]
    for k, t in enumerate((f[2:10], a[2:10], s[2:10], w[1:9])):
        field_ref[k] = t[:, 8:32]
    resid = f[4:8] - fine_apply(u[1:7], a[4:8], s[4:8])
    f = pair_planes([resid], rows_ref)
    a, s = coefs[:3], coefs[3:]
    for k, t in enumerate((f[0], a[1], s[1])):
        one_ref[k] = t

    none = jnp.zeros_like(f)
    f = jnp.concatenate([none, f, none], axis=0)
    w = relax_weight(a, s, 0.25)
    v = w * f
    v = v + w * (f - middle_apply(v, a, s))
    resid = f - middle_apply(v, a, s)
    spread = ones_where(iota((128, 128), 1) % 32 == (iota((128, 128), 0) % 64) // 2, 0.125)
    own = ones_where(iota((16, 128), 0) // 2 == iota((16, 128), 1) // 32 + 2)
    mixed = dot(resid.reshape(48, 128), spread).reshape(3, 16, 128)
    rows = [mixed[k] * own for k in range(3)]
    mixed = dot(jnp.concatenate([a[1], s[1]], axis=0), spread).reshape(2, 16, 128)
    rows += [mixed[k] * own for k in range(2)] + [jnp.zeros((1, 128), F32)] * 3
    piece = jnp.concatenate([jnp.sum(t, axis=0, keepdims=True) for t in rows], axis=0)
    piece_ref[...] = jnp.broadcast_to(piece[None], piece_ref.shape)


def middle_apply(v, scale, shift):
    rows = v.shape[1]
    lane = iota((rows, 128), 1)
    row = iota((rows, 128), 0)
    swap = pltpu.roll(v, 64, 2)
    edge = jnp.zeros_like(swap[:1])
    prev = jnp.concatenate([edge, swap[:-1]], axis=0)
    later = jnp.concatenate([swap[1:], edge], axis=0)
    box = v + swap + jnp.where(lane < 64, prev, later)
    box = (
        box
        + jnp.where(row > 0, pltpu.roll(box, 1, 1), 0.0)
        + jnp.where(row < rows - 1, pltpu.roll(box, rows - 1, 1), 0.0)
    )
    box = lane_box(box, 64)
    return 0.25 * scale * (27.0 * v - box) + shift * v


def quarter_row(shape, dim):
    i = iota(shape, dim)
    return 4 * (i % 8) + i // 8


def quarter_mask():
    return ones_where(iota((4, 8, 128), 2) // 32 == iota((4, 8, 128), 0))


def gather_kernel(got_ref, piece_ref, rows_ref):
    core = lax.axis_index("c")
    half = got_ref.shape[0] // 2
    rows_ref[: 2 * half] = got_ref[...]

    def column(at, k):
        return rows_ref[pl.ds(at * half + k, half // 8, stride=8)]

    outward = 2 * core
    piece = jnp.concatenate(
        [
            column(core, outward),
            column(core, 1) + column(1 - core, outward),
            column(core, 3),
            column(core, 4),
        ],
        axis=0,
    )
    piece_ref[...] = jnp.broadcast_to(piece[None], piece_ref.shape)


def smooth_kernel(
    own_ref, mate_ref, outer_ref, inner_ref, field_ref, iter_ref, matrix_ref
):
    left = lax.axis_index("c") == 0
    for k in range(3):
        mate, outer, inner = mate_ref[k], outer_ref[:, k], inner_ref[k]
        field_ref[k, 0] = jnp.where(left, outer[0], inner)
        field_ref[k, 1] = jnp.where(left, outer[1], mate)
        field_ref[k, 2] = own_ref[k]
        field_ref[k, 3] = jnp.where(left, mate, outer[0])
        field_ref[k, 4] = jnp.where(left, inner, outer[1])
    f, a, s = (field_ref[k] for k in range(3))
    w = relax_weight(a, s, 0.25)
    field_ref[3] = w
    v = w * f
    iter_ref[...] = v + w * (f - middle_apply(v, a, s))
    matrix_ref[...] = box_matrix()


def box_matrix():
    lane, out = iota((256, 256), 0) % 128, iota((256, 256), 1)
    group, to = lane // 32, out % 128 // 32
    near = jnp.abs(lane % 32 - out % 32) <= 1
    same = (out < 128) & (jnp.abs(group - to) <= 1)
    wrap = (out >= 128) & (jnp.abs(group - to) == 3)
    return ones_where(near & (same | wrap)).astype(jnp.bfloat16)


def coarse_box(v, matrix):
    rows = (v[:-2] + v[1:-1] + v[2:]).reshape(-1, 128)
    high = rows.astype(jnp.bfloat16)
    low = (rows - high.astype(F32)).astype(jnp.bfloat16)
    both = lax.dot_general(
        jnp.concatenate([high, low], axis=1),
        matrix,
        (((1,), (0,)), ((), ())),
        preferred_element_type=F32,
    )
    box, wrap = (both[:, k : k + 128].reshape(-1, 8, 128) for k in (0, 128))
    lane, row = iota((8, 128), 1), iota((8, 128), 0)
    up = jnp.where((lane < 32) & (row > 0), pltpu.roll(wrap, 1, 1), 0.0)
    down = jnp.where((lane >= 96) & (row < 7), pltpu.roll(wrap, 7, 1), 0.0)
    return box + up + down


def total(plane):
    return jnp.sum(jnp.sum(plane, axis=0, keepdims=True), axis=1, keepdims=True)


def solve_coarse(q_ref, a_ref, d_ref, inverse_ref, z_ref, image_ref, e_ref, matrix):
    planes = q_ref.shape[0]
    chunk = 16 if planes % 16 == 0 else 2
    starts = range(0, planes, chunk)
    none = jnp.zeros((1, 8, 128), F32)
    z_ref[:1] = none
    z_ref[planes + 1 :] = none
    for i in (0, 1, planes + 2, planes + 3):
        e_ref[i : i + 1] = none
    for i in starts:
        own = slice(i, i + chunk)
        inverse = 1.0 / (d_ref[own] - a_ref[own])
        inverse_ref[own] = inverse
        z_ref[i + 1 : i + chunk + 1] = q_ref[own] * inverse
    for step in range(COARSE):
        upper = lower = jnp.zeros((8, 128), F32)
        for i in starts:
            own = slice(i, i + chunk)
            z = z_ref[i : i + chunk + 2]
            image = d_ref[own] * z[1:-1] - a_ref[own] * coarse_box(z, matrix)
            image_ref[own] = image
            upper = upper + jnp.sum(image * q_ref[own], axis=0)
            lower = lower + jnp.sum(image * image, axis=0)
        alpha = (total(upper) / total(lower))[None]
        for i in starts:
            own = slice(i, i + chunk)
            inner = slice(i + 1, i + chunk + 1)
            outer = slice(i + 2, i + chunk + 2)
            gain = alpha * z_ref[inner]
            e_ref[outer] = gain if step == 0 else e_ref[outer] + gain
            if step < COARSE - 1:
                q = q_ref[own] - alpha * image_ref[own]
                q_ref[own] = q
                z_ref[inner] = q * inverse_ref[own]


def last_kernel(
    got_ref, mate_ref, matrix_ref, field_ref, middle_ref, fine_ref, iter_ref, out_ref,
    q_ref, a_ref, d_ref, inverse_ref, z_ref, image_ref, coarse_ref, middle_rows, fine_rows,
):
    nx = lax.axis_size("x")
    chip = lax.axis_index("y") * nx + lax.axis_index("x")
    core = lax.axis_index("c")
    rank = lax.axis_index("z")
    planes = 2 * got_ref.shape[0]

    got, mate = got_ref[...], mate_ref[...]
    halves = jnp.where(core == 0, got, mate), jnp.where(core == 0, mate, got)

    def part(half, k):
        return halves[half][:, 8 * k : 8 * k + 8]

    def pairs(first, second):
        return jnp.concatenate([first[:, None], second[:, None]], axis=1).reshape(planes, 8, 128)

    edge = jnp.zeros_like(part(0, 0)[:1])
    q_ref[...] = pairs(
        part(0, 1) + jnp.concatenate([edge, part(1, 0)[:-1]], axis=0),
        part(1, 1) + jnp.concatenate([part(0, 0)[1:], edge], axis=0),
    )
    a = 0.0625 * pairs(part(0, 2), part(1, 2))
    a_ref[...] = a
    d_ref[...] = 27.0 * a + pairs(part(0, 3), part(1, 3))
    solve_coarse(
        q_ref, a_ref, d_ref, inverse_ref, z_ref, image_ref, coarse_ref, matrix_ref[...]
    )
    near = coarse_ref[pl.ds(chip * 2 + core, 5)]

    mask = quarter_mask()
    stack = jnp.concatenate([(near[p][None] * mask).reshape(32, 128) for p in range(5)], axis=0)
    spread = ones_where(iota((128, 128), 0) % 32 == (iota((128, 128), 1) % 64) // 2)
    mixed = dot(stack, spread)
    size = (middle_rows.shape[0] - 16) // 5
    edge = jnp.zeros((4, 128), F32)
    window = []
    for p in range(5):
        at = size * p
        middle_rows[at : at + 4] = edge
        middle_rows[at + size - 4 : at + size] = edge
        for k in range(4):
            t = mixed[32 * p + 8 * k : 32 * p + 8 * k + 8]
            for i in (4, 5):
                middle_rows[pl.ds(at + 2 * k + i, 8, stride=8)] = t
        window.append(middle_rows[pl.ds(pl.multiple_of(at + rank * 8, 8), 16)][None])
    v = middle_ref[...] + jnp.concatenate(window, axis=0)
    f, a, s, w = (field_ref[k] for k in range(4))
    for _ in range(2):
        v = v + w * (f - middle_apply(v, a, s))

    lane, out = iota((128, 256), 0), iota((128, 256), 1)
    mixed = dot(v[1:4].reshape(48, 128), ones_where(lane == out // 2))
    halves = [mixed[:16, 128:], mixed[16:32, :128], mixed[16:32, 128:], mixed[32:, :128]]
    refined = []
    for p, t in enumerate(halves):
        for i in range(2):
            fine_rows[pl.ds(24 * p + i, 12, stride=2)] = t[2:14]
        refined += [fine_rows[24 * p : 24 * p + 24][None]] * 2
    refined = jnp.concatenate(refined, axis=0)

    f, a, s, w = (fine_ref[k] for k in range(4))
    u = iter_ref[...] + jnp.where(a > 0.25, refined, 0.0)
    for i in (1, 2):
        j = 8 - i
        u = u[1:-1] + w[i:j] * (f[i:j] - fine_apply(u, a[i:j], s[i:j]))
    out_ref[...] = u[:, 4:20]


def call(kernel, outs, *args, scratch=()):
    return pl.pallas_call(
        kernel,
        out_shape=[
            jax.ShapeDtypeStruct(*(out if isinstance(out[0], tuple) else (out, F32)))
            for out in outs
        ],
        in_specs=[pl.BlockSpec(memory_space=pltpu.VMEM)] * len(args),
        out_specs=[pl.BlockSpec(memory_space=pltpu.VMEM)] * len(outs),
        scratch_shapes=[pltpu.VMEM(shape, F32) for shape in scratch],
        compiler_params=pltpu.CompilerParams(vmem_limit_bytes=24 * 2**20),
    )(*args)


def shards(source, row_scale, shift_field):
    ny, nx, nz = lax.axis_size("y"), lax.axis_size("x"), lax.axis_size("z")
    chips = ny * nx
    first = lax.axis_index("c") == 0

    own = jnp.stack([source, row_scale, shift_field])
    head, tail = call(edge_kernel, [(120, 128), (120, 128)], own)
    up = [(i, i + 1) for i in range(nz - 1)]
    down = [(i + 1, i) for i in range(nz - 1)]
    before = lax.ppermute(tail, "z", up)
    after = lax.ppermute(head, "z", down)
    own, face = call(block_kernel, [(3, 4, 40, 128), (336, 128)], own, before, after)
    facing = []
    for i in range(chips - 1):
        facing += [(2 * i + 1, 2 * i + 2), (2 * i + 2, 2 * i + 1)]
    swap = [(0, 1), (1, 0)]
    face = lax.ppermute(face, ("y", "x", "c"), facing)
    mate = lax.ppermute(own, "c", swap)
    fine_iter, fine_fields, sent, one = call(
        fine_kernel,
        [(8, 24, 128), (4, 8, 24, 128), (2 * nz, 8, 128), (3, 16, 128)],
        own, mate, face,
        scratch=[(12 * 40 + 16, 128), (2 * 40 + 16, 128)],
    )

    got = lax.all_to_all(sent, ("c", "z"), 0, 0).reshape(16 * nz, 128)
    (sent,) = call(
        gather_kernel, [(chips, 32, 128)], got, scratch=[(16 * nz + 16, 128)]
    )
    one, sent = lax.optimization_barrier((one, sent))
    half = lax.all_to_all(sent, ("y", "x"), 0, 0)

    mate = lax.ppermute(one, "c", swap)
    pairs = jnp.stack([jnp.where(first, one, mate), jnp.where(first, mate, one)])
    ring = []
    for i in range(chips - 1):
        ring += [(2 * i, 2 * i + 2), (2 * i + 3, 2 * i + 1)]
    outer = lax.ppermute(pairs, ("y", "x", "c"), ring)
    inner = lax.ppermute(one, ("y", "x", "c"), [(j, i) for i, j in ring])
    fields, middle_iter, matrix = call(
        smooth_kernel,
        [(4, 5, 16, 128), (5, 16, 128), ((256, 256), jnp.bfloat16)],
        one, mate, outer, inner,
    )
    half, fields, middle_iter = lax.optimization_barrier((half, fields, middle_iter))
    half_mate = lax.ppermute(half, "c", swap)
    (result,) = call(
        last_kernel, [source.shape],
        half, half_mate, matrix, fields, middle_iter, fine_fields, fine_iter,
        scratch=[(2 * chips, 8, 128)] * 4
        + [(2 * chips + 2, 8, 128), (2 * chips, 8, 128), (2 * chips + 4, 8, 128)]
        + [(5 * (8 * nz + 8) + 16, 128), (4 * 24 + 16, 128)],
    )
    return result


def solution(mesh):
    ny, nx = (8, 4) if mesh.devices.shape[0] == 64 else (mesh.devices.shape[0] // 2, 1)
    nz = mesh.devices.shape[1]
    split = Mesh(mesh.devices.reshape(ny, nx, 2, nz), ("y", "x", "c", "z"))
    spec = P(("y", "x", "c"), "z", None)
    return jax.shard_map(
        shards, mesh=split, in_specs=(spec, spec, spec), out_specs=spec, check_vma=False
    )
```

```python
import jax
import jax.numpy as jnp
from jax import lax
from jax.experimental import pallas as pl
from jax.experimental.pallas import tpu as pltpu
from jax.sharding import Mesh, PartitionSpec as P

COARSE = 4
DAMPING = 0.8
F32 = jnp.float32


def dot(a, b):
    high = a.astype(jnp.bfloat16)
    rest = a - high.astype(F32)
    middle = rest.astype(jnp.bfloat16)
    low = (rest - middle.astype(F32)).astype(jnp.bfloat16)
    parts = lax.dot_general(
        jnp.concatenate([high, middle, low], axis=0),
        b.astype(jnp.bfloat16),
        (((1,), (0,)), ((), ())),
        preferred_element_type=F32,
    )
    n = a.shape[0]
    return parts[:n] + parts[n : 2 * n] + parts[2 * n :]


def iota(shape, dim):
    return lax.broadcasted_iota(jnp.int32, shape, dim)


def ones_where(cond, value=1.0):
    return jnp.where(cond, jnp.float32(value), jnp.float32(0.0))


def lane_box(v, period):
    axis = v.ndim - 1
    lane = iota(v.shape[-2:], 1) % period
    below = jnp.where(lane > 0, pltpu.roll(v, 1, axis), 0.0)
    above = jnp.where(lane < period - 1, pltpu.roll(v, 127, axis), 0.0)
    return v + below + above


def relax_weight(scale, shift, level_scale):
    inside = scale > 0.25
    diag = jnp.where(inside, 26.0 * level_scale * scale + shift, 1.0)
    return jnp.where(inside, DAMPING / diag, 0.0)


def fine_apply(v, scale, shift):
    rows = v.shape[1]
    box = v[:-2] + v[1:-1] + v[2:]
    box = box + pltpu.roll(box, 1, 1) + pltpu.roll(box, rows - 1, 1)
    box = lane_box(box, 128)
    mid = v[1:-1]
    return scale * (27.0 * mid - box) + shift * mid


def pair_planes(quads, rows_ref):
    parts = []
    for k, t in enumerate(quads):
        halves = []
        for i in (0, 2):
            at = 40 * (2 * k + i // 2)
            rows_ref[at : at + 40] = t[i] + t[i + 1]
            halves.append(
                rows_ref[pl.ds(at + 4, 16, stride=2)] + rows_ref[pl.ds(at + 5, 16, stride=2)]
            )
        parts.append(jnp.concatenate(halves, axis=1))
    lane, out = iota((256, 128), 0), iota((256, 128), 1)
    pack = ones_where(lane // 2 == out, 0.125)
    return dot(jnp.concatenate(parts, axis=0), pack).reshape(len(quads), 16, 128)


def edge_kernel(own_ref, first_ref, last_ref):
    for k in range(3):
        for p in range(4):
            at = 10 * (4 * k + p)
            first_ref[at : at + 10] = own_ref[k, p, :10]
            last_ref[at : at + 10] = own_ref[k, p, 6:]


def block_kernel(own_ref, before_ref, after_ref, block_ref, face_ref, mate_ref):
    left = lax.axis_index("c") == 0
    none = jnp.zeros((2, 128), F32)
    for k in range(3):
        for p in range(4):
            at = 10 * (4 * k + p)
            block_ref[k, p, 12:28] = own_ref[k, p]
            block_ref[k, p, 2:12] = before_ref[at : at + 10]
            block_ref[k, p, 28:38] = after_ref[at : at + 10]
            block_ref[k, p, :2] = none
            block_ref[k, p, 38:] = none

    def send(at, k, low, high, rows):
        low, high = block_ref[k, low, rows], block_ref[k, high, rows]
        size = low.shape[0]
        face_ref[at : at + size] = jnp.where(left, low, high)
        mate_ref[at : at + size] = jnp.where(left, high, low)

    for k in range(3):
        for p in range(2):
            send(40 * (2 * k + p), k, p, p + 2, slice(0, 40))
        send(240 + 24 * k, k, 2, 1, slice(8, 32))
    send(312, 1, 3, 0, slice(8, 32))
    face_ref[336:] = jnp.zeros((8, 128), F32)


def fine_kernel(
    own_ref, mate_ref, face_ref, iter_ref, field_ref, piece_ref, one_ref, coef_rows, rows_ref
):
    left = lax.axis_index("c") == 0
    face, mate = face_ref[:336], mate_ref[...]
    low, high = jnp.where(left, face, mate), jnp.where(left, mate, face)
    pad = jnp.zeros((1, 8, 128), F32)
    blocks = []
    for k in range(3):
        sides = []
        for t in (low, high):
            far = [t[240 + 24 * k : 264 + 24 * k], t[312:]]
            if k != 1:
                far[1] = jnp.zeros_like(far[1])
            far = [jnp.concatenate([pad, u[None], pad], axis=1) for u in far]
            sides.append([t[80 * k : 80 * k + 80].reshape(2, 40, 128)] + far)
        blocks.append(jnp.concatenate(sides[0][::-1] + [own_ref[k]] + sides[1], axis=0))
    f, a, s = blocks
    coefs = pair_planes([t[4 * p : 4 * p + 4] for t in (a, s) for p in range(3)], coef_rows)
    w = relax_weight(a[1:11], s[1:11], 1.0)
    u = w * f[1:11]
    u = u[1:-1] + w[1:-1] * (f[2:10] - fine_apply(u, a[2:10], s[2:10]))
    iter_ref[...] = u[:, 8:32]
    for k, t in enumerate((f[2:10], a[2:10], s[2:10], w[1:9])):
        field_ref[k] = t[:, 8:32]
    resid = f[4:8] - fine_apply(u[1:7], a[4:8], s[4:8])
    f = pair_planes([resid], rows_ref)
    a, s = coefs[:3], coefs[3:]
    for k, t in enumerate((f[0], a[1], s[1])):
        one_ref[k] = t

    none = jnp.zeros_like(f)
    f = jnp.concatenate([none, f, none], axis=0)
    w = relax_weight(a, s, 0.25)
    v = w * f
    v = v + w * (f - middle_apply(v, a, s))
    resid = f - middle_apply(v, a, s)
    spread = ones_where(iota((128, 128), 1) % 32 == (iota((128, 128), 0) % 64) // 2, 0.125)
    own = ones_where(iota((16, 128), 0) // 2 == iota((16, 128), 1) // 32 + 2)
    mixed = dot(resid.reshape(48, 128), spread).reshape(3, 16, 128)
    rows = [mixed[k] * own for k in range(3)]
    mixed = dot(jnp.concatenate([a[1], s[1]], axis=0), spread).reshape(2, 16, 128)
    rows += [mixed[k] * own for k in range(2)] + [jnp.zeros((1, 128), F32)] * 3
    piece = jnp.concatenate([jnp.sum(t, axis=0, keepdims=True) for t in rows], axis=0)
    piece_ref[...] = jnp.broadcast_to(piece[None], piece_ref.shape)


def middle_apply(v, scale, shift):
    rows = v.shape[1]
    lane = iota((rows, 128), 1)
    row = iota((rows, 128), 0)
    swap = pltpu.roll(v, 64, 2)
    edge = jnp.zeros_like(swap[:1])
    prev = jnp.concatenate([edge, swap[:-1]], axis=0)
    later = jnp.concatenate([swap[1:], edge], axis=0)
    box = v + swap + jnp.where(lane < 64, prev, later)
    box = (
        box
        + jnp.where(row > 0, pltpu.roll(box, 1, 1), 0.0)
        + jnp.where(row < rows - 1, pltpu.roll(box, rows - 1, 1), 0.0)
    )
    box = lane_box(box, 64)
    return 0.25 * scale * (27.0 * v - box) + shift * v


def quarter_row(shape, dim):
    i = iota(shape, dim)
    return 4 * (i % 8) + i // 8


def quarter_mask():
    return ones_where(iota((4, 8, 128), 2) // 32 == iota((4, 8, 128), 0))


def gather_kernel(got_ref, piece_ref, rows_ref):
    core = lax.axis_index("c")
    half = got_ref.shape[0] // 2
    rows_ref[: 2 * half] = got_ref[...]

    def column(at, k):
        return rows_ref[pl.ds(at * half + k, half // 8, stride=8)]

    outward = 2 * core
    piece = jnp.concatenate(
        [
            column(core, outward),
            column(core, 1) + column(1 - core, outward),
            column(core, 3),
            column(core, 4),
        ],
        axis=0,
    )
    piece_ref[...] = jnp.broadcast_to(piece[None], piece_ref.shape)


def smooth_kernel(
    own_ref, mate_ref, outer_ref, inner_ref, field_ref, iter_ref, matrix_ref
):
    left = lax.axis_index("c") == 0
    for k in range(3):
        mate, outer, inner = mate_ref[k], outer_ref[:, k], inner_ref[k]
        field_ref[k, 0] = jnp.where(left, outer[0], inner)
        field_ref[k, 1] = jnp.where(left, outer[1], mate)
        field_ref[k, 2] = own_ref[k]
        field_ref[k, 3] = jnp.where(left, mate, outer[0])
        field_ref[k, 4] = jnp.where(left, inner, outer[1])
    f, a, s = (field_ref[k] for k in range(3))
    w = relax_weight(a, s, 0.25)
    field_ref[3] = w
    v = w * f
    iter_ref[...] = v + w * (f - middle_apply(v, a, s))
    matrix_ref[...] = box_matrix()


def box_matrix():
    lane, out = iota((256, 256), 0) % 128, iota((256, 256), 1)
    group, to = lane // 32, out % 128 // 32
    near = jnp.abs(lane % 32 - out % 32) <= 1
    same = (out < 128) & (jnp.abs(group - to) <= 1)
    wrap = (out >= 128) & (jnp.abs(group - to) == 3)
    return ones_where(near & (same | wrap)).astype(jnp.bfloat16)


def coarse_box(v, matrix):
    rows = (v[:-2] + v[1:-1] + v[2:]).reshape(-1, 128)
    high = rows.astype(jnp.bfloat16)
    low = (rows - high.astype(F32)).astype(jnp.bfloat16)
    both = lax.dot_general(
        jnp.concatenate([high, low], axis=1),
        matrix,
        (((1,), (0,)), ((), ())),
        preferred_element_type=F32,
    )
    box, wrap = (both[:, k : k + 128].reshape(-1, 8, 128) for k in (0, 128))
    lane, row = iota((8, 128), 1), iota((8, 128), 0)
    up = jnp.where((lane < 32) & (row > 0), pltpu.roll(wrap, 1, 1), 0.0)
    down = jnp.where((lane >= 96) & (row < 7), pltpu.roll(wrap, 7, 1), 0.0)
    return box + up + down


def total(plane):
    return jnp.sum(jnp.sum(plane, axis=0, keepdims=True), axis=1, keepdims=True)


def solve_coarse(q_ref, a_ref, d_ref, inverse_ref, w_ref, y_ref, at, matrix):
    planes = a_ref.shape[0]
    chunk = 16 if planes % 16 == 0 else 2
    starts = range(0, planes, chunk)
    none = jnp.zeros((2, 8, 128), F32)
    for ref in (q_ref, inverse_ref, w_ref):
        ref[:2] = none
        ref[planes + 2 :] = none
    for i in starts:
        own, padded = slice(i, i + chunk), slice(i + 2, i + chunk + 2)
        inverse_ref[padded] = 1.0 / (d_ref[own] - a_ref[own])

    def product(ref):
        for i in starts:
            own, wide = slice(i, i + chunk), slice(i + 1, i + chunk + 3)
            z = ref[wide] * inverse_ref[wide]
            y_ref[own] = d_ref[own] * z[1:-1] - a_ref[own] * coarse_box(z, matrix)

    product(q_ref)
    solution = jnp.zeros((5, 8, 128), F32)
    for step in range(COARSE):
        upper = lower = jnp.zeros((8, 128), F32)
        for i in starts:
            own, padded = slice(i, i + chunk), slice(i + 2, i + chunk + 2)
            w, q = y_ref[own], q_ref[padded]
            if step > 0:
                old = w_ref[padded]
                w, q = old - alpha * w, q - alpha * old
                q_ref[padded] = q
            w_ref[padded] = w
            upper = upper + jnp.sum(w * q, axis=0)
            lower = lower + jnp.sum(w * w, axis=0)
        alpha = (total(upper) / total(lower))[None]
        if step < COARSE - 1:
            product(w_ref)
        solution = solution + alpha * q_ref[pl.ds(at, 5)]
    return solution * inverse_ref[pl.ds(at, 5)]


def last_kernel(
    got_ref, mate_ref, matrix_ref, field_ref, middle_ref, fine_ref, iter_ref, out_ref,
    q_ref, a_ref, d_ref, inverse_ref, w_ref, y_ref, middle_rows, fine_rows,
):
    nx = lax.axis_size("x")
    chip = lax.axis_index("y") * nx + lax.axis_index("x")
    core = lax.axis_index("c")
    rank = lax.axis_index("z")
    planes = 2 * got_ref.shape[0]

    got, mate = got_ref[...], mate_ref[...]
    halves = jnp.where(core == 0, got, mate), jnp.where(core == 0, mate, got)

    def part(half, k):
        return halves[half][:, 8 * k : 8 * k + 8]

    def pairs(first, second):
        return jnp.concatenate([first[:, None], second[:, None]], axis=1).reshape(planes, 8, 128)

    edge = jnp.zeros_like(part(0, 0)[:1])
    q_ref[2 : planes + 2] = pairs(
        part(0, 1) + jnp.concatenate([edge, part(1, 0)[:-1]], axis=0),
        part(1, 1) + jnp.concatenate([part(0, 0)[1:], edge], axis=0),
    )
    a = 0.0625 * pairs(part(0, 2), part(1, 2))
    a_ref[...] = a
    d_ref[...] = 27.0 * a + pairs(part(0, 3), part(1, 3))
    near = solve_coarse(
        q_ref, a_ref, d_ref, inverse_ref, w_ref, y_ref, chip * 2 + core, matrix_ref[...]
    )

    mask = quarter_mask()
    stack = jnp.concatenate([(near[p][None] * mask).reshape(32, 128) for p in range(5)], axis=0)
    spread = ones_where(iota((128, 128), 0) % 32 == (iota((128, 128), 1) % 64) // 2)
    mixed = dot(stack, spread)
    size = (middle_rows.shape[0] - 16) // 5
    edge = jnp.zeros((4, 128), F32)
    window = []
    for p in range(5):
        at = size * p
        middle_rows[at : at + 4] = edge
        middle_rows[at + size - 4 : at + size] = edge
        for k in range(4):
            t = mixed[32 * p + 8 * k : 32 * p + 8 * k + 8]
            for i in (4, 5):
                middle_rows[pl.ds(at + 2 * k + i, 8, stride=8)] = t
        window.append(middle_rows[pl.ds(pl.multiple_of(at + rank * 8, 8), 16)][None])
    v = middle_ref[...] + jnp.concatenate(window, axis=0)
    f, a, s, w = (field_ref[k] for k in range(4))
    for _ in range(2):
        v = v + w * (f - middle_apply(v, a, s))

    lane, out = iota((128, 256), 0), iota((128, 256), 1)
    mixed = dot(v[1:4].reshape(48, 128), ones_where(lane == out // 2))
    halves = [mixed[:16, 128:], mixed[16:32, :128], mixed[16:32, 128:], mixed[32:, :128]]
    refined = []
    for p, t in enumerate(halves):
        for i in range(2):
            fine_rows[pl.ds(24 * p + i, 12, stride=2)] = t[2:14]
        refined += [fine_rows[24 * p : 24 * p + 24][None]] * 2
    refined = jnp.concatenate(refined, axis=0)

    f, a, s, w = (fine_ref[k] for k in range(4))
    u = iter_ref[...] + jnp.where(a > 0.25, refined, 0.0)
    for i in (1, 2):
        j = 8 - i
        u = u[1:-1] + w[i:j] * (f[i:j] - fine_apply(u, a[i:j], s[i:j]))
    out_ref[...] = u[:, 4:20]


def call(kernel, outs, *args, scratch=()):
    return pl.pallas_call(
        kernel,
        out_shape=[
            jax.ShapeDtypeStruct(*(out if isinstance(out[0], tuple) else (out, F32)))
            for out in outs
        ],
        in_specs=[pl.BlockSpec(memory_space=pltpu.VMEM)] * len(args),
        out_specs=[pl.BlockSpec(memory_space=pltpu.VMEM)] * len(outs),
        scratch_shapes=[pltpu.VMEM(shape, F32) for shape in scratch],
        compiler_params=pltpu.CompilerParams(vmem_limit_bytes=24 * 2**20),
    )(*args)


def shards(source, row_scale, shift_field):
    ny, nx, nz = lax.axis_size("y"), lax.axis_size("x"), lax.axis_size("z")
    chips = ny * nx
    first = lax.axis_index("c") == 0

    own = jnp.stack([source, row_scale, shift_field])
    head, tail = call(edge_kernel, [(120, 128), (120, 128)], own)
    up = [(i, i + 1) for i in range(nz - 1)]
    down = [(i + 1, i) for i in range(nz - 1)]
    before = lax.ppermute(tail, "z", up)
    after = lax.ppermute(head, "z", down)
    own, face, mate = call(
        block_kernel, [(3, 4, 40, 128), (344, 128), (336, 128)], own, before, after
    )
    facing = []
    for i in range(chips - 1):
        facing += [(2 * i + 1, 2 * i + 2), (2 * i + 2, 2 * i + 1)]
    swap = [(0, 1), (1, 0)]
    face = lax.ppermute(face, ("y", "x", "c"), facing)
    mate = lax.ppermute(mate, "c", swap)
    fine_iter, fine_fields, sent, one = call(
        fine_kernel,
        [(8, 24, 128), (4, 8, 24, 128), (2 * nz, 8, 128), (3, 16, 128)],
        own, mate, face,
        scratch=[(12 * 40 + 16, 128), (2 * 40 + 16, 128)],
    )

    got = lax.all_to_all(sent, ("c", "z"), 0, 0).reshape(16 * nz, 128)
    (sent,) = call(
        gather_kernel, [(chips, 32, 128)], got, scratch=[(16 * nz + 16, 128)]
    )
    one, sent = lax.optimization_barrier((one, sent))
    half = lax.all_to_all(sent, ("y", "x"), 0, 0)

    mate = lax.ppermute(one, "c", swap)
    pairs = jnp.stack([jnp.where(first, one, mate), jnp.where(first, mate, one)])
    ring = []
    for i in range(chips - 1):
        ring += [(2 * i, 2 * i + 2), (2 * i + 3, 2 * i + 1)]
    outer = lax.ppermute(pairs, ("y", "x", "c"), ring)
    inner = lax.ppermute(one, ("y", "x", "c"), [(j, i) for i, j in ring])
    fields, middle_iter, matrix = call(
        smooth_kernel,
        [(4, 5, 16, 128), (5, 16, 128), ((256, 256), jnp.bfloat16)],
        one, mate, outer, inner,
    )
    half, fields, middle_iter = lax.optimization_barrier((half, fields, middle_iter))
    half_mate = lax.ppermute(half, "c", swap)
    (result,) = call(
        last_kernel, [source.shape],
        half, half_mate, matrix, fields, middle_iter, fine_fields, fine_iter,
        scratch=[(2 * chips + 4, 8, 128)] + [(2 * chips, 8, 128)] * 2
        + [(2 * chips + 4, 8, 128)] * 2 + [(2 * chips, 8, 128)]
        + [(5 * (8 * nz + 8) + 16, 128), (4 * 24 + 16, 128)],
    )
    return result


def solution(mesh):
    ny, nx = (8, 4) if mesh.devices.shape[0] == 64 else (mesh.devices.shape[0] // 2, 1)
    nz = mesh.devices.shape[1]
    split = Mesh(mesh.devices.reshape(ny, nx, 2, nz), ("y", "x", "c", "z"))
    spec = P(("y", "x", "c"), "z", None)
    return jax.shard_map(
        shards, mesh=split, in_specs=(spec, spec, spec), out_specs=spec, check_vma=False
    )
```

```python
import jax
import jax.numpy as jnp
from jax import lax
from jax.experimental import pallas as pl
from jax.experimental.pallas import tpu as pltpu
from jax.sharding import Mesh, PartitionSpec as P

COARSE = 4
DAMPING = 0.8
F32 = jnp.float32


def dot(a, b):
    high = a.astype(jnp.bfloat16)
    rest = a - high.astype(F32)
    middle = rest.astype(jnp.bfloat16)
    low = (rest - middle.astype(F32)).astype(jnp.bfloat16)
    parts = lax.dot_general(
        jnp.concatenate([high, middle, low], axis=0),
        b.astype(jnp.bfloat16),
        (((1,), (0,)), ((), ())),
        preferred_element_type=F32,
    )
    n = a.shape[0]
    return parts[:n] + parts[n : 2 * n] + parts[2 * n :]


def iota(shape, dim):
    return lax.broadcasted_iota(jnp.int32, shape, dim)


def ones_where(cond, value=1.0):
    return jnp.where(cond, jnp.float32(value), jnp.float32(0.0))


def lane_box(v, period):
    axis = v.ndim - 1
    lane = iota(v.shape[-2:], 1) % period
    below = jnp.where(lane > 0, pltpu.roll(v, 1, axis), 0.0)
    above = jnp.where(lane < period - 1, pltpu.roll(v, 127, axis), 0.0)
    return v + below + above


def relax_weight(scale, shift, level_scale):
    inside = scale > 0.25
    diag = jnp.where(inside, 26.0 * level_scale * scale + shift, 1.0)
    return jnp.where(inside, DAMPING / diag, 0.0)


def fine_apply(v, scale, shift):
    rows = v.shape[1]
    box = v[:-2] + v[1:-1] + v[2:]
    box = box + pltpu.roll(box, 1, 1) + pltpu.roll(box, rows - 1, 1)
    box = lane_box(box, 128)
    mid = v[1:-1]
    return scale * (27.0 * mid - box) + shift * mid


def pair_planes(quads, rows_ref):
    parts = []
    for k, t in enumerate(quads):
        halves = []
        for i in (0, 2):
            at = 40 * (2 * k + i // 2)
            rows_ref[at : at + 40] = t[i] + t[i + 1]
            halves.append(
                rows_ref[pl.ds(at + 4, 16, stride=2)] + rows_ref[pl.ds(at + 5, 16, stride=2)]
            )
        parts.append(jnp.concatenate(halves, axis=1))
    lane, out = iota((256, 128), 0), iota((256, 128), 1)
    pack = ones_where(lane // 2 == out, 0.125)
    return dot(jnp.concatenate(parts, axis=0), pack).reshape(len(quads), 16, 128)


def edge_kernel(own_ref, first_ref, last_ref):
    for k in range(3):
        for p in range(4):
            at = 10 * (4 * k + p)
            first_ref[at : at + 10] = own_ref[k, p, :10]
            last_ref[at : at + 10] = own_ref[k, p, 6:]


def block_kernel(own_ref, before_ref, after_ref, block_ref, face_ref, mate_ref):
    left = lax.axis_index("c") == 0
    none = jnp.zeros((2, 128), F32)
    for k in range(3):
        for p in range(4):
            at = 10 * (4 * k + p)
            block_ref[k, p, 12:28] = own_ref[k, p]
            block_ref[k, p, 2:12] = before_ref[at : at + 10]
            block_ref[k, p, 28:38] = after_ref[at : at + 10]
            block_ref[k, p, :2] = none
            block_ref[k, p, 38:] = none

    def send(at, k, low, high, rows):
        low, high = block_ref[k, low, rows], block_ref[k, high, rows]
        size = low.shape[0]
        face_ref[at : at + size] = jnp.where(left, low, high)
        mate_ref[at : at + size] = jnp.where(left, high, low)

    for k in range(3):
        for p in range(2):
            send(40 * (2 * k + p), k, p, p + 2, slice(0, 40))
        send(240 + 24 * k, k, 2, 1, slice(8, 32))
    send(312, 1, 3, 0, slice(8, 32))
    face_ref[336:] = jnp.zeros((8, 128), F32)


def fine_kernel(
    own_ref, mate_ref, face_ref, iter_ref, field_ref, piece_ref, one_ref, coef_rows, rows_ref
):
    left = lax.axis_index("c") == 0
    face, mate = face_ref[:336], mate_ref[...]
    low, high = jnp.where(left, face, mate), jnp.where(left, mate, face)
    pad = jnp.zeros((1, 8, 128), F32)
    blocks = []
    for k in range(3):
        sides = []
        for t in (low, high):
            far = [t[240 + 24 * k : 264 + 24 * k], t[312:]]
            if k != 1:
                far[1] = jnp.zeros_like(far[1])
            far = [jnp.concatenate([pad, u[None], pad], axis=1) for u in far]
            sides.append([t[80 * k : 80 * k + 80].reshape(2, 40, 128)] + far)
        blocks.append(jnp.concatenate(sides[0][::-1] + [own_ref[k]] + sides[1], axis=0))
    f, a, s = blocks
    coefs = pair_planes([t[4 * p : 4 * p + 4] for t in (a, s) for p in range(3)], coef_rows)
    w = relax_weight(a[1:11], s[1:11], 1.0)
    u = w * f[1:11]
    u = u[1:-1] + w[1:-1] * (f[2:10] - fine_apply(u, a[2:10], s[2:10]))
    iter_ref[...] = u[:, 8:32]
    for k, t in enumerate((f[2:10], a[2:10], s[2:10], w[1:9])):
        field_ref[k] = t[:, 8:32]
    resid = f[4:8] - fine_apply(u[1:7], a[4:8], s[4:8])
    f = pair_planes([resid], rows_ref)
    a, s = coefs[:3], coefs[3:]
    for k, t in enumerate((f[0], a[1], s[1])):
        one_ref[k] = t

    none = jnp.zeros_like(f)
    f = jnp.concatenate([none, f, none], axis=0)
    w = relax_weight(a, s, 0.25)
    v = w * f
    v = v + w * (f - middle_apply(v, a, s))
    resid = f - middle_apply(v, a, s)
    spread = ones_where(iota((128, 128), 1) % 32 == (iota((128, 128), 0) % 64) // 2, 0.125)
    own = ones_where(iota((16, 128), 0) // 2 == iota((16, 128), 1) // 32 + 2)
    mixed = dot(resid.reshape(48, 128), spread).reshape(3, 16, 128)
    rows = [mixed[k] * own for k in range(3)]
    mixed = dot(jnp.concatenate([a[1], s[1]], axis=0), spread).reshape(2, 16, 128)
    rows += [mixed[k] * own for k in range(2)] + [jnp.zeros((1, 128), F32)] * 3
    piece = jnp.concatenate([jnp.sum(t, axis=0, keepdims=True) for t in rows], axis=0)
    piece_ref[...] = jnp.broadcast_to(piece[None], piece_ref.shape)


def middle_apply(v, scale, shift):
    rows = v.shape[1]
    lane = iota((rows, 128), 1)
    row = iota((rows, 128), 0)
    swap = pltpu.roll(v, 64, 2)
    edge = jnp.zeros_like(swap[:1])
    prev = jnp.concatenate([edge, swap[:-1]], axis=0)
    later = jnp.concatenate([swap[1:], edge], axis=0)
    box = v + swap + jnp.where(lane < 64, prev, later)
    box = (
        box
        + jnp.where(row > 0, pltpu.roll(box, 1, 1), 0.0)
        + jnp.where(row < rows - 1, pltpu.roll(box, rows - 1, 1), 0.0)
    )
    box = lane_box(box, 64)
    return 0.25 * scale * (27.0 * v - box) + shift * v


def quarter_row(shape, dim):
    i = iota(shape, dim)
    return 4 * (i % 8) + i // 8


def quarter_mask():
    return ones_where(iota((4, 8, 128), 2) // 32 == iota((4, 8, 128), 0))


def gather_kernel(got_ref, piece_ref, rows_ref):
    core = lax.axis_index("c")
    half = got_ref.shape[0] // 2
    rows_ref[: 2 * half] = got_ref[...]

    def column(at, k):
        return rows_ref[pl.ds(at * half + k, half // 8, stride=8)]

    outward = 2 * core
    piece = jnp.concatenate(
        [
            column(core, outward),
            column(core, 1) + column(1 - core, outward),
            column(core, 3),
            column(core, 4),
        ],
        axis=0,
    )
    piece_ref[...] = jnp.broadcast_to(piece[None], piece_ref.shape)


def smooth_kernel(
    own_ref, mate_ref, outer_ref, inner_ref, field_ref, iter_ref, matrix_ref
):
    left = lax.axis_index("c") == 0
    for k in range(3):
        mate, outer, inner = mate_ref[k], outer_ref[:, k], inner_ref[k]
        field_ref[k, 0] = jnp.where(left, outer[0], inner)
        field_ref[k, 1] = jnp.where(left, outer[1], mate)
        field_ref[k, 2] = own_ref[k]
        field_ref[k, 3] = jnp.where(left, mate, outer[0])
        field_ref[k, 4] = jnp.where(left, inner, outer[1])
    f, a, s = (field_ref[k] for k in range(3))
    w = relax_weight(a, s, 0.25)
    field_ref[3] = w
    v = w * f
    iter_ref[...] = v + w * (f - middle_apply(v, a, s))
    matrix_ref[...] = box_matrix()


def box_matrix():
    lane, out = iota((256, 256), 0) % 128, iota((256, 256), 1)
    group, to = lane // 32, out % 128 // 32
    near = jnp.abs(lane % 32 - out % 32) <= 1
    same = (out < 128) & (jnp.abs(group - to) <= 1)
    wrap = (out >= 128) & (jnp.abs(group - to) == 3)
    return ones_where(near & (same | wrap)).astype(jnp.bfloat16)


def coarse_box(v, matrix):
    rows = (v[:-2] + v[1:-1] + v[2:]).reshape(-1, 128)
    high = rows.astype(jnp.bfloat16)
    low = (rows - high.astype(F32)).astype(jnp.bfloat16)
    both = lax.dot_general(
        jnp.concatenate([high, low], axis=1),
        matrix,
        (((1,), (0,)), ((), ())),
        preferred_element_type=F32,
    )
    box, wrap = (both[:, k : k + 128].reshape(-1, 8, 128) for k in (0, 128))
    lane, row = iota((8, 128), 1), iota((8, 128), 0)
    up = jnp.where((lane < 32) & (row > 0), pltpu.roll(wrap, 1, 1), 0.0)
    down = jnp.where((lane >= 96) & (row < 7), pltpu.roll(wrap, 7, 1), 0.0)
    return box + up + down


def total(plane):
    return jnp.sum(jnp.sum(plane, axis=0, keepdims=True), axis=1, keepdims=True)


def solve_coarse(q_ref, a_ref, d_ref, inverse_ref, w_ref, y_ref, at, matrix):
    planes = a_ref.shape[0]
    chunk = 16 if planes % 16 == 0 else 2
    starts = range(0, planes, chunk)
    none = jnp.zeros((2, 8, 128), F32)
    for ref in (q_ref, inverse_ref, w_ref):
        ref[:2] = none
        ref[planes + 2 :] = none
    for i in starts:
        own, padded = slice(i, i + chunk), slice(i + 2, i + chunk + 2)
        inverse_ref[padded] = 1.0 / (d_ref[own] - a_ref[own])

    span = 2 * chunk if planes % (2 * chunk) == 0 else chunk

    def product(ref):
        for i in range(0, planes, span):
            own, wide = slice(i, i + span), slice(i + 1, i + span + 3)
            z = ref[wide] * inverse_ref[wide]
            y_ref[own] = d_ref[own] * z[1:-1] - a_ref[own] * coarse_box(z, matrix)

    product(q_ref)
    solution = jnp.zeros((5, 8, 128), F32)
    for step in range(COARSE):
        upper = lower = jnp.zeros((8, 128), F32)
        for i in starts:
            own, padded = slice(i, i + chunk), slice(i + 2, i + chunk + 2)
            w, q = y_ref[own], q_ref[padded]
            if step > 0:
                old = w_ref[padded]
                w, q = old - alpha * w, q - alpha * old
                q_ref[padded] = q
            w_ref[padded] = w
            upper = upper + jnp.sum(w * q, axis=0)
            lower = lower + jnp.sum(w * w, axis=0)
        alpha = (total(upper) / total(lower))[None]
        if step < COARSE - 1:
            product(w_ref)
        solution = solution + alpha * q_ref[pl.ds(at, 5)]
    return solution * inverse_ref[pl.ds(at, 5)]


def last_kernel(
    got_ref, mate_ref, matrix_ref, field_ref, middle_ref, fine_ref, iter_ref, out_ref,
    q_ref, a_ref, d_ref, inverse_ref, w_ref, y_ref, mine_out, mate_out, middle_rows, fine_rows,
):
    nx = lax.axis_size("x")
    chip = lax.axis_index("y") * nx + lax.axis_index("x")
    core = lax.axis_index("c")
    rank = lax.axis_index("z")

    chips = got_ref.shape[0]
    order = [i % nx * (chips // nx) + i // nx for i in range(chips)]
    none = jnp.zeros((1, 8, 128), F32)
    for ref, outward_ref in ((got_ref, mine_out), (mate_ref, mate_out)):
        outward_ref[:1] = none
        outward_ref[chips + 1 :] = none
        for i in range(chips):
            outward_ref[i + 1] = ref[order[i], :8]
    for ref, outward_ref, side in ((got_ref, mate_out, core), (mate_ref, mine_out, 1 - core)):
        for i in range(chips):
            piece = ref.at[order[i]]
            q = piece[8:16][None] + outward_ref[pl.ds(i + 2 * side, 1)]
            a = 0.0625 * piece[16:24][None]
            q_ref[pl.ds(2 * i + 2 + side, 1)] = q
            a_ref[pl.ds(2 * i + side, 1)] = a
            d_ref[pl.ds(2 * i + side, 1)] = 27.0 * a + piece[24:32][None]
    near = solve_coarse(
        q_ref, a_ref, d_ref, inverse_ref, w_ref, y_ref, chip * 2 + core, matrix_ref[...]
    )

    mask = quarter_mask()
    stack = jnp.concatenate([(near[p][None] * mask).reshape(32, 128) for p in range(5)], axis=0)
    spread = ones_where(iota((128, 128), 0) % 32 == (iota((128, 128), 1) % 64) // 2)
    mixed = dot(stack, spread)
    size = (middle_rows.shape[0] - 16) // 5
    edge = jnp.zeros((4, 128), F32)
    window = []
    for p in range(5):
        at = size * p
        middle_rows[at : at + 4] = edge
        middle_rows[at + size - 4 : at + size] = edge
        for k in range(4):
            t = mixed[32 * p + 8 * k : 32 * p + 8 * k + 8]
            for i in (4, 5):
                middle_rows[pl.ds(at + 2 * k + i, 8, stride=8)] = t
        window.append(middle_rows[pl.ds(pl.multiple_of(at + rank * 8, 8), 16)][None])
    v = middle_ref[...] + jnp.concatenate(window, axis=0)
    f, a, s, w = (field_ref[k] for k in range(4))
    for _ in range(2):
        v = v + w * (f - middle_apply(v, a, s))

    lane, out = iota((128, 256), 0), iota((128, 256), 1)
    mixed = dot(v[1:4].reshape(48, 128), ones_where(lane == out // 2))
    halves = [mixed[:16, 128:], mixed[16:32, :128], mixed[16:32, 128:], mixed[32:, :128]]
    refined = []
    for p, t in enumerate(halves):
        for i in range(2):
            fine_rows[pl.ds(24 * p + i, 12, stride=2)] = t[2:14]
        refined += [fine_rows[24 * p : 24 * p + 24][None]] * 2
    refined = jnp.concatenate(refined, axis=0)

    f, a, s, w = (fine_ref[k] for k in range(4))
    u = iter_ref[...] + jnp.where(a > 0.25, refined, 0.0)
    for i in (1, 2):
        j = 8 - i
        u = u[1:-1] + w[i:j] * (f[i:j] - fine_apply(u, a[i:j], s[i:j]))
    out_ref[...] = u[:, 4:20]


def call(kernel, outs, *args, scratch=()):
    return pl.pallas_call(
        kernel,
        out_shape=[
            jax.ShapeDtypeStruct(*(out if isinstance(out[0], tuple) else (out, F32)))
            for out in outs
        ],
        in_specs=[pl.BlockSpec(memory_space=pltpu.VMEM)] * len(args),
        out_specs=[pl.BlockSpec(memory_space=pltpu.VMEM)] * len(outs),
        scratch_shapes=[pltpu.VMEM(shape, F32) for shape in scratch],
        compiler_params=pltpu.CompilerParams(vmem_limit_bytes=24 * 2**20),
    )(*args)


def shards(source, row_scale, shift_field):
    ny, nx, nz = lax.axis_size("y"), lax.axis_size("x"), lax.axis_size("z")
    chips = ny * nx
    first = lax.axis_index("c") == 0

    own = jnp.stack([source, row_scale, shift_field])
    head, tail = call(edge_kernel, [(120, 128), (120, 128)], own)
    up = [(i, i + 1) for i in range(nz - 1)]
    down = [(i + 1, i) for i in range(nz - 1)]
    before = lax.ppermute(tail, "z", up)
    after = lax.ppermute(head, "z", down)
    own, face, mate = call(
        block_kernel, [(3, 4, 40, 128), (344, 128), (336, 128)], own, before, after
    )
    facing = []
    for i in range(chips - 1):
        facing += [(2 * i + 1, 2 * i + 2), (2 * i + 2, 2 * i + 1)]
    swap = [(0, 1), (1, 0)]
    face = lax.ppermute(face, ("y", "x", "c"), facing)
    mate = lax.ppermute(mate, "c", swap)
    fine_iter, fine_fields, sent, one = call(
        fine_kernel,
        [(8, 24, 128), (4, 8, 24, 128), (2 * nz, 8, 128), (3, 16, 128)],
        own, mate, face,
        scratch=[(12 * 40 + 16, 128), (2 * 40 + 16, 128)],
    )

    got = lax.all_to_all(sent, ("c", "z"), 0, 0).reshape(16 * nz, 128)
    (sent,) = call(
        gather_kernel, [(chips, 32, 128)], got, scratch=[(16 * nz + 16, 128)]
    )
    one, sent = lax.optimization_barrier((one, sent))
    half = lax.all_to_all(sent, ("x", "y"), 0, 0)

    mate = lax.ppermute(one, "c", swap)
    pairs = jnp.stack([jnp.where(first, one, mate), jnp.where(first, mate, one)])
    ring = []
    for i in range(chips - 1):
        ring += [(2 * i, 2 * i + 2), (2 * i + 3, 2 * i + 1)]
    outer = lax.ppermute(pairs, ("y", "x", "c"), ring)
    inner = lax.ppermute(one, ("y", "x", "c"), [(j, i) for i, j in ring])
    fields, middle_iter, matrix = call(
        smooth_kernel,
        [(4, 5, 16, 128), (5, 16, 128), ((256, 256), jnp.bfloat16)],
        one, mate, outer, inner,
    )
    half, fields, middle_iter = lax.optimization_barrier((half, fields, middle_iter))
    half_mate = lax.ppermute(half, "c", swap)
    (result,) = call(
        last_kernel, [source.shape],
        half, half_mate, matrix, fields, middle_iter, fine_fields, fine_iter,
        scratch=[(2 * chips + 4, 8, 128)] + [(2 * chips, 8, 128)] * 2
        + [(2 * chips + 4, 8, 128)] * 2 + [(2 * chips, 8, 128)] + [(chips + 2, 8, 128)] * 2
        + [(5 * (8 * nz + 8) + 16, 128), (4 * 24 + 16, 128)],
    )
    return result


def solution(mesh):
    ny, nx = (8, 4) if mesh.devices.shape[0] == 64 else (mesh.devices.shape[0] // 2, 1)
    nz = mesh.devices.shape[1]
    split = Mesh(mesh.devices.reshape(ny, nx, 2, nz), ("y", "x", "c", "z"))
    spec = P(("y", "x", "c"), "z", None)
    return jax.shard_map(
        shards, mesh=split, in_specs=(spec, spec, spec), out_specs=spec, check_vma=False
    )
```

```python
import jax
import jax.numpy as jnp
from jax import lax
from jax.experimental import pallas as pl
from jax.experimental.pallas import tpu as pltpu
from jax.sharding import Mesh, PartitionSpec as P

COARSE = 4
DAMPING = 0.8
F32 = jnp.float32


def split(a):
    high = a.astype(jnp.bfloat16)
    rest = a - high.astype(F32)
    middle = rest.astype(jnp.bfloat16)
    low = (rest - middle.astype(F32)).astype(jnp.bfloat16)
    return [high, middle, low]


def dot(a, b):
    parts = lax.dot_general(
        jnp.concatenate(split(a), axis=0),
        b.astype(jnp.bfloat16),
        (((1,), (0,)), ((), ())),
        preferred_element_type=F32,
    )
    n = a.shape[0]
    return parts[:n] + parts[n : 2 * n] + parts[2 * n :]


def iota(shape, dim):
    return lax.broadcasted_iota(jnp.int32, shape, dim)


def ones_where(cond, value=1.0):
    return jnp.where(cond, jnp.float32(value), jnp.float32(0.0))


def lane_box(v, period):
    axis = v.ndim - 1
    lane = iota(v.shape[-2:], 1) % period
    below = jnp.where(lane > 0, pltpu.roll(v, 1, axis), 0.0)
    above = jnp.where(lane < period - 1, pltpu.roll(v, 127, axis), 0.0)
    return v + below + above


def relax_weight(scale, shift, level_scale):
    inside = scale > 0.25
    diag = jnp.where(inside, 26.0 * level_scale * scale + shift, 1.0)
    return jnp.where(inside, DAMPING / diag, 0.0)


def fine_apply(v, scale, shift):
    rows = v.shape[1]
    box = v[:-2] + v[1:-1] + v[2:]
    box = box + pltpu.roll(box, 1, 1) + pltpu.roll(box, rows - 1, 1)
    box = lane_box(box, 128)
    mid = v[1:-1]
    return scale * (27.0 * mid - box) + shift * mid


def pair_planes(quads, rows_ref):
    parts = []
    for k, t in enumerate(quads):
        halves = []
        for i in (0, 2):
            at = 40 * (2 * k + i // 2)
            rows_ref[at : at + 40] = t[i] + t[i + 1]
            halves.append(
                rows_ref[pl.ds(at + 4, 16, stride=2)] + rows_ref[pl.ds(at + 5, 16, stride=2)]
            )
        parts.append(jnp.concatenate(halves, axis=1))
    lane, out = iota((256, 128), 0), iota((256, 128), 1)
    pack = ones_where(lane // 2 == out, 0.125)
    return dot(jnp.concatenate(parts, axis=0), pack).reshape(len(quads), 16, 128)


def edge_kernel(own_ref, first_ref, last_ref):
    for k in range(3):
        for p in range(4):
            at = 10 * (4 * k + p)
            first_ref[at : at + 10] = own_ref[k, p, :10]
            last_ref[at : at + 10] = own_ref[k, p, 6:]


def block_kernel(own_ref, before_ref, after_ref, block_ref, face_ref, mate_ref):
    left = lax.axis_index("c") == 0
    none = jnp.zeros((2, 128), F32)
    for k in range(3):
        for p in range(4):
            at = 10 * (4 * k + p)
            block_ref[k, p, 12:28] = own_ref[k, p]
            block_ref[k, p, 2:12] = before_ref[at : at + 10]
            block_ref[k, p, 28:38] = after_ref[at : at + 10]
            block_ref[k, p, :2] = none
            block_ref[k, p, 38:] = none

    def send(at, k, low, high, rows):
        low, high = block_ref[k, low, rows], block_ref[k, high, rows]
        size = low.shape[0]
        face_ref[at : at + size] = jnp.where(left, low, high)
        mate_ref[at : at + size] = jnp.where(left, high, low)

    for k in range(3):
        for p in range(2):
            send(40 * (2 * k + p), k, p, p + 2, slice(0, 40))
        send(240 + 24 * k, k, 2, 1, slice(8, 32))
    send(312, 1, 3, 0, slice(8, 32))
    face_ref[336:] = jnp.zeros((8, 128), F32)


def fine_kernel(
    own_ref, mate_ref, face_ref, iter_ref, field_ref, piece_ref, one_ref, coef_rows, rows_ref
):
    left = lax.axis_index("c") == 0
    face, mate = face_ref[:336], mate_ref[...]
    low, high = jnp.where(left, face, mate), jnp.where(left, mate, face)
    pad = jnp.zeros((1, 8, 128), F32)
    blocks = []
    for k in range(3):
        sides = []
        for t in (low, high):
            far = [t[240 + 24 * k : 264 + 24 * k], t[312:]]
            if k != 1:
                far[1] = jnp.zeros_like(far[1])
            far = [jnp.concatenate([pad, u[None], pad], axis=1) for u in far]
            sides.append([t[80 * k : 80 * k + 80].reshape(2, 40, 128)] + far)
        blocks.append(jnp.concatenate(sides[0][::-1] + [own_ref[k]] + sides[1], axis=0))
    f, a, s = blocks
    coefs = pair_planes([t[4 * p : 4 * p + 4] for t in (a, s) for p in range(3)], coef_rows)
    w = relax_weight(a[1:11], s[1:11], 1.0)
    u = w * f[1:11]
    u = u[1:-1] + w[1:-1] * (f[2:10] - fine_apply(u, a[2:10], s[2:10]))
    iter_ref[...] = u[:, 8:32]
    for k, t in enumerate((f[2:10], a[2:10], s[2:10], w[1:9])):
        field_ref[k] = t[:, 8:32]
    resid = f[4:8] - fine_apply(u[1:7], a[4:8], s[4:8])
    f = pair_planes([resid], rows_ref)
    a, s = coefs[:3], coefs[3:]
    for k, t in enumerate((f[0], a[1], s[1])):
        one_ref[k] = t

    none = jnp.zeros_like(f)
    f = jnp.concatenate([none, f, none], axis=0)
    w = relax_weight(a, s, 0.25)
    v = w * f
    v = v + w * (f - middle_apply(v, a, s))
    resid = f - middle_apply(v, a, s)
    spread = ones_where(iota((128, 128), 1) % 32 == (iota((128, 128), 0) % 64) // 2, 0.125)
    own = ones_where(iota((16, 128), 0) // 2 == iota((16, 128), 1) // 32 + 2)
    mixed = dot(resid.reshape(48, 128), spread).reshape(3, 16, 128)
    rows = [mixed[k] * own for k in range(3)]
    mixed = dot(jnp.concatenate([a[1], s[1]], axis=0), spread).reshape(2, 16, 128)
    rows += [mixed[k] * own for k in range(2)] + [jnp.zeros((1, 128), F32)] * 3
    piece = jnp.concatenate([jnp.sum(t, axis=0, keepdims=True) for t in rows], axis=0)
    piece_ref[...] = jnp.broadcast_to(piece[None], piece_ref.shape)


def middle_apply(v, scale, shift):
    rows = v.shape[1]
    lane = iota((rows, 128), 1)
    row = iota((rows, 128), 0)
    swap = pltpu.roll(v, 64, 2)
    edge = jnp.zeros_like(swap[:1])
    prev = jnp.concatenate([edge, swap[:-1]], axis=0)
    later = jnp.concatenate([swap[1:], edge], axis=0)
    box = v + swap + jnp.where(lane < 64, prev, later)
    box = (
        box
        + jnp.where(row > 0, pltpu.roll(box, 1, 1), 0.0)
        + jnp.where(row < rows - 1, pltpu.roll(box, rows - 1, 1), 0.0)
    )
    box = lane_box(box, 64)
    return 0.25 * scale * (27.0 * v - box) + shift * v


def quarter_row(shape, dim):
    i = iota(shape, dim)
    return 4 * (i % 8) + i // 8


def quarter_mask():
    return ones_where(iota((4, 8, 128), 2) // 32 == iota((4, 8, 128), 0))


def gather_kernel(got_ref, piece_ref, rows_ref):
    core = lax.axis_index("c")
    half = got_ref.shape[0] // 2
    rows_ref[: 2 * half] = got_ref[...]

    def column(at, k):
        return rows_ref[pl.ds(at * half + k, half // 8, stride=8)]

    outward = 2 * core
    piece = jnp.concatenate(
        [
            column(core, outward),
            column(core, 1) + column(1 - core, outward),
            column(core, 3),
            column(core, 4),
        ],
        axis=0,
    )
    piece_ref[...] = jnp.broadcast_to(piece[None], piece_ref.shape)


def smooth_kernel(
    own_ref, mate_ref, outer_ref, inner_ref, field_ref, iter_ref, matrix_ref
):
    left = lax.axis_index("c") == 0
    for k in range(3):
        mate, outer, inner = mate_ref[k], outer_ref[:, k], inner_ref[k]
        field_ref[k, 0] = jnp.where(left, outer[0], inner)
        field_ref[k, 1] = jnp.where(left, outer[1], mate)
        field_ref[k, 2] = own_ref[k]
        field_ref[k, 3] = jnp.where(left, mate, outer[0])
        field_ref[k, 4] = jnp.where(left, inner, outer[1])
    f, a, s = (field_ref[k] for k in range(3))
    w = relax_weight(a, s, 0.25)
    field_ref[3] = w
    v = w * f
    iter_ref[...] = v + w * (f - middle_apply(v, a, s))
    matrix_ref[...] = box_matrix()


def box_matrix():
    lane, out = iota((384, 256), 0) % 128, iota((384, 256), 1)
    group, to = lane // 32, out % 128 // 32
    near = jnp.abs(lane % 32 - out % 32) <= 1
    same = (out < 128) & (jnp.abs(group - to) <= 1)
    wrap = (out >= 128) & (jnp.abs(group - to) == 3)
    return ones_where(near & (same | wrap)).astype(jnp.bfloat16)


def coarse_box(v, matrix):
    rows = (v[:-2] + v[1:-1] + v[2:]).reshape(-1, 128)
    both = lax.dot_general(
        jnp.concatenate(split(rows), axis=1),
        matrix,
        (((1,), (0,)), ((), ())),
        preferred_element_type=F32,
    )
    box, wrap = (both[:, k : k + 128].reshape(-1, 8, 128) for k in (0, 128))
    lane, row = iota((8, 128), 1), iota((8, 128), 0)
    up = jnp.where((lane < 32) & (row > 0), pltpu.roll(wrap, 1, 1), 0.0)
    down = jnp.where((lane >= 96) & (row < 7), pltpu.roll(wrap, 7, 1), 0.0)
    return box + up + down


def total(plane):
    return jnp.sum(jnp.sum(plane, axis=0, keepdims=True), axis=1, keepdims=True)


def solve_coarse(q_ref, a_ref, d_ref, inverse_ref, w_ref, y_ref, at, matrix):
    planes = a_ref.shape[0]
    chunk = 16 if planes % 16 == 0 else 2
    starts = range(0, planes, chunk)
    none = jnp.zeros((2, 8, 128), F32)
    for ref in (q_ref, inverse_ref, w_ref):
        ref[:2] = none
        ref[planes + 2 :] = none
    for i in starts:
        own, padded = slice(i, i + chunk), slice(i + 2, i + chunk + 2)
        inverse_ref[padded] = 1.0 / (d_ref[own] - a_ref[own])

    def product(ref):
        for i in starts:
            own, wide = slice(i, i + chunk), slice(i + 1, i + chunk + 3)
            z = ref[wide] * inverse_ref[wide]
            y_ref[own] = d_ref[own] * z[1:-1] - a_ref[own] * coarse_box(z, matrix)

    product(q_ref)
    solution = jnp.zeros((5, 8, 128), F32)
    for step in range(COARSE):
        upper = lower = jnp.zeros((8, 128), F32)
        for i in starts:
            own, padded = slice(i, i + chunk), slice(i + 2, i + chunk + 2)
            w, q = y_ref[own], q_ref[padded]
            if step > 0:
                old = w_ref[padded]
                w, q = old - alpha * w, q - alpha * old
                q_ref[padded] = q
            w_ref[padded] = w
            upper = upper + jnp.sum(w * q, axis=0)
            lower = lower + jnp.sum(w * w, axis=0)
        alpha = (total(upper) / total(lower))[None]
        if step < COARSE - 1:
            product(w_ref)
        solution = solution + alpha * q_ref[pl.ds(at, 5)]
    return solution * inverse_ref[pl.ds(at, 5)]


def last_kernel(
    got_ref, mate_ref, matrix_ref, field_ref, middle_ref, fine_ref, iter_ref, out_ref,
    q_ref, a_ref, d_ref, inverse_ref, w_ref, y_ref, middle_rows, fine_rows,
):
    nx = lax.axis_size("x")
    chip = lax.axis_index("y") * nx + lax.axis_index("x")
    core = lax.axis_index("c")
    rank = lax.axis_index("z")
    planes = 2 * got_ref.shape[0]

    got, mate = got_ref[...], mate_ref[...]
    halves = jnp.where(core == 0, got, mate), jnp.where(core == 0, mate, got)

    def part(half, k):
        return halves[half][:, 8 * k : 8 * k + 8]

    def pairs(first, second):
        return jnp.concatenate([first[:, None], second[:, None]], axis=1).reshape(planes, 8, 128)

    edge = jnp.zeros_like(part(0, 0)[:1])
    q_ref[2 : planes + 2] = pairs(
        part(0, 1) + jnp.concatenate([edge, part(1, 0)[:-1]], axis=0),
        part(1, 1) + jnp.concatenate([part(0, 0)[1:], edge], axis=0),
    )
    a = 0.0625 * pairs(part(0, 2), part(1, 2))
    a_ref[...] = a
    d_ref[...] = 27.0 * a + pairs(part(0, 3), part(1, 3))
    near = solve_coarse(
        q_ref, a_ref, d_ref, inverse_ref, w_ref, y_ref, chip * 2 + core, matrix_ref[...]
    )

    mask = quarter_mask()
    stack = jnp.concatenate([(near[p][None] * mask).reshape(32, 128) for p in range(5)], axis=0)
    spread = ones_where(iota((128, 128), 0) % 32 == (iota((128, 128), 1) % 64) // 2)
    mixed = dot(stack, spread)
    size = (middle_rows.shape[0] - 16) // 5
    edge = jnp.zeros((4, 128), F32)
    window = []
    for p in range(5):
        at = size * p
        middle_rows[at : at + 4] = edge
        middle_rows[at + size - 4 : at + size] = edge
        for k in range(4):
            t = mixed[32 * p + 8 * k : 32 * p + 8 * k + 8]
            for i in (4, 5):
                middle_rows[pl.ds(at + 2 * k + i, 8, stride=8)] = t
        window.append(middle_rows[pl.ds(pl.multiple_of(at + rank * 8, 8), 16)][None])
    v = middle_ref[...] + jnp.concatenate(window, axis=0)
    f, a, s, w = (field_ref[k] for k in range(4))
    for _ in range(2):
        v = v + w * (f - middle_apply(v, a, s))

    lane, out = iota((128, 256), 0), iota((128, 256), 1)
    mixed = dot(v[1:4].reshape(48, 128), ones_where(lane == out // 2))
    halves = [mixed[:16, 128:], mixed[16:32, :128], mixed[16:32, 128:], mixed[32:, :128]]
    refined = []
    for p, t in enumerate(halves):
        for i in range(2):
            fine_rows[pl.ds(24 * p + i, 12, stride=2)] = t[2:14]
        refined += [fine_rows[24 * p : 24 * p + 24][None]] * 2
    refined = jnp.concatenate(refined, axis=0)

    f, a, s, w = (fine_ref[k] for k in range(4))
    u = iter_ref[...] + jnp.where(a > 0.25, refined, 0.0)
    for i in (1, 2):
        j = 8 - i
        u = u[1:-1] + w[i:j] * (f[i:j] - fine_apply(u, a[i:j], s[i:j]))
    out_ref[...] = u[:, 4:20]


def call(kernel, outs, *args, scratch=()):
    return pl.pallas_call(
        kernel,
        out_shape=[
            jax.ShapeDtypeStruct(*(out if isinstance(out[0], tuple) else (out, F32)))
            for out in outs
        ],
        in_specs=[pl.BlockSpec(memory_space=pltpu.VMEM)] * len(args),
        out_specs=[pl.BlockSpec(memory_space=pltpu.VMEM)] * len(outs),
        scratch_shapes=[pltpu.VMEM(shape, F32) for shape in scratch],
        compiler_params=pltpu.CompilerParams(vmem_limit_bytes=24 * 2**20),
    )(*args)


def shards(source, row_scale, shift_field):
    ny, nx, nz = lax.axis_size("y"), lax.axis_size("x"), lax.axis_size("z")
    chips = ny * nx
    first = lax.axis_index("c") == 0

    own = jnp.stack([source, row_scale, shift_field])
    head, tail = call(edge_kernel, [(120, 128), (120, 128)], own)
    up = [(i, i + 1) for i in range(nz - 1)]
    down = [(i + 1, i) for i in range(nz - 1)]
    before = lax.ppermute(tail, "z", up)
    after = lax.ppermute(head, "z", down)
    own, face, mate = call(
        block_kernel, [(3, 4, 40, 128), (344, 128), (336, 128)], own, before, after
    )
    facing = []
    for i in range(chips - 1):
        facing += [(2 * i + 1, 2 * i + 2), (2 * i + 2, 2 * i + 1)]
    swap = [(0, 1), (1, 0)]
    face = lax.ppermute(face, ("y", "x", "c"), facing)
    mate = lax.ppermute(mate, "c", swap)
    fine_iter, fine_fields, sent, one = call(
        fine_kernel,
        [(8, 24, 128), (4, 8, 24, 128), (2 * nz, 8, 128), (3, 16, 128)],
        own, mate, face,
        scratch=[(12 * 40 + 16, 128), (2 * 40 + 16, 128)],
    )

    got = lax.all_to_all(sent, ("c", "z"), 0, 0).reshape(16 * nz, 128)
    (sent,) = call(
        gather_kernel, [(chips, 32, 128)], got, scratch=[(16 * nz + 16, 128)]
    )
    one, sent = lax.optimization_barrier((one, sent))
    half = lax.all_to_all(sent, ("y", "x"), 0, 0)

    mate = lax.ppermute(one, "c", swap)
    pairs = jnp.stack([jnp.where(first, one, mate), jnp.where(first, mate, one)])
    ring = []
    for i in range(chips - 1):
        ring += [(2 * i, 2 * i + 2), (2 * i + 3, 2 * i + 1)]
    outer = lax.ppermute(pairs, ("y", "x", "c"), ring)
    inner = lax.ppermute(one, ("y", "x", "c"), [(j, i) for i, j in ring])
    fields, middle_iter, matrix = call(
        smooth_kernel,
        [(4, 5, 16, 128), (5, 16, 128), ((384, 256), jnp.bfloat16)],
        one, mate, outer, inner,
    )
    half, fields, middle_iter = lax.optimization_barrier((half, fields, middle_iter))
    half_mate = lax.ppermute(half, "c", swap)
    (result,) = call(
        last_kernel, [source.shape],
        half, half_mate, matrix, fields, middle_iter, fine_fields, fine_iter,
        scratch=[(2 * chips + 4, 8, 128)] + [(2 * chips, 8, 128)] * 2
        + [(2 * chips + 4, 8, 128)] * 2 + [(2 * chips, 8, 128)]
        + [(5 * (8 * nz + 8) + 16, 128), (4 * 24 + 16, 128)],
    )
    return result


def solution(mesh):
    ny, nx = (8, 4) if mesh.devices.shape[0] == 64 else (mesh.devices.shape[0] // 2, 1)
    nz = mesh.devices.shape[1]
    split = Mesh(mesh.devices.reshape(ny, nx, 2, nz), ("y", "x", "c", "z"))
    spec = P(("y", "x", "c"), "z", None)
    return jax.shard_map(
        shards, mesh=split, in_specs=(spec, spec, spec), out_specs=spec, check_vma=False
    )
```

```python
import jax
import jax.numpy as jnp
from jax import lax
from jax.experimental import pallas as pl
from jax.experimental.pallas import tpu as pltpu
from jax.sharding import Mesh, PartitionSpec as P

COARSE = 4
DAMPING = 0.8
F32 = jnp.float32


def split(a):
    high = a.astype(jnp.bfloat16)
    rest = a - high.astype(F32)
    middle = rest.astype(jnp.bfloat16)
    low = (rest - middle.astype(F32)).astype(jnp.bfloat16)
    return [high, middle, low]


def dot(a, b):
    parts = lax.dot_general(
        jnp.concatenate(split(a), axis=0),
        b.astype(jnp.bfloat16),
        (((1,), (0,)), ((), ())),
        preferred_element_type=F32,
    )
    n = a.shape[0]
    return parts[:n] + parts[n : 2 * n] + parts[2 * n :]


def iota(shape, dim):
    return lax.broadcasted_iota(jnp.int32, shape, dim)


def ones_where(cond, value=1.0):
    return jnp.where(cond, jnp.float32(value), jnp.float32(0.0))


def lane_box(v, period):
    axis = v.ndim - 1
    lane = iota(v.shape[-2:], 1) % period
    below = jnp.where(lane > 0, pltpu.roll(v, 1, axis), 0.0)
    above = jnp.where(lane < period - 1, pltpu.roll(v, 127, axis), 0.0)
    return v + below + above


def relax_weight(scale, shift, level_scale):
    inside = scale > 0.25
    diag = jnp.where(inside, 26.0 * level_scale * scale + shift, 1.0)
    return jnp.where(inside, DAMPING / diag, 0.0)


def fine_apply(v, scale, shift):
    rows = v.shape[1]
    box = v[:-2] + v[1:-1] + v[2:]
    box = box + pltpu.roll(box, 1, 1) + pltpu.roll(box, rows - 1, 1)
    box = lane_box(box, 128)
    mid = v[1:-1]
    return scale * (27.0 * mid - box) + shift * mid


def pair_planes(quads, rows_ref):
    parts = []
    for k, t in enumerate(quads):
        halves = []
        for i in (0, 2):
            at = 40 * (2 * k + i // 2)
            rows_ref[at : at + 40] = t[i] + t[i + 1]
            halves.append(
                rows_ref[pl.ds(at + 4, 16, stride=2)] + rows_ref[pl.ds(at + 5, 16, stride=2)]
            )
        parts.append(jnp.concatenate(halves, axis=1))
    lane, out = iota((256, 128), 0), iota((256, 128), 1)
    pack = ones_where(lane // 2 == out, 0.125)
    return dot(jnp.concatenate(parts, axis=0), pack).reshape(len(quads), 16, 128)


def edge_kernel(own_ref, first_ref, last_ref):
    for k in range(3):
        for p in range(4):
            at = 10 * (4 * k + p)
            first_ref[at : at + 10] = own_ref[k, p, :10]
            last_ref[at : at + 10] = own_ref[k, p, 6:]


def block_kernel(own_ref, before_ref, after_ref, block_ref, face_ref, mate_ref):
    left = lax.axis_index("c") == 0
    none = jnp.zeros((2, 128), F32)
    for k in range(3):
        for p in range(4):
            at = 10 * (4 * k + p)
            block_ref[k, p, 12:28] = own_ref[k, p]
            block_ref[k, p, 2:12] = before_ref[at : at + 10]
            block_ref[k, p, 28:38] = after_ref[at : at + 10]
            block_ref[k, p, :2] = none
            block_ref[k, p, 38:] = none

    def send(at, k, low, high, rows):
        low, high = block_ref[k, low, rows], block_ref[k, high, rows]
        size = low.shape[0]
        face_ref[at : at + size] = jnp.where(left, low, high)
        mate_ref[at : at + size] = jnp.where(left, high, low)

    for k in range(3):
        for p in range(2):
            send(40 * (2 * k + p), k, p, p + 2, slice(0, 40))
        send(240 + 24 * k, k, 2, 1, slice(8, 32))
    send(312, 1, 3, 0, slice(8, 32))
    face_ref[336:] = jnp.zeros((8, 128), F32)


def fine_kernel(
    own_ref, mate_ref, face_ref, iter_ref, field_ref, piece_ref, one_ref, coef_rows, rows_ref
):
    left = lax.axis_index("c") == 0
    face, mate = face_ref[:336], mate_ref[...]
    low, high = jnp.where(left, face, mate), jnp.where(left, mate, face)
    pad = jnp.zeros((1, 8, 128), F32)
    blocks = []
    for k in range(3):
        sides = []
        for t in (low, high):
            far = [t[240 + 24 * k : 264 + 24 * k], t[312:]]
            if k != 1:
                far[1] = jnp.zeros_like(far[1])
            far = [jnp.concatenate([pad, u[None], pad], axis=1) for u in far]
            sides.append([t[80 * k : 80 * k + 80].reshape(2, 40, 128)] + far)
        blocks.append(jnp.concatenate(sides[0][::-1] + [own_ref[k]] + sides[1], axis=0))
    f, a, s = blocks
    coefs = pair_planes([t[4 * p : 4 * p + 4] for t in (a, s) for p in range(3)], coef_rows)
    w = relax_weight(a[1:11], s[1:11], 1.0)
    u = w * f[1:11]
    u = u[1:-1] + w[1:-1] * (f[2:10] - fine_apply(u, a[2:10], s[2:10]))
    iter_ref[...] = u[:, 8:32]
    for k, t in enumerate((f[2:10], a[2:10], s[2:10], w[1:9])):
        field_ref[k] = t[:, 8:32]
    resid = f[4:8] - fine_apply(u[1:7], a[4:8], s[4:8])
    f = pair_planes([resid], rows_ref)
    a, s = coefs[:3], coefs[3:]
    for k, t in enumerate((f[0], a[1], s[1])):
        one_ref[k] = t

    none = jnp.zeros_like(f)
    f = jnp.concatenate([none, f, none], axis=0)
    w = relax_weight(a, s, 0.25)
    v = w * f
    v = v + w * (f - middle_apply(v, a, s))
    resid = f - middle_apply(v, a, s)
    spread = ones_where(iota((128, 128), 1) % 32 == (iota((128, 128), 0) % 64) // 2, 0.125)
    own = ones_where(iota((16, 128), 0) // 2 == iota((16, 128), 1) // 32 + 2)
    mixed = dot(resid.reshape(48, 128), spread).reshape(3, 16, 128)
    rows = [mixed[k] * own for k in range(3)]
    mixed = dot(jnp.concatenate([a[1], s[1]], axis=0), spread).reshape(2, 16, 128)
    rows += [mixed[k] * own for k in range(2)] + [jnp.zeros((1, 128), F32)] * 3
    piece = jnp.concatenate([jnp.sum(t, axis=0, keepdims=True) for t in rows], axis=0)
    piece_ref[...] = jnp.broadcast_to(piece[None], piece_ref.shape)


def middle_apply(v, scale, shift):
    rows = v.shape[1]
    lane = iota((rows, 128), 1)
    row = iota((rows, 128), 0)
    swap = pltpu.roll(v, 64, 2)
    edge = jnp.zeros_like(swap[:1])
    prev = jnp.concatenate([edge, swap[:-1]], axis=0)
    later = jnp.concatenate([swap[1:], edge], axis=0)
    box = v + swap + jnp.where(lane < 64, prev, later)
    box = (
        box
        + jnp.where(row > 0, pltpu.roll(box, 1, 1), 0.0)
        + jnp.where(row < rows - 1, pltpu.roll(box, rows - 1, 1), 0.0)
    )
    box = lane_box(box, 64)
    return 0.25 * scale * (27.0 * v - box) + shift * v


def quarter_row(shape, dim):
    i = iota(shape, dim)
    return 4 * (i % 8) + i // 8


def quarter_mask():
    return ones_where(iota((4, 8, 128), 2) // 32 == iota((4, 8, 128), 0))


def gather_kernel(got_ref, piece_ref, rows_ref):
    core = lax.axis_index("c")
    half = got_ref.shape[0] // 2
    rows_ref[: 2 * half] = got_ref[...]

    def column(at, k):
        return rows_ref[pl.ds(at * half + k, half // 8, stride=8)]

    outward = 2 * core
    piece = jnp.concatenate(
        [
            column(core, outward),
            column(core, 1) + column(1 - core, outward),
            column(core, 3),
            column(core, 4),
        ],
        axis=0,
    )
    piece_ref[...] = jnp.broadcast_to(piece[None], piece_ref.shape)


def smooth_kernel(
    own_ref, mate_ref, outer_ref, inner_ref, field_ref, iter_ref, matrix_ref
):
    left = lax.axis_index("c") == 0
    for k in range(3):
        mate, outer, inner = mate_ref[k], outer_ref[:, k], inner_ref[k]
        field_ref[k, 0] = jnp.where(left, outer[0], inner)
        field_ref[k, 1] = jnp.where(left, outer[1], mate)
        field_ref[k, 2] = own_ref[k]
        field_ref[k, 3] = jnp.where(left, mate, outer[0])
        field_ref[k, 4] = jnp.where(left, inner, outer[1])
    f, a, s = (field_ref[k] for k in range(3))
    w = relax_weight(a, s, 0.25)
    field_ref[3] = w
    v = w * f
    iter_ref[...] = v + w * (f - middle_apply(v, a, s))
    matrix_ref[...] = box_matrix()


def box_matrix():
    lane, out = iota((384, 256), 0) % 128, iota((384, 256), 1)
    group, to = lane // 32, out % 128 // 32
    near = jnp.abs(lane % 32 - out % 32) <= 1
    same = (out < 128) & (jnp.abs(group - to) <= 1)
    wrap = (out >= 128) & (jnp.abs(group - to) == 3)
    return ones_where(near & (same | wrap)).astype(jnp.bfloat16)


def coarse_box(v, matrix):
    rows = (v[:-2] + v[1:-1] + v[2:]).reshape(-1, 128)
    both = lax.dot_general(
        jnp.concatenate(split(rows), axis=1),
        matrix,
        (((1,), (0,)), ((), ())),
        preferred_element_type=F32,
    )
    box, wrap = (both[:, k : k + 128].reshape(-1, 8, 128) for k in (0, 128))
    lane, row = iota((8, 128), 1), iota((8, 128), 0)
    up = jnp.where((lane < 32) & (row > 0), pltpu.roll(wrap, 1, 1), 0.0)
    down = jnp.where((lane >= 96) & (row < 7), pltpu.roll(wrap, 7, 1), 0.0)
    return box + up + down


def total(plane):
    return jnp.sum(jnp.sum(plane, axis=0, keepdims=True), axis=1, keepdims=True)


def solve_coarse(q_ref, a_ref, d_ref, inverse_ref, w_ref, y_ref, at, matrix):
    planes = a_ref.shape[0]
    chunk = 16 if planes % 16 == 0 else 2
    starts = range(0, planes, chunk)
    none = jnp.zeros((2, 8, 128), F32)
    for ref in (q_ref, inverse_ref, w_ref):
        ref[:2] = none
        ref[planes + 2 :] = none
    for i in starts:
        own, padded = slice(i, i + chunk), slice(i + 2, i + chunk + 2)
        inverse_ref[padded] = 1.0 / (d_ref[own] - a_ref[own])

    def product(ref):
        for i in starts:
            own, wide = slice(i, i + chunk), slice(i + 1, i + chunk + 3)
            z = ref[wide] * inverse_ref[wide]
            y_ref[own] = d_ref[own] * z[1:-1] - a_ref[own] * coarse_box(z, matrix)

    def update(alpha):
        upper = lower = jnp.zeros((8, 128), F32)
        for i in starts:
            own, padded = slice(i, i + chunk), slice(i + 2, i + chunk + 2)
            w, q = y_ref[own], q_ref[padded]
            if alpha is not None:
                old = w_ref[padded]
                w, q = old - alpha * w, q - alpha * old
                q_ref[padded] = q
            w_ref[padded] = w
            upper = upper + jnp.sum(w * q, axis=0)
            lower = lower + jnp.sum(w * w, axis=0)
        return upper, lower

    def gain(upper, lower):
        alpha = (total(upper) / total(lower))[None]
        return alpha, alpha * q_ref[pl.ds(at, 5)]

    def step(_, carry):
        solution, upper, lower = carry
        alpha, part = gain(upper, lower)
        product(w_ref)
        return (solution + part, *update(alpha))

    product(q_ref)
    carry = (jnp.zeros((5, 8, 128), F32), *update(None))
    solution, upper, lower = lax.fori_loop(0, COARSE - 1, step, carry)
    solution = solution + gain(upper, lower)[1]
    return solution * inverse_ref[pl.ds(at, 5)]


def last_kernel(
    got_ref, mate_ref, matrix_ref, field_ref, middle_ref, fine_ref, iter_ref, out_ref,
    q_ref, a_ref, d_ref, inverse_ref, w_ref, y_ref, middle_rows, fine_rows,
):
    nx = lax.axis_size("x")
    chip = lax.axis_index("y") * nx + lax.axis_index("x")
    core = lax.axis_index("c")
    rank = lax.axis_index("z")
    planes = 2 * got_ref.shape[0]

    got, mate = got_ref[...], mate_ref[...]
    halves = jnp.where(core == 0, got, mate), jnp.where(core == 0, mate, got)

    def part(half, k):
        return halves[half][:, 8 * k : 8 * k + 8]

    def pairs(first, second):
        return jnp.concatenate([first[:, None], second[:, None]], axis=1).reshape(planes, 8, 128)

    edge = jnp.zeros_like(part(0, 0)[:1])
    q_ref[2 : planes + 2] = pairs(
        part(0, 1) + jnp.concatenate([edge, part(1, 0)[:-1]], axis=0),
        part(1, 1) + jnp.concatenate([part(0, 0)[1:], edge], axis=0),
    )
    a = 0.0625 * pairs(part(0, 2), part(1, 2))
    a_ref[...] = a
    d_ref[...] = 27.0 * a + pairs(part(0, 3), part(1, 3))
    near = solve_coarse(
        q_ref, a_ref, d_ref, inverse_ref, w_ref, y_ref, chip * 2 + core, matrix_ref[...]
    )

    mask = quarter_mask()
    stack = jnp.concatenate([(near[p][None] * mask).reshape(32, 128) for p in range(5)], axis=0)
    spread = ones_where(iota((128, 128), 0) % 32 == (iota((128, 128), 1) % 64) // 2)
    mixed = dot(stack, spread)
    size = (middle_rows.shape[0] - 16) // 5
    edge = jnp.zeros((4, 128), F32)
    window = []
    for p in range(5):
        at = size * p
        middle_rows[at : at + 4] = edge
        middle_rows[at + size - 4 : at + size] = edge
        for k in range(4):
            t = mixed[32 * p + 8 * k : 32 * p + 8 * k + 8]
            for i in (4, 5):
                middle_rows[pl.ds(at + 2 * k + i, 8, stride=8)] = t
        window.append(middle_rows[pl.ds(pl.multiple_of(at + rank * 8, 8), 16)][None])
    v = middle_ref[...] + jnp.concatenate(window, axis=0)
    f, a, s, w = (field_ref[k] for k in range(4))
    for _ in range(2):
        v = v + w * (f - middle_apply(v, a, s))

    lane, out = iota((128, 256), 0), iota((128, 256), 1)
    mixed = dot(v[1:4].reshape(48, 128), ones_where(lane == out // 2))
    halves = [mixed[:16, 128:], mixed[16:32, :128], mixed[16:32, 128:], mixed[32:, :128]]
    refined = []
    for p, t in enumerate(halves):
        for i in range(2):
            fine_rows[pl.ds(24 * p + i, 12, stride=2)] = t[2:14]
        refined += [fine_rows[24 * p : 24 * p + 24][None]] * 2
    refined = jnp.concatenate(refined, axis=0)

    f, a, s, w = (fine_ref[k] for k in range(4))
    u = iter_ref[...] + jnp.where(a > 0.25, refined, 0.0)
    for i in (1, 2):
        j = 8 - i
        u = u[1:-1] + w[i:j] * (f[i:j] - fine_apply(u, a[i:j], s[i:j]))
    out_ref[...] = u[:, 4:20]


def call(kernel, outs, *args, scratch=()):
    return pl.pallas_call(
        kernel,
        out_shape=[
            jax.ShapeDtypeStruct(*(out if isinstance(out[0], tuple) else (out, F32)))
            for out in outs
        ],
        in_specs=[pl.BlockSpec(memory_space=pltpu.VMEM)] * len(args),
        out_specs=[pl.BlockSpec(memory_space=pltpu.VMEM)] * len(outs),
        scratch_shapes=[pltpu.VMEM(shape, F32) for shape in scratch],
        compiler_params=pltpu.CompilerParams(vmem_limit_bytes=24 * 2**20),
    )(*args)


def shards(source, row_scale, shift_field):
    ny, nx, nz = lax.axis_size("y"), lax.axis_size("x"), lax.axis_size("z")
    chips = ny * nx
    first = lax.axis_index("c") == 0

    own = jnp.stack([source, row_scale, shift_field])
    head, tail = call(edge_kernel, [(120, 128), (120, 128)], own)
    up = [(i, i + 1) for i in range(nz - 1)]
    down = [(i + 1, i) for i in range(nz - 1)]
    before = lax.ppermute(tail, "z", up)
    after = lax.ppermute(head, "z", down)
    own, face, mate = call(
        block_kernel, [(3, 4, 40, 128), (344, 128), (336, 128)], own, before, after
    )
    facing = []
    for i in range(chips - 1):
        facing += [(2 * i + 1, 2 * i + 2), (2 * i + 2, 2 * i + 1)]
    swap = [(0, 1), (1, 0)]
    face = lax.ppermute(face, ("y", "x", "c"), facing)
    mate = lax.ppermute(mate, "c", swap)
    fine_iter, fine_fields, sent, one = call(
        fine_kernel,
        [(8, 24, 128), (4, 8, 24, 128), (2 * nz, 8, 128), (3, 16, 128)],
        own, mate, face,
        scratch=[(12 * 40 + 16, 128), (2 * 40 + 16, 128)],
    )

    got = lax.all_to_all(sent, ("c", "z"), 0, 0).reshape(16 * nz, 128)
    (sent,) = call(
        gather_kernel, [(chips, 32, 128)], got, scratch=[(16 * nz + 16, 128)]
    )
    one, sent = lax.optimization_barrier((one, sent))
    half = lax.all_to_all(sent, ("y", "x"), 0, 0)

    mate = lax.ppermute(one, "c", swap)
    pairs = jnp.stack([jnp.where(first, one, mate), jnp.where(first, mate, one)])
    ring = []
    for i in range(chips - 1):
        ring += [(2 * i, 2 * i + 2), (2 * i + 3, 2 * i + 1)]
    outer = lax.ppermute(pairs, ("y", "x", "c"), ring)
    inner = lax.ppermute(one, ("y", "x", "c"), [(j, i) for i, j in ring])
    fields, middle_iter, matrix = call(
        smooth_kernel,
        [(4, 5, 16, 128), (5, 16, 128), ((384, 256), jnp.bfloat16)],
        one, mate, outer, inner,
    )
    half, fields, middle_iter = lax.optimization_barrier((half, fields, middle_iter))
    half_mate = lax.ppermute(half, "c", swap)
    (result,) = call(
        last_kernel, [source.shape],
        half, half_mate, matrix, fields, middle_iter, fine_fields, fine_iter,
        scratch=[(2 * chips + 4, 8, 128)] + [(2 * chips, 8, 128)] * 2
        + [(2 * chips + 4, 8, 128)] * 2 + [(2 * chips, 8, 128)]
        + [(5 * (8 * nz + 8) + 16, 128), (4 * 24 + 16, 128)],
    )
    return result


def solution(mesh):
    ny, nx = (8, 4) if mesh.devices.shape[0] == 64 else (mesh.devices.shape[0] // 2, 1)
    nz = mesh.devices.shape[1]
    split = Mesh(mesh.devices.reshape(ny, nx, 2, nz), ("y", "x", "c", "z"))
    spec = P(("y", "x", "c"), "z", None)
    return jax.shard_map(
        shards, mesh=split, in_specs=(spec, spec, spec), out_specs=spec, check_vma=False
    )
```

```python
import jax
import jax.numpy as jnp
from jax import lax
from jax.experimental import pallas as pl
from jax.experimental.pallas import tpu as pltpu
from jax.sharding import Mesh, PartitionSpec as P

COARSE = 4
DAMPING = 0.8
F32 = jnp.float32


def split(a):
    high = a.astype(jnp.bfloat16)
    rest = a - high.astype(F32)
    middle = rest.astype(jnp.bfloat16)
    low = (rest - middle.astype(F32)).astype(jnp.bfloat16)
    return [high, middle, low]


def dot(a, b):
    parts = lax.dot_general(
        jnp.concatenate(split(a), axis=0),
        b.astype(jnp.bfloat16),
        (((1,), (0,)), ((), ())),
        preferred_element_type=F32,
    )
    n = a.shape[0]
    return parts[:n] + parts[n : 2 * n] + parts[2 * n :]


def iota(shape, dim):
    return lax.broadcasted_iota(jnp.int32, shape, dim)


def ones_where(cond, value=1.0):
    return jnp.where(cond, jnp.float32(value), jnp.float32(0.0))


def lane_box(v, period):
    axis = v.ndim - 1
    lane = iota(v.shape[-2:], 1) % period
    below = jnp.where(lane > 0, pltpu.roll(v, 1, axis), 0.0)
    above = jnp.where(lane < period - 1, pltpu.roll(v, 127, axis), 0.0)
    return v + below + above


def relax_weight(scale, shift, level_scale):
    inside = scale > 0.25
    diag = jnp.where(inside, 26.0 * level_scale * scale + shift, 1.0)
    return jnp.where(inside, DAMPING / diag, 0.0)


def fine_apply(v, scale, shift):
    rows = v.shape[1]
    box = v[:-2] + v[1:-1] + v[2:]
    box = box + pltpu.roll(box, 1, 1) + pltpu.roll(box, rows - 1, 1)
    box = lane_box(box, 128)
    mid = v[1:-1]
    return scale * (27.0 * mid - box) + shift * mid


def pair_planes(quads, rows_ref):
    parts = []
    for k, t in enumerate(quads):
        halves = []
        for i in (0, 2):
            at = 40 * (2 * k + i // 2)
            rows_ref[at : at + 40] = t[i] + t[i + 1]
            halves.append(
                rows_ref[pl.ds(at + 4, 16, stride=2)] + rows_ref[pl.ds(at + 5, 16, stride=2)]
            )
        parts.append(jnp.concatenate(halves, axis=1))
    lane, out = iota((256, 128), 0), iota((256, 128), 1)
    pack = ones_where(lane // 2 == out, 0.125)
    return dot(jnp.concatenate(parts, axis=0), pack).reshape(len(quads), 16, 128)


def edge_kernel(own_ref, first_ref, last_ref):
    for k in range(3):
        for p in range(4):
            at = 10 * (4 * k + p)
            first_ref[at : at + 10] = own_ref[k, p, :10]
            last_ref[at : at + 10] = own_ref[k, p, 6:]


def block_kernel(own_ref, before_ref, after_ref, block_ref, face_ref, mate_ref):
    left = lax.axis_index("c") == 0
    none = jnp.zeros((2, 128), F32)
    for k in range(3):
        for p in range(4):
            at = 10 * (4 * k + p)
            block_ref[k, p, 12:28] = own_ref[k, p]
            block_ref[k, p, 2:12] = before_ref[at : at + 10]
            block_ref[k, p, 28:38] = after_ref[at : at + 10]
            block_ref[k, p, :2] = none
            block_ref[k, p, 38:] = none

    def send(at, k, low, high, rows):
        low, high = block_ref[k, low, rows], block_ref[k, high, rows]
        size = low.shape[0]
        face_ref[at : at + size] = jnp.where(left, low, high)
        mate_ref[at : at + size] = jnp.where(left, high, low)

    for k in range(3):
        for p in range(2):
            send(40 * (2 * k + p), k, p, p + 2, slice(0, 40))
        send(240 + 24 * k, k, 2, 1, slice(8, 32))
    send(312, 1, 3, 0, slice(8, 32))
    face_ref[336:] = jnp.zeros((8, 128), F32)


def fine_kernel(
    own_ref, mate_ref, face_ref, iter_ref, field_ref, piece_ref, one_ref, coef_rows, rows_ref
):
    left = lax.axis_index("c") == 0
    face, mate = face_ref[:336], mate_ref[...]
    low, high = jnp.where(left, face, mate), jnp.where(left, mate, face)
    pad = jnp.zeros((1, 8, 128), F32)
    blocks = []
    for k in range(3):
        sides = []
        for t in (low, high):
            far = [t[240 + 24 * k : 264 + 24 * k], t[312:]]
            if k != 1:
                far[1] = jnp.zeros_like(far[1])
            far = [jnp.concatenate([pad, u[None], pad], axis=1) for u in far]
            sides.append([t[80 * k : 80 * k + 80].reshape(2, 40, 128)] + far)
        blocks.append(jnp.concatenate(sides[0][::-1] + [own_ref[k]] + sides[1], axis=0))
    f, a, s = blocks
    coefs = pair_planes([t[4 * p : 4 * p + 4] for t in (a, s) for p in range(3)], coef_rows)
    w = relax_weight(a[1:11], s[1:11], 1.0)
    u = w * f[1:11]
    u = u[1:-1] + w[1:-1] * (f[2:10] - fine_apply(u, a[2:10], s[2:10]))
    iter_ref[...] = u[:, 8:32]
    for k, t in enumerate((f[2:10], a[2:10], s[2:10], w[1:9])):
        field_ref[k] = t[:, 8:32]
    resid = f[4:8] - fine_apply(u[1:7], a[4:8], s[4:8])
    f = pair_planes([resid], rows_ref)
    a, s = coefs[:3], coefs[3:]
    for k, t in enumerate((f[0], a[1], s[1])):
        one_ref[k] = t

    none = jnp.zeros_like(f)
    f = jnp.concatenate([none, f, none], axis=0)
    w = relax_weight(a, s, 0.25)
    v = w * f
    v = v + w * (f - middle_apply(v, a, s))
    resid = f - middle_apply(v, a, s)
    spread = ones_where(iota((128, 128), 1) % 32 == (iota((128, 128), 0) % 64) // 2, 0.125)
    own = ones_where(iota((16, 128), 0) // 2 == iota((16, 128), 1) // 32 + 2)
    mixed = dot(resid.reshape(48, 128), spread).reshape(3, 16, 128)
    rows = [mixed[k] * own for k in range(3)]
    mixed = dot(jnp.concatenate([a[1], s[1]], axis=0), spread).reshape(2, 16, 128)
    rows += [mixed[k] * own for k in range(2)] + [jnp.zeros((1, 128), F32)] * 3
    piece = jnp.concatenate([jnp.sum(t, axis=0, keepdims=True) for t in rows], axis=0)
    piece_ref[...] = jnp.broadcast_to(piece[None], piece_ref.shape)


def middle_apply(v, scale, shift):
    rows = v.shape[1]
    lane = iota((rows, 128), 1)
    row = iota((rows, 128), 0)
    swap = pltpu.roll(v, 64, 2)
    edge = jnp.zeros_like(swap[:1])
    prev = jnp.concatenate([edge, swap[:-1]], axis=0)
    later = jnp.concatenate([swap[1:], edge], axis=0)
    box = v + swap + jnp.where(lane < 64, prev, later)
    box = (
        box
        + jnp.where(row > 0, pltpu.roll(box, 1, 1), 0.0)
        + jnp.where(row < rows - 1, pltpu.roll(box, rows - 1, 1), 0.0)
    )
    box = lane_box(box, 64)
    return 0.25 * scale * (27.0 * v - box) + shift * v


def quarter_row(shape, dim):
    i = iota(shape, dim)
    return 4 * (i % 8) + i // 8


def quarter_mask():
    return ones_where(iota((4, 8, 128), 2) // 32 == iota((4, 8, 128), 0))


def gather_kernel(got_ref, piece_ref, rows_ref):
    core = lax.axis_index("c")
    half = got_ref.shape[0] // 2
    rows_ref[: 2 * half] = got_ref[...]

    def column(at, k):
        return rows_ref[pl.ds(at * half + k, half // 8, stride=8)]

    outward = 2 * core
    piece = jnp.concatenate(
        [
            column(core, outward),
            column(core, 1) + column(1 - core, outward),
            column(core, 3),
            column(core, 4),
        ],
        axis=0,
    )
    piece_ref[...] = jnp.broadcast_to(piece[None], piece_ref.shape)


def smooth_kernel(
    own_ref, mate_ref, outer_ref, inner_ref, field_ref, iter_ref, matrix_ref
):
    left = lax.axis_index("c") == 0
    for k in range(3):
        mate, outer, inner = mate_ref[k], outer_ref[:, k], inner_ref[k]
        field_ref[k, 0] = jnp.where(left, outer[0], inner)
        field_ref[k, 1] = jnp.where(left, outer[1], mate)
        field_ref[k, 2] = own_ref[k]
        field_ref[k, 3] = jnp.where(left, mate, outer[0])
        field_ref[k, 4] = jnp.where(left, inner, outer[1])
    f, a, s = (field_ref[k] for k in range(3))
    w = relax_weight(a, s, 0.25)
    field_ref[3] = w
    v = w * f
    iter_ref[...] = v + w * (f - middle_apply(v, a, s))
    matrix_ref[...] = box_matrix()


def box_matrix():
    lane, out = iota((384, 256), 0) % 128, iota((384, 256), 1)
    group, to = lane // 32, out % 128 // 32
    near = jnp.abs(lane % 32 - out % 32) <= 1
    same = (out < 128) & (jnp.abs(group - to) <= 1)
    wrap = (out >= 128) & (jnp.abs(group - to) == 3)
    return ones_where(near & (same | wrap)).astype(jnp.bfloat16)


def coarse_box(v, matrix):
    rows = (v[:-2] + v[1:-1] + v[2:]).reshape(-1, 128)
    both = lax.dot_general(
        jnp.concatenate(split(rows), axis=1),
        matrix,
        (((1,), (0,)), ((), ())),
        preferred_element_type=F32,
    )
    box, wrap = (both[:, k : k + 128].reshape(-1, 8, 128) for k in (0, 128))
    lane, row = iota((8, 128), 1), iota((8, 128), 0)
    up = jnp.where((lane < 32) & (row > 0), pltpu.roll(wrap, 1, 1), 0.0)
    down = jnp.where((lane >= 96) & (row < 7), pltpu.roll(wrap, 7, 1), 0.0)
    return box + up + down


def total(plane):
    return jnp.sum(jnp.sum(plane, axis=0, keepdims=True), axis=1, keepdims=True)


def solve_coarse(q_ref, a_ref, d_ref, inverse_ref, w_ref, y_ref, at, matrix):
    planes = a_ref.shape[0]
    chunk = 16 if planes % 16 == 0 else 2
    starts = range(0, planes, chunk)
    none = jnp.zeros((2, 8, 128), F32)
    for ref in (q_ref, inverse_ref, w_ref):
        ref[:2] = none
        ref[planes + 2 :] = none
    for i in starts:
        own, padded = slice(i, i + chunk), slice(i + 2, i + chunk + 2)
        inverse_ref[padded] = 1.0 / (d_ref[own] - a_ref[own])

    def product(ref):
        for i in starts:
            own, wide = slice(i, i + chunk), slice(i + 1, i + chunk + 3)
            z = ref[wide] * inverse_ref[wide]
            y_ref[own] = d_ref[own] * z[1:-1] - a_ref[own] * coarse_box(z, matrix)

    product(q_ref)
    solution = jnp.zeros((5, 8, 128), F32)
    for step in range(COARSE):
        upper = lower = jnp.zeros((8, 128), F32)
        for i in starts:
            own, padded = slice(i, i + chunk), slice(i + 2, i + chunk + 2)
            w, q = y_ref[own], q_ref[padded]
            if step > 0:
                old = w_ref[padded]
                w, q = old - alpha * w, q - alpha * old
                q_ref[padded] = q
            w_ref[padded] = w
            upper = upper + jnp.sum(w * q, axis=0)
            lower = lower + jnp.sum(w * w, axis=0)
        alpha = (total(upper) / total(lower))[None]
        if step < COARSE - 1:
            product(w_ref)
        solution = solution + alpha * q_ref[pl.ds(at, 5)]
    return solution * inverse_ref[pl.ds(at, 5)]


def last_kernel(
    got_ref, mate_ref, matrix_ref, field_ref, middle_ref, fine_ref, iter_ref, out_ref,
    q_ref, a_ref, d_ref, inverse_ref, w_ref, y_ref, middle_rows, fine_rows,
):
    nx = lax.axis_size("x")
    chip = lax.axis_index("y") * nx + lax.axis_index("x")
    core = lax.axis_index("c")
    rank = lax.axis_index("z")
    planes = 2 * got_ref.shape[0]

    got, mate = got_ref[...], mate_ref[...]
    second = jnp.where(core == 0, mate, got)
    second = jnp.concatenate([second[i : i + 1] for i in reversed(range(planes // 2))], axis=0)
    halves = jnp.where(core == 0, got, mate), second

    def part(half, k):
        return halves[half][:, 8 * k : 8 * k + 8]

    def pairs(first, second):
        return jnp.concatenate([first[:, None], second[:, None]], axis=1).reshape(planes, 8, 128)

    edge = jnp.zeros_like(part(0, 0)[:1])
    q_ref[2 : planes + 2] = pairs(
        part(0, 1) + jnp.concatenate([edge, part(1, 0)[:-1]], axis=0),
        part(1, 1) + jnp.concatenate([part(0, 0)[1:], edge], axis=0),
    )
    a = 0.0625 * pairs(part(0, 2), part(1, 2))
    a_ref[...] = a
    d_ref[...] = 27.0 * a + pairs(part(0, 3), part(1, 3))
    near = solve_coarse(
        q_ref, a_ref, d_ref, inverse_ref, w_ref, y_ref, chip * 2 + core, matrix_ref[...]
    )

    mask = quarter_mask()
    stack = jnp.concatenate([(near[p][None] * mask).reshape(32, 128) for p in range(5)], axis=0)
    spread = ones_where(iota((128, 128), 0) % 32 == (iota((128, 128), 1) % 64) // 2)
    mixed = dot(stack, spread)
    size = (middle_rows.shape[0] - 16) // 5
    edge = jnp.zeros((4, 128), F32)
    window = []
    for p in range(5):
        at = size * p
        middle_rows[at : at + 4] = edge
        middle_rows[at + size - 4 : at + size] = edge
        for k in range(4):
            t = mixed[32 * p + 8 * k : 32 * p + 8 * k + 8]
            for i in (4, 5):
                middle_rows[pl.ds(at + 2 * k + i, 8, stride=8)] = t
        window.append(middle_rows[pl.ds(pl.multiple_of(at + rank * 8, 8), 16)][None])
    v = middle_ref[...] + jnp.concatenate(window, axis=0)
    f, a, s, w = (field_ref[k] for k in range(4))
    for _ in range(2):
        v = v + w * (f - middle_apply(v, a, s))

    lane, out = iota((128, 256), 0), iota((128, 256), 1)
    mixed = dot(v[1:4].reshape(48, 128), ones_where(lane == out // 2))
    halves = [mixed[:16, 128:], mixed[16:32, :128], mixed[16:32, 128:], mixed[32:, :128]]
    refined = []
    for p, t in enumerate(halves):
        for i in range(2):
            fine_rows[pl.ds(24 * p + i, 12, stride=2)] = t[2:14]
        refined += [fine_rows[24 * p : 24 * p + 24][None]] * 2
    refined = jnp.concatenate(refined, axis=0)

    f, a, s, w = (fine_ref[k] for k in range(4))
    u = iter_ref[...] + jnp.where(a > 0.25, refined, 0.0)
    for i in (1, 2):
        j = 8 - i
        u = u[1:-1] + w[i:j] * (f[i:j] - fine_apply(u, a[i:j], s[i:j]))
    out_ref[...] = u[:, 4:20]


def call(kernel, outs, *args, scratch=()):
    return pl.pallas_call(
        kernel,
        out_shape=[
            jax.ShapeDtypeStruct(*(out if isinstance(out[0], tuple) else (out, F32)))
            for out in outs
        ],
        in_specs=[pl.BlockSpec(memory_space=pltpu.VMEM)] * len(args),
        out_specs=[pl.BlockSpec(memory_space=pltpu.VMEM)] * len(outs),
        scratch_shapes=[pltpu.VMEM(shape, F32) for shape in scratch],
        compiler_params=pltpu.CompilerParams(vmem_limit_bytes=24 * 2**20),
    )(*args)


def shards(source, row_scale, shift_field):
    ny, nx, nz = lax.axis_size("y"), lax.axis_size("x"), lax.axis_size("z")
    chips = ny * nx
    first = lax.axis_index("c") == 0

    own = jnp.stack([source, row_scale, shift_field])
    head, tail = call(edge_kernel, [(120, 128), (120, 128)], own)
    up = [(i, i + 1) for i in range(nz - 1)]
    down = [(i + 1, i) for i in range(nz - 1)]
    before = lax.ppermute(tail, "z", up)
    after = lax.ppermute(head, "z", down)
    own, face, mate = call(
        block_kernel, [(3, 4, 40, 128), (344, 128), (336, 128)], own, before, after
    )
    facing = []
    for i in range(chips - 1):
        facing += [(2 * i + 1, 2 * i + 2), (2 * i + 2, 2 * i + 1)]
    swap = [(0, 1), (1, 0)]
    face = lax.ppermute(face, ("y", "x", "c"), facing)
    mate = lax.ppermute(mate, "c", swap)
    fine_iter, fine_fields, sent, one = call(
        fine_kernel,
        [(8, 24, 128), (4, 8, 24, 128), (2 * nz, 8, 128), (3, 16, 128)],
        own, mate, face,
        scratch=[(12 * 40 + 16, 128), (2 * 40 + 16, 128)],
    )

    got = lax.all_to_all(sent, ("c", "z"), 0, 0).reshape(16 * nz, 128)
    (sent,) = call(
        gather_kernel, [(chips, 32, 128)], got, scratch=[(16 * nz + 16, 128)]
    )
    one, sent = lax.optimization_barrier((one, sent))
    evens = list(range(0, 2 * chips, 2))
    odds = [i + 1 for i in reversed(evens)]
    half = lax.all_to_all(
        sent, ("y", "x", "c"), 0, 0, axis_index_groups=[evens, odds]
    )

    mate = lax.ppermute(one, "c", swap)
    pairs = jnp.stack([jnp.where(first, one, mate), jnp.where(first, mate, one)])
    ring = []
    for i in range(chips - 1):
        ring += [(2 * i, 2 * i + 2), (2 * i + 3, 2 * i + 1)]
    outer = lax.ppermute(pairs, ("y", "x", "c"), ring)
    inner = lax.ppermute(one, ("y", "x", "c"), [(j, i) for i, j in ring])
    fields, middle_iter, matrix = call(
        smooth_kernel,
        [(4, 5, 16, 128), (5, 16, 128), ((384, 256), jnp.bfloat16)],
        one, mate, outer, inner,
    )
    half, fields, middle_iter = lax.optimization_barrier((half, fields, middle_iter))
    half_mate = lax.ppermute(half, "c", swap)
    (result,) = call(
        last_kernel, [source.shape],
        half, half_mate, matrix, fields, middle_iter, fine_fields, fine_iter,
        scratch=[(2 * chips + 4, 8, 128)] + [(2 * chips, 8, 128)] * 2
        + [(2 * chips + 4, 8, 128)] * 2 + [(2 * chips, 8, 128)]
        + [(5 * (8 * nz + 8) + 16, 128), (4 * 24 + 16, 128)],
    )
    return result


def solution(mesh):
    ny, nx = (8, 4) if mesh.devices.shape[0] == 64 else (mesh.devices.shape[0] // 2, 1)
    nz = mesh.devices.shape[1]
    split = Mesh(mesh.devices.reshape(ny, nx, 2, nz), ("y", "x", "c", "z"))
    spec = P(("y", "x", "c"), "z", None)
    return jax.shard_map(
        shards, mesh=split, in_specs=(spec, spec, spec), out_specs=spec, check_vma=False
    )
```

```python
import jax
import jax.numpy as jnp
from jax import lax
from jax.experimental import pallas as pl
from jax.experimental.pallas import tpu as pltpu
from jax.sharding import Mesh, PartitionSpec as P

COARSE = 4
DAMPING = 0.8
F32 = jnp.float32


def split(a):
    high = a.astype(jnp.bfloat16)
    rest = a - high.astype(F32)
    middle = rest.astype(jnp.bfloat16)
    low = (rest - middle.astype(F32)).astype(jnp.bfloat16)
    return [high, middle, low]


def dot(a, b):
    parts = lax.dot_general(
        jnp.concatenate(split(a), axis=0),
        b.astype(jnp.bfloat16),
        (((1,), (0,)), ((), ())),
        preferred_element_type=F32,
    )
    n = a.shape[0]
    return parts[:n] + parts[n : 2 * n] + parts[2 * n :]


def iota(shape, dim):
    return lax.broadcasted_iota(jnp.int32, shape, dim)


def ones_where(cond, value=1.0):
    return jnp.where(cond, jnp.float32(value), jnp.float32(0.0))


def lane_box(v, period):
    axis = v.ndim - 1
    lane = iota(v.shape[-2:], 1) % period
    below = jnp.where(lane > 0, pltpu.roll(v, 1, axis), 0.0)
    above = jnp.where(lane < period - 1, pltpu.roll(v, 127, axis), 0.0)
    return v + below + above


def relax_weight(scale, shift, level_scale):
    inside = scale > 0.25
    diag = jnp.where(inside, 26.0 * level_scale * scale + shift, 1.0)
    return jnp.where(inside, DAMPING / diag, 0.0)


def fine_apply(v, scale, shift):
    rows = v.shape[1]
    box = v[:-2] + v[1:-1] + v[2:]
    box = box + pltpu.roll(box, 1, 1) + pltpu.roll(box, rows - 1, 1)
    box = lane_box(box, 128)
    mid = v[1:-1]
    return scale * (27.0 * mid - box) + shift * mid


def pair_planes(quads, rows_ref):
    parts = []
    for k, t in enumerate(quads):
        halves = []
        for i in (0, 2):
            at = 40 * (2 * k + i // 2)
            rows_ref[at : at + 40] = t[i] + t[i + 1]
            halves.append(
                rows_ref[pl.ds(at + 4, 16, stride=2)] + rows_ref[pl.ds(at + 5, 16, stride=2)]
            )
        parts.append(jnp.concatenate(halves, axis=1))
    lane, out = iota((256, 128), 0), iota((256, 128), 1)
    pack = ones_where(lane // 2 == out, 0.125)
    return dot(jnp.concatenate(parts, axis=0), pack).reshape(len(quads), 16, 128)


def edge_kernel(own_ref, first_ref, last_ref):
    for k in range(3):
        for p in range(4):
            at = 10 * (4 * k + p)
            first_ref[at : at + 10] = own_ref[k, p, :10]
            last_ref[at : at + 10] = own_ref[k, p, 6:]


def block_kernel(own_ref, before_ref, after_ref, block_ref, face_ref, mate_ref):
    left = lax.axis_index("c") == 0
    none = jnp.zeros((2, 128), F32)
    for k in range(3):
        for p in range(4):
            at = 10 * (4 * k + p)
            block_ref[k, p, 12:28] = own_ref[k, p]
            block_ref[k, p, 2:12] = before_ref[at : at + 10]
            block_ref[k, p, 28:38] = after_ref[at : at + 10]
            block_ref[k, p, :2] = none
            block_ref[k, p, 38:] = none

    def send(at, k, low, high, rows):
        low, high = block_ref[k, low, rows], block_ref[k, high, rows]
        size = low.shape[0]
        face_ref[at : at + size] = jnp.where(left, low, high)
        mate_ref[at : at + size] = jnp.where(left, high, low)

    for k in range(3):
        for p in range(2):
            send(40 * (2 * k + p), k, p, p + 2, slice(0, 40))
        send(240 + 24 * k, k, 2, 1, slice(8, 32))
    send(312, 1, 3, 0, slice(8, 32))
    face_ref[336:] = jnp.zeros((8, 128), F32)


def fine_kernel(
    own_ref, mate_ref, face_ref, iter_ref, field_ref, piece_ref, one_ref, coef_rows, rows_ref
):
    left = lax.axis_index("c") == 0
    face, mate = face_ref[:336], mate_ref[...]
    low, high = jnp.where(left, face, mate), jnp.where(left, mate, face)
    pad = jnp.zeros((1, 8, 128), F32)
    blocks = []
    for k in range(3):
        sides = []
        for t in (low, high):
            far = [t[240 + 24 * k : 264 + 24 * k], t[312:]]
            if k != 1:
                far[1] = jnp.zeros_like(far[1])
            far = [jnp.concatenate([pad, u[None], pad], axis=1) for u in far]
            sides.append([t[80 * k : 80 * k + 80].reshape(2, 40, 128)] + far)
        blocks.append(jnp.concatenate(sides[0][::-1] + [own_ref[k]] + sides[1], axis=0))
    f, a, s = blocks
    coefs = pair_planes([t[4 * p : 4 * p + 4] for t in (a, s) for p in range(3)], coef_rows)
    w = relax_weight(a[1:11], s[1:11], 1.0)
    u = w * f[1:11]
    u = u[1:-1] + w[1:-1] * (f[2:10] - fine_apply(u, a[2:10], s[2:10]))
    iter_ref[...] = u[:, 8:32]
    for k, t in enumerate((f[2:10], a[2:10], s[2:10], w[1:9])):
        field_ref[k] = t[:, 8:32]
    resid = f[4:8] - fine_apply(u[1:7], a[4:8], s[4:8])
    f = pair_planes([resid], rows_ref)
    a, s = coefs[:3], coefs[3:]
    for k, t in enumerate((f[0], a[1], s[1])):
        one_ref[k] = t

    none = jnp.zeros_like(f)
    f = jnp.concatenate([none, f, none], axis=0)
    w = relax_weight(a, s, 0.25)
    v = w * f
    v = v + w * (f - middle_apply(v, a, s))
    resid = f - middle_apply(v, a, s)
    spread = ones_where(iota((128, 128), 1) % 32 == (iota((128, 128), 0) % 64) // 2, 0.125)
    own = ones_where(iota((16, 128), 0) // 2 == iota((16, 128), 1) // 32 + 2)
    mixed = dot(resid.reshape(48, 128), spread).reshape(3, 16, 128)
    rows = [mixed[k] * own for k in range(3)]
    mixed = dot(jnp.concatenate([a[1], s[1]], axis=0), spread).reshape(2, 16, 128)
    rows += [mixed[k] * own for k in range(2)] + [jnp.zeros((1, 128), F32)] * 3
    piece = jnp.concatenate([jnp.sum(t, axis=0, keepdims=True) for t in rows], axis=0)
    piece_ref[...] = jnp.broadcast_to(piece[None], piece_ref.shape)


def middle_apply(v, scale, shift):
    rows = v.shape[1]
    lane = iota((rows, 128), 1)
    row = iota((rows, 128), 0)
    swap = pltpu.roll(v, 64, 2)
    edge = jnp.zeros_like(swap[:1])
    prev = jnp.concatenate([edge, swap[:-1]], axis=0)
    later = jnp.concatenate([swap[1:], edge], axis=0)
    box = v + swap + jnp.where(lane < 64, prev, later)
    box = (
        box
        + jnp.where(row > 0, pltpu.roll(box, 1, 1), 0.0)
        + jnp.where(row < rows - 1, pltpu.roll(box, rows - 1, 1), 0.0)
    )
    box = lane_box(box, 64)
    return 0.25 * scale * (27.0 * v - box) + shift * v


def quarter_row(shape, dim):
    i = iota(shape, dim)
    return 4 * (i % 8) + i // 8


def quarter_mask():
    return ones_where(iota((4, 8, 128), 2) // 32 == iota((4, 8, 128), 0))


def gather_kernel(got_ref, piece_ref, rows_ref, block_ref, sems):
    core = lax.axis_index("c")
    half = got_ref.shape[0] // 2
    rows_ref[: 2 * half] = got_ref[...]

    def column(at, k):
        return rows_ref[pl.ds(at * half + k, half // 8, stride=8)]

    outward = 2 * core
    piece = jnp.concatenate(
        [
            column(core, outward),
            column(core, 1) + column(1 - core, outward),
            column(core, 3),
            column(core, 4),
        ],
        axis=0,
    )
    block_ref[...] = jnp.broadcast_to(piece[None], block_ref.shape)
    size = block_ref.shape[0]
    copies = [
        pltpu.make_async_copy(block_ref, piece_ref.at[pl.ds(size * k, size)], sems.at[k])
        for k in range(piece_ref.shape[0] // size)
    ]
    for copy in copies:
        copy.start()
    for copy in copies:
        copy.wait()


def smooth_kernel(
    own_ref, mate_ref, outer_ref, inner_ref, field_ref, iter_ref, matrix_ref
):
    left = lax.axis_index("c") == 0
    for k in range(3):
        mate, outer, inner = mate_ref[k], outer_ref[:, k], inner_ref[k]
        field_ref[k, 0] = jnp.where(left, outer[0], inner)
        field_ref[k, 1] = jnp.where(left, outer[1], mate)
        field_ref[k, 2] = own_ref[k]
        field_ref[k, 3] = jnp.where(left, mate, outer[0])
        field_ref[k, 4] = jnp.where(left, inner, outer[1])
    f, a, s = (field_ref[k] for k in range(3))
    w = relax_weight(a, s, 0.25)
    field_ref[3] = w
    v = w * f
    iter_ref[...] = v + w * (f - middle_apply(v, a, s))
    matrix_ref[...] = box_matrix()


def box_matrix():
    lane, out = iota((384, 256), 0) % 128, iota((384, 256), 1)
    group, to = lane // 32, out % 128 // 32
    near = jnp.abs(lane % 32 - out % 32) <= 1
    same = (out < 128) & (jnp.abs(group - to) <= 1)
    wrap = (out >= 128) & (jnp.abs(group - to) == 3)
    return ones_where(near & (same | wrap)).astype(jnp.bfloat16)


def coarse_box(v, matrix):
    rows = (v[:-2] + v[1:-1] + v[2:]).reshape(-1, 128)
    both = lax.dot_general(
        jnp.concatenate(split(rows), axis=1),
        matrix,
        (((1,), (0,)), ((), ())),
        preferred_element_type=F32,
    )
    box, wrap = (both[:, k : k + 128].reshape(-1, 8, 128) for k in (0, 128))
    lane, row = iota((8, 128), 1), iota((8, 128), 0)
    up = jnp.where((lane < 32) & (row > 0), pltpu.roll(wrap, 1, 1), 0.0)
    down = jnp.where((lane >= 96) & (row < 7), pltpu.roll(wrap, 7, 1), 0.0)
    return box + up + down


def total(plane):
    return jnp.sum(jnp.sum(plane, axis=0, keepdims=True), axis=1, keepdims=True)


def solve_coarse(q_ref, a_ref, d_ref, inverse_ref, w_ref, y_ref, at, matrix):
    planes = a_ref.shape[0]
    chunk = 16 if planes % 16 == 0 else 2
    starts = range(0, planes, chunk)
    none = jnp.zeros((2, 8, 128), F32)
    for ref in (q_ref, inverse_ref, w_ref):
        ref[:2] = none
        ref[planes + 2 :] = none
    for i in starts:
        own, padded = slice(i, i + chunk), slice(i + 2, i + chunk + 2)
        inverse_ref[padded] = 1.0 / (d_ref[own] - a_ref[own])

    def product(ref):
        for i in starts:
            own, wide = slice(i, i + chunk), slice(i + 1, i + chunk + 3)
            z = ref[wide] * inverse_ref[wide]
            y_ref[own] = d_ref[own] * z[1:-1] - a_ref[own] * coarse_box(z, matrix)

    product(q_ref)
    solution = jnp.zeros((5, 8, 128), F32)
    for step in range(COARSE):
        upper = lower = jnp.zeros((8, 128), F32)
        for i in starts:
            own, padded = slice(i, i + chunk), slice(i + 2, i + chunk + 2)
            w, q = y_ref[own], q_ref[padded]
            if step > 0:
                old = w_ref[padded]
                w, q = old - alpha * w, q - alpha * old
                q_ref[padded] = q
            w_ref[padded] = w
            upper = upper + jnp.sum(w * q, axis=0)
            lower = lower + jnp.sum(w * w, axis=0)
        alpha = (total(upper) / total(lower))[None]
        if step < COARSE - 1:
            product(w_ref)
        solution = solution + alpha * q_ref[pl.ds(at, 5)]
    return solution * inverse_ref[pl.ds(at, 5)]


def chip_order(ny, nx):
    rows = [0]
    while len(rows) < ny:
        step = ny // (2 * len(rows))
        rows = rows + [r + step for r in rows]
    return [nx * r + x for r in rows for x in range(nx)]


def last_kernel(
    got_ref, mate_ref, matrix_ref, field_ref, middle_ref, fine_ref, iter_ref, out_ref,
    q_ref, a_ref, d_ref, inverse_ref, w_ref, y_ref, middle_rows, fine_rows,
):
    nx = lax.axis_size("x")
    chip = lax.axis_index("y") * nx + lax.axis_index("x")
    core = lax.axis_index("c")
    rank = lax.axis_index("z")
    planes = 2 * got_ref.shape[0]

    got, mate = got_ref[...], mate_ref[...]
    order = chip_order(lax.axis_size("y"), nx)
    place = [order.index(chip) for chip in range(len(order))]
    halves = []
    for half in (jnp.where(core == 0, got, mate), jnp.where(core == 0, mate, got)):
        halves.append(jnp.concatenate([half[i : i + 1] for i in place], axis=0))
        place = [len(order) - 1 - i for i in place]

    def part(half, k):
        return halves[half][:, 8 * k : 8 * k + 8]

    def pairs(first, second):
        return jnp.concatenate([first[:, None], second[:, None]], axis=1).reshape(planes, 8, 128)

    edge = jnp.zeros_like(part(0, 0)[:1])
    q_ref[2 : planes + 2] = pairs(
        part(0, 1) + jnp.concatenate([edge, part(1, 0)[:-1]], axis=0),
        part(1, 1) + jnp.concatenate([part(0, 0)[1:], edge], axis=0),
    )
    a = 0.0625 * pairs(part(0, 2), part(1, 2))
    a_ref[...] = a
    d_ref[...] = 27.0 * a + pairs(part(0, 3), part(1, 3))
    near = solve_coarse(
        q_ref, a_ref, d_ref, inverse_ref, w_ref, y_ref, chip * 2 + core, matrix_ref[...]
    )

    mask = quarter_mask()
    stack = jnp.concatenate([(near[p][None] * mask).reshape(32, 128) for p in range(5)], axis=0)
    spread = ones_where(iota((128, 128), 0) % 32 == (iota((128, 128), 1) % 64) // 2)
    mixed = dot(stack, spread)
    size = (middle_rows.shape[0] - 16) // 5
    edge = jnp.zeros((4, 128), F32)
    window = []
    for p in range(5):
        at = size * p
        middle_rows[at : at + 4] = edge
        middle_rows[at + size - 4 : at + size] = edge
        for k in range(4):
            t = mixed[32 * p + 8 * k : 32 * p + 8 * k + 8]
            for i in (4, 5):
                middle_rows[pl.ds(at + 2 * k + i, 8, stride=8)] = t
        window.append(middle_rows[pl.ds(pl.multiple_of(at + rank * 8, 8), 16)][None])
    v = middle_ref[...] + jnp.concatenate(window, axis=0)
    f, a, s, w = (field_ref[k] for k in range(4))
    for _ in range(2):
        v = v + w * (f - middle_apply(v, a, s))

    lane, out = iota((128, 256), 0), iota((128, 256), 1)
    mixed = dot(v[1:4].reshape(48, 128), ones_where(lane == out // 2))
    halves = [mixed[:16, 128:], mixed[16:32, :128], mixed[16:32, 128:], mixed[32:, :128]]
    refined = []
    for p, t in enumerate(halves):
        for i in range(2):
            fine_rows[pl.ds(24 * p + i, 12, stride=2)] = t[2:14]
        refined += [fine_rows[24 * p : 24 * p + 24][None]] * 2
    refined = jnp.concatenate(refined, axis=0)

    f, a, s, w = (fine_ref[k] for k in range(4))
    u = iter_ref[...] + jnp.where(a > 0.25, refined, 0.0)
    for i in (1, 2):
        j = 8 - i
        u = u[1:-1] + w[i:j] * (f[i:j] - fine_apply(u, a[i:j], s[i:j]))
    out_ref[...] = u[:, 4:20]


def call(kernel, outs, *args, scratch=()):
    return pl.pallas_call(
        kernel,
        out_shape=[
            jax.ShapeDtypeStruct(*(out if isinstance(out[0], tuple) else (out, F32)))
            for out in outs
        ],
        in_specs=[pl.BlockSpec(memory_space=pltpu.VMEM)] * len(args),
        out_specs=[pl.BlockSpec(memory_space=pltpu.VMEM)] * len(outs),
        scratch_shapes=[pltpu.VMEM(shape, F32) for shape in scratch],
        compiler_params=pltpu.CompilerParams(vmem_limit_bytes=24 * 2**20),
    )(*args)


def shards(source, row_scale, shift_field):
    ny, nx, nz = lax.axis_size("y"), lax.axis_size("x"), lax.axis_size("z")
    chips = ny * nx
    first = lax.axis_index("c") == 0

    own = jnp.stack([source, row_scale, shift_field])
    head, tail = call(edge_kernel, [(120, 128), (120, 128)], own)
    up = [(i, i + 1) for i in range(nz - 1)]
    down = [(i + 1, i) for i in range(nz - 1)]
    before = lax.ppermute(tail, "z", up)
    after = lax.ppermute(head, "z", down)
    own, face, mate = call(
        block_kernel, [(3, 4, 40, 128), (344, 128), (336, 128)], own, before, after
    )
    facing = []
    for i in range(chips - 1):
        facing += [(2 * i + 1, 2 * i + 2), (2 * i + 2, 2 * i + 1)]
    swap = [(0, 1), (1, 0)]
    face = lax.ppermute(face, ("y", "x", "c"), facing)
    mate = lax.ppermute(mate, "c", swap)
    fine_iter, fine_fields, sent, one = call(
        fine_kernel,
        [(8, 24, 128), (4, 8, 24, 128), (2 * nz, 8, 128), (3, 16, 128)],
        own, mate, face,
        scratch=[(12 * 40 + 16, 128), (2 * 40 + 16, 128)],
    )

    got = lax.all_to_all(sent, ("c", "z"), 0, 0).reshape(16 * nz, 128)
    size = 4 if chips % 4 == 0 else 1
    sent = pl.pallas_call(
        gather_kernel,
        out_shape=jax.ShapeDtypeStruct((chips, 32, 128), F32),
        in_specs=[pl.BlockSpec(memory_space=pltpu.VMEM)],
        out_specs=pl.BlockSpec(memory_space=pl.ANY),
        scratch_shapes=[
            pltpu.VMEM((16 * nz + 16, 128), F32),
            pltpu.VMEM((size, 32, 128), F32),
            pltpu.SemaphoreType.DMA((chips // size,)),
        ],
        compiler_params=pltpu.CompilerParams(vmem_limit_bytes=24 * 2**20),
    )(got)
    one, sent = lax.optimization_barrier((one, sent))
    evens = [2 * chip for chip in chip_order(ny, nx)]
    odds = [i + 1 for i in reversed(evens)]
    half = lax.all_to_all(
        sent, ("y", "x", "c"), 0, 0, axis_index_groups=[evens, odds]
    )

    mate = lax.ppermute(one, "c", swap)
    pairs = jnp.stack([jnp.where(first, one, mate), jnp.where(first, mate, one)])
    ring = []
    for i in range(chips - 1):
        ring += [(2 * i, 2 * i + 2), (2 * i + 3, 2 * i + 1)]
    outer = lax.ppermute(pairs, ("y", "x", "c"), ring)
    inner = lax.ppermute(one, ("y", "x", "c"), [(j, i) for i, j in ring])
    fields, middle_iter, matrix = call(
        smooth_kernel,
        [(4, 5, 16, 128), (5, 16, 128), ((384, 256), jnp.bfloat16)],
        one, mate, outer, inner,
    )
    half, fields, middle_iter = lax.optimization_barrier((half, fields, middle_iter))
    half_mate = lax.ppermute(half, "c", swap)
    (result,) = call(
        last_kernel, [source.shape],
        half, half_mate, matrix, fields, middle_iter, fine_fields, fine_iter,
        scratch=[(2 * chips + 4, 8, 128)] + [(2 * chips, 8, 128)] * 2
        + [(2 * chips + 4, 8, 128)] * 2 + [(2 * chips, 8, 128)]
        + [(5 * (8 * nz + 8) + 16, 128), (4 * 24 + 16, 128)],
    )
    return result


def solution(mesh):
    ny, nx = (8, 4) if mesh.devices.shape[0] == 64 else (mesh.devices.shape[0] // 2, 1)
    nz = mesh.devices.shape[1]
    split = Mesh(mesh.devices.reshape(ny, nx, 2, nz), ("y", "x", "c", "z"))
    spec = P(("y", "x", "c"), "z", None)
    return jax.shard_map(
        shards, mesh=split, in_specs=(spec, spec, spec), out_specs=spec, check_vma=False
    )
```

```python
import jax
import jax.numpy as jnp
from jax import lax
from jax.experimental import pallas as pl
from jax.experimental.pallas import tpu as pltpu
from jax.sharding import Mesh, PartitionSpec as P

COARSE = 4
DAMPING = 0.8
F32 = jnp.float32


def split(a):
    high = a.astype(jnp.bfloat16)
    rest = a - high.astype(F32)
    middle = rest.astype(jnp.bfloat16)
    low = (rest - middle.astype(F32)).astype(jnp.bfloat16)
    return [high, middle, low]


def dot(a, b):
    parts = lax.dot_general(
        jnp.concatenate(split(a), axis=0),
        b.astype(jnp.bfloat16),
        (((1,), (0,)), ((), ())),
        preferred_element_type=F32,
    )
    n = a.shape[0]
    return parts[:n] + parts[n : 2 * n] + parts[2 * n :]


def iota(shape, dim):
    return lax.broadcasted_iota(jnp.int32, shape, dim)


def ones_where(cond, value=1.0):
    return jnp.where(cond, jnp.float32(value), jnp.float32(0.0))


def lane_box(v, period):
    axis = v.ndim - 1
    lane = iota(v.shape[-2:], 1) % period
    below = jnp.where(lane > 0, pltpu.roll(v, 1, axis), 0.0)
    above = jnp.where(lane < period - 1, pltpu.roll(v, 127, axis), 0.0)
    return v + below + above


def relax_weight(scale, shift, level_scale):
    inside = scale > 0.25
    diag = jnp.where(inside, 26.0 * level_scale * scale + shift, 1.0)
    return jnp.where(inside, DAMPING / diag, 0.0)


def fine_apply(v, scale, shift):
    rows = v.shape[1]
    box = v[:-2] + v[1:-1] + v[2:]
    box = box + pltpu.roll(box, 1, 1) + pltpu.roll(box, rows - 1, 1)
    box = lane_box(box, 128)
    mid = v[1:-1]
    return scale * (27.0 * mid - box) + shift * mid


def pair_planes(quads, rows_ref):
    parts = []
    for k, t in enumerate(quads):
        halves = []
        for i in (0, 2):
            at = 40 * (2 * k + i // 2)
            rows_ref[at : at + 40] = t[i] + t[i + 1]
            halves.append(
                rows_ref[pl.ds(at + 4, 16, stride=2)] + rows_ref[pl.ds(at + 5, 16, stride=2)]
            )
        parts.append(jnp.concatenate(halves, axis=1))
    lane, out = iota((256, 128), 0), iota((256, 128), 1)
    pack = ones_where(lane // 2 == out, 0.125)
    return dot(jnp.concatenate(parts, axis=0), pack).reshape(len(quads), 16, 128)


def edge_kernel(own_ref, first_ref, last_ref):
    for k in range(3):
        for p in range(4):
            at = 10 * (4 * k + p)
            first_ref[at : at + 10] = own_ref[k, p, :10]
            last_ref[at : at + 10] = own_ref[k, p, 6:]


def block_kernel(own_ref, before_ref, after_ref, block_ref, face_ref, mate_ref):
    left = lax.axis_index("c") == 0
    none = jnp.zeros((2, 128), F32)
    for k in range(3):
        for p in range(4):
            at = 10 * (4 * k + p)
            block_ref[k, p, 12:28] = own_ref[k, p]
            block_ref[k, p, 2:12] = before_ref[at : at + 10]
            block_ref[k, p, 28:38] = after_ref[at : at + 10]
            block_ref[k, p, :2] = none
            block_ref[k, p, 38:] = none

    def send(at, k, low, high, rows):
        low, high = block_ref[k, low, rows], block_ref[k, high, rows]
        size = low.shape[0]
        face_ref[at : at + size] = jnp.where(left, low, high)
        mate_ref[at : at + size] = jnp.where(left, high, low)

    for k in range(3):
        for p in range(2):
            send(40 * (2 * k + p), k, p, p + 2, slice(0, 40))
        send(240 + 24 * k, k, 2, 1, slice(8, 32))
    send(312, 1, 3, 0, slice(8, 32))
    face_ref[336:] = jnp.zeros((8, 128), F32)


def fine_kernel(
    own_ref, mate_ref, face_ref, iter_ref, field_ref, piece_ref, one_ref, coef_rows, rows_ref
):
    left = lax.axis_index("c") == 0
    face, mate = face_ref[:336], mate_ref[...]
    low, high = jnp.where(left, face, mate), jnp.where(left, mate, face)
    pad = jnp.zeros((1, 8, 128), F32)
    blocks = []
    for k in range(3):
        sides = []
        for t in (low, high):
            far = [t[240 + 24 * k : 264 + 24 * k], t[312:]]
            if k != 1:
                far[1] = jnp.zeros_like(far[1])
            far = [jnp.concatenate([pad, u[None], pad], axis=1) for u in far]
            sides.append([t[80 * k : 80 * k + 80].reshape(2, 40, 128)] + far)
        blocks.append(jnp.concatenate(sides[0][::-1] + [own_ref[k]] + sides[1], axis=0))
    f, a, s = blocks
    coefs = pair_planes([t[4 * p : 4 * p + 4] for t in (a, s) for p in range(3)], coef_rows)
    w = relax_weight(a[1:11], s[1:11], 1.0)
    u = w * f[1:11]
    u = u[1:-1] + w[1:-1] * (f[2:10] - fine_apply(u, a[2:10], s[2:10]))
    iter_ref[...] = u[:, 8:32]
    for k, t in enumerate((f[2:10], a[2:10], s[2:10], w[1:9])):
        field_ref[k] = t[:, 8:32]
    resid = f[4:8] - fine_apply(u[1:7], a[4:8], s[4:8])
    f = pair_planes([resid], rows_ref)
    a, s = coefs[:3], coefs[3:]
    for k, t in enumerate((f[0], a[1], s[1])):
        one_ref[k] = t

    none = jnp.zeros_like(f)
    f = jnp.concatenate([none, f, none], axis=0)
    w = relax_weight(a, s, 0.25)
    v = w * f
    v = v + w * (f - middle_apply(v, a, s))
    resid = f - middle_apply(v, a, s)
    spread = ones_where(iota((128, 128), 1) % 32 == (iota((128, 128), 0) % 64) // 2, 0.125)
    own = ones_where(iota((16, 128), 0) // 2 == iota((16, 128), 1) // 32 + 2)
    mixed = dot(resid.reshape(48, 128), spread).reshape(3, 16, 128)
    rows = [mixed[k] * own for k in range(3)]
    mixed = dot(jnp.concatenate([a[1], s[1]], axis=0), spread).reshape(2, 16, 128)
    rows += [mixed[k] * own for k in range(2)] + [jnp.zeros((1, 128), F32)] * 3
    piece = jnp.concatenate([jnp.sum(t, axis=0, keepdims=True) for t in rows], axis=0)
    piece_ref[...] = jnp.broadcast_to(piece[None], piece_ref.shape)


def middle_apply(v, scale, shift):
    rows = v.shape[1]
    lane = iota((rows, 128), 1)
    row = iota((rows, 128), 0)
    swap = pltpu.roll(v, 64, 2)
    edge = jnp.zeros_like(swap[:1])
    prev = jnp.concatenate([edge, swap[:-1]], axis=0)
    later = jnp.concatenate([swap[1:], edge], axis=0)
    box = v + swap + jnp.where(lane < 64, prev, later)
    box = (
        box
        + jnp.where(row > 0, pltpu.roll(box, 1, 1), 0.0)
        + jnp.where(row < rows - 1, pltpu.roll(box, rows - 1, 1), 0.0)
    )
    box = lane_box(box, 64)
    return 0.25 * scale * (27.0 * v - box) + shift * v


def quarter_row(shape, dim):
    i = iota(shape, dim)
    return 4 * (i % 8) + i // 8


def quarter_mask():
    return ones_where(iota((4, 8, 128), 2) // 32 == iota((4, 8, 128), 0))


def gather_kernel(got_ref, piece_ref, rows_ref, block_ref, sems):
    core = lax.axis_index("c")
    half = got_ref.shape[0] // 2
    rows_ref[: 2 * half] = got_ref[...]

    def column(at, k):
        return rows_ref[pl.ds(at * half + k, half // 8, stride=8)]

    outward = 2 * core
    piece = jnp.concatenate(
        [
            column(core, outward),
            column(core, 1) + column(1 - core, outward),
            column(core, 3),
            column(core, 4),
        ],
        axis=0,
    )
    block_ref[...] = jnp.broadcast_to(piece[None], block_ref.shape)
    size = block_ref.shape[0]
    copies = [
        pltpu.make_async_copy(block_ref, piece_ref.at[pl.ds(size * k, size)], sems.at[k])
        for k in range(piece_ref.shape[0] // size)
    ]
    for copy in copies:
        copy.start()
    for copy in copies:
        copy.wait()


def smooth_kernel(
    own_ref, mate_ref, outer_ref, inner_ref, field_ref, iter_ref, matrix_ref
):
    left = lax.axis_index("c") == 0
    for k in range(3):
        mate, outer, inner = mate_ref[k], outer_ref[:, k], inner_ref[k]
        field_ref[k, 0] = jnp.where(left, outer[0], inner)
        field_ref[k, 1] = jnp.where(left, outer[1], mate)
        field_ref[k, 2] = own_ref[k]
        field_ref[k, 3] = jnp.where(left, mate, outer[0])
        field_ref[k, 4] = jnp.where(left, inner, outer[1])
    f, a, s = (field_ref[k] for k in range(3))
    w = relax_weight(a, s, 0.25)
    field_ref[3] = w
    v = w * f
    iter_ref[...] = v + w * (f - middle_apply(v, a, s))
    matrix_ref[...] = box_matrix()


def box_matrix():
    lane, out = iota((384, 256), 0) % 128, iota((384, 256), 1)
    group, to = lane // 32, out % 128 // 32
    near = jnp.abs(lane % 32 - out % 32) <= 1
    same = (out < 128) & (jnp.abs(group - to) <= 1)
    wrap = (out >= 128) & (jnp.abs(group - to) == 3)
    return ones_where(near & (same | wrap)).astype(jnp.bfloat16)


def coarse_box(v, matrix):
    rows = (v[:-2] + v[1:-1] + v[2:]).reshape(-1, 128)
    both = lax.dot_general(
        jnp.concatenate(split(rows), axis=1),
        matrix,
        (((1,), (0,)), ((), ())),
        preferred_element_type=F32,
    )
    box, wrap = (both[:, k : k + 128].reshape(-1, 8, 128) for k in (0, 128))
    lane, row = iota((8, 128), 1), iota((8, 128), 0)
    up = jnp.where((lane < 32) & (row > 0), pltpu.roll(wrap, 1, 1), 0.0)
    down = jnp.where((lane >= 96) & (row < 7), pltpu.roll(wrap, 7, 1), 0.0)
    return box + up + down


def total(plane):
    return jnp.sum(jnp.sum(plane, axis=0, keepdims=True), axis=1, keepdims=True)


def solve_coarse(q_ref, a_ref, d_ref, inverse_ref, w_ref, y_ref, at, matrix):
    planes = a_ref.shape[0]
    chunk = 16 if planes % 16 == 0 else 2
    starts = range(0, planes, chunk)
    none = jnp.zeros((2, 8, 128), F32)
    for ref in (q_ref, inverse_ref, w_ref):
        ref[:2] = none
        ref[planes + 2 :] = none
    for i in starts:
        own, padded = slice(i, i + chunk), slice(i + 2, i + chunk + 2)
        inverse_ref[padded] = 1.0 / (d_ref[own] - a_ref[own])

    def product(ref):
        wide = slice(1, planes + 3)
        z = ref[wide] * inverse_ref[wide]
        y_ref[...] = d_ref[...] * z[1:-1] - a_ref[...] * coarse_box(z, matrix)

    product(q_ref)
    solution = jnp.zeros((5, 8, 128), F32)
    for step in range(COARSE):
        upper = lower = jnp.zeros((8, 128), F32)
        for i in starts:
            own, padded = slice(i, i + chunk), slice(i + 2, i + chunk + 2)
            w, q = y_ref[own], q_ref[padded]
            if step > 0:
                old = w_ref[padded]
                w, q = old - alpha * w, q - alpha * old
                q_ref[padded] = q
            w_ref[padded] = w
            upper = upper + jnp.sum(w * q, axis=0)
            lower = lower + jnp.sum(w * w, axis=0)
        alpha = (total(upper) / total(lower))[None]
        if step < COARSE - 1:
            product(w_ref)
        solution = solution + alpha * q_ref[pl.ds(at, 5)]
    return solution * inverse_ref[pl.ds(at, 5)]


def chip_order(ny, nx):
    rows = [0]
    while len(rows) < ny:
        step = ny // (2 * len(rows))
        rows = rows + [r + step for r in rows]
    return [nx * r + x for r in rows for x in range(nx)]


def last_kernel(
    got_ref, mate_ref, matrix_ref, field_ref, middle_ref, fine_ref, iter_ref, out_ref,
    q_ref, a_ref, d_ref, inverse_ref, w_ref, y_ref, middle_rows, fine_rows,
):
    nx = lax.axis_size("x")
    chip = lax.axis_index("y") * nx + lax.axis_index("x")
    core = lax.axis_index("c")
    rank = lax.axis_index("z")
    planes = 2 * got_ref.shape[0]

    got, mate = got_ref[...], mate_ref[...]
    order = chip_order(lax.axis_size("y"), nx)
    place = [order.index(chip) for chip in range(len(order))]
    halves = []
    for half in (jnp.where(core == 0, got, mate), jnp.where(core == 0, mate, got)):
        halves.append(jnp.concatenate([half[i : i + 1] for i in place], axis=0))
        place = [len(order) - 1 - i for i in place]

    def part(half, k):
        return halves[half][:, 8 * k : 8 * k + 8]

    def pairs(first, second):
        return jnp.concatenate([first[:, None], second[:, None]], axis=1).reshape(planes, 8, 128)

    edge = jnp.zeros_like(part(0, 0)[:1])
    q_ref[2 : planes + 2] = pairs(
        part(0, 1) + jnp.concatenate([edge, part(1, 0)[:-1]], axis=0),
        part(1, 1) + jnp.concatenate([part(0, 0)[1:], edge], axis=0),
    )
    a = 0.0625 * pairs(part(0, 2), part(1, 2))
    a_ref[...] = a
    d_ref[...] = 27.0 * a + pairs(part(0, 3), part(1, 3))
    near = solve_coarse(
        q_ref, a_ref, d_ref, inverse_ref, w_ref, y_ref, chip * 2 + core, matrix_ref[...]
    )

    mask = quarter_mask()
    stack = jnp.concatenate([(near[p][None] * mask).reshape(32, 128) for p in range(5)], axis=0)
    spread = ones_where(iota((128, 128), 0) % 32 == (iota((128, 128), 1) % 64) // 2)
    mixed = dot(stack, spread)
    size = (middle_rows.shape[0] - 16) // 5
    edge = jnp.zeros((4, 128), F32)
    window = []
    for p in range(5):
        at = size * p
        middle_rows[at : at + 4] = edge
        middle_rows[at + size - 4 : at + size] = edge
        for k in range(4):
            t = mixed[32 * p + 8 * k : 32 * p + 8 * k + 8]
            for i in (4, 5):
                middle_rows[pl.ds(at + 2 * k + i, 8, stride=8)] = t
        window.append(middle_rows[pl.ds(pl.multiple_of(at + rank * 8, 8), 16)][None])
    v = middle_ref[...] + jnp.concatenate(window, axis=0)
    f, a, s, w = (field_ref[k] for k in range(4))
    for _ in range(2):
        v = v + w * (f - middle_apply(v, a, s))

    lane, out = iota((128, 256), 0), iota((128, 256), 1)
    mixed = dot(v[1:4].reshape(48, 128), ones_where(lane == out // 2))
    halves = [mixed[:16, 128:], mixed[16:32, :128], mixed[16:32, 128:], mixed[32:, :128]]
    refined = []
    for p, t in enumerate(halves):
        for i in range(2):
            fine_rows[pl.ds(24 * p + i, 12, stride=2)] = t[2:14]
        refined += [fine_rows[24 * p : 24 * p + 24][None]] * 2
    refined = jnp.concatenate(refined, axis=0)

    f, a, s, w = (fine_ref[k] for k in range(4))
    u = iter_ref[...] + jnp.where(a > 0.25, refined, 0.0)
    for i in (1, 2):
        j = 8 - i
        u = u[1:-1] + w[i:j] * (f[i:j] - fine_apply(u, a[i:j], s[i:j]))
    out_ref[...] = u[:, 4:20]


def call(kernel, outs, *args, scratch=()):
    return pl.pallas_call(
        kernel,
        out_shape=[
            jax.ShapeDtypeStruct(*(out if isinstance(out[0], tuple) else (out, F32)))
            for out in outs
        ],
        in_specs=[pl.BlockSpec(memory_space=pltpu.VMEM)] * len(args),
        out_specs=[pl.BlockSpec(memory_space=pltpu.VMEM)] * len(outs),
        scratch_shapes=[pltpu.VMEM(shape, F32) for shape in scratch],
        compiler_params=pltpu.CompilerParams(vmem_limit_bytes=24 * 2**20),
    )(*args)


def shards(source, row_scale, shift_field):
    ny, nx, nz = lax.axis_size("y"), lax.axis_size("x"), lax.axis_size("z")
    chips = ny * nx
    first = lax.axis_index("c") == 0

    own = jnp.stack([source, row_scale, shift_field])
    head, tail = call(edge_kernel, [(120, 128), (120, 128)], own)
    up = [(i, i + 1) for i in range(nz - 1)]
    down = [(i + 1, i) for i in range(nz - 1)]
    before = lax.ppermute(tail, "z", up)
    after = lax.ppermute(head, "z", down)
    own, face, mate = call(
        block_kernel, [(3, 4, 40, 128), (344, 128), (336, 128)], own, before, after
    )
    facing = []
    for i in range(chips - 1):
        facing += [(2 * i + 1, 2 * i + 2), (2 * i + 2, 2 * i + 1)]
    swap = [(0, 1), (1, 0)]
    face = lax.ppermute(face, ("y", "x", "c"), facing)
    mate = lax.ppermute(mate, "c", swap)
    fine_iter, fine_fields, sent, one = call(
        fine_kernel,
        [(8, 24, 128), (4, 8, 24, 128), (2 * nz, 8, 128), (3, 16, 128)],
        own, mate, face,
        scratch=[(12 * 40 + 16, 128), (2 * 40 + 16, 128)],
    )

    got = lax.all_to_all(sent, ("c", "z"), 0, 0).reshape(16 * nz, 128)
    size = 4 if chips % 4 == 0 else 1
    sent = pl.pallas_call(
        gather_kernel,
        out_shape=jax.ShapeDtypeStruct((chips, 32, 128), F32),
        in_specs=[pl.BlockSpec(memory_space=pltpu.VMEM)],
        out_specs=pl.BlockSpec(memory_space=pl.ANY),
        scratch_shapes=[
            pltpu.VMEM((16 * nz + 16, 128), F32),
            pltpu.VMEM((size, 32, 128), F32),
            pltpu.SemaphoreType.DMA((chips // size,)),
        ],
        compiler_params=pltpu.CompilerParams(vmem_limit_bytes=24 * 2**20),
    )(got)
    one, sent = lax.optimization_barrier((one, sent))
    evens = [2 * chip for chip in chip_order(ny, nx)]
    odds = [i + 1 for i in reversed(evens)]
    half = lax.all_to_all(
        sent, ("y", "x", "c"), 0, 0, axis_index_groups=[evens, odds]
    )

    mate = lax.ppermute(one, "c", swap)
    pairs = jnp.stack([jnp.where(first, one, mate), jnp.where(first, mate, one)])
    ring = []
    for i in range(chips - 1):
        ring += [(2 * i, 2 * i + 2), (2 * i + 3, 2 * i + 1)]
    outer = lax.ppermute(pairs, ("y", "x", "c"), ring)
    inner = lax.ppermute(one, ("y", "x", "c"), [(j, i) for i, j in ring])
    half, outer, inner = lax.optimization_barrier((half, outer, inner))
    half_mate = lax.ppermute(half, "c", swap)
    fields, middle_iter, matrix = call(
        smooth_kernel,
        [(4, 5, 16, 128), (5, 16, 128), ((384, 256), jnp.bfloat16)],
        one, mate, outer, inner,
    )
    (result,) = call(
        last_kernel, [source.shape],
        half, half_mate, matrix, fields, middle_iter, fine_fields, fine_iter,
        scratch=[(2 * chips + 4, 8, 128)] + [(2 * chips, 8, 128)] * 2
        + [(2 * chips + 4, 8, 128)] * 2 + [(2 * chips, 8, 128)]
        + [(5 * (8 * nz + 8) + 16, 128), (4 * 24 + 16, 128)],
    )
    return result


def solution(mesh):
    ny, nx = (8, 4) if mesh.devices.shape[0] == 64 else (mesh.devices.shape[0] // 2, 1)
    nz = mesh.devices.shape[1]
    split = Mesh(mesh.devices.reshape(ny, nx, 2, nz), ("y", "x", "c", "z"))
    spec = P(("y", "x", "c"), "z", None)
    return jax.shard_map(
        shards, mesh=split, in_specs=(spec, spec, spec), out_specs=spec, check_vma=False
    )
```

```python
import jax
import jax.numpy as jnp
from jax import lax
from jax.experimental import pallas as pl
from jax.experimental.pallas import tpu as pltpu
from jax.sharding import Mesh, PartitionSpec as P

COARSE = 4
DAMPING = 0.8
F32 = jnp.float32


def split(a):
    high = a.astype(jnp.bfloat16)
    rest = a - high.astype(F32)
    middle = rest.astype(jnp.bfloat16)
    low = (rest - middle.astype(F32)).astype(jnp.bfloat16)
    return [high, middle, low]


def dot(a, b):
    parts = lax.dot_general(
        jnp.concatenate(split(a), axis=0),
        b.astype(jnp.bfloat16),
        (((1,), (0,)), ((), ())),
        preferred_element_type=F32,
    )
    n = a.shape[0]
    return parts[:n] + parts[n : 2 * n] + parts[2 * n :]


def iota(shape, dim):
    return lax.broadcasted_iota(jnp.int32, shape, dim)


def ones_where(cond, value=1.0):
    return jnp.where(cond, jnp.float32(value), jnp.float32(0.0))


def lane_box(v, period):
    axis = v.ndim - 1
    lane = iota(v.shape[-2:], 1) % period
    below = jnp.where(lane > 0, pltpu.roll(v, 1, axis), 0.0)
    above = jnp.where(lane < period - 1, pltpu.roll(v, 127, axis), 0.0)
    return v + below + above


def relax_weight(scale, shift, level_scale):
    inside = scale > 0.25
    diag = jnp.where(inside, 26.0 * level_scale * scale + shift, 1.0)
    return jnp.where(inside, DAMPING / diag, 0.0)


def fine_apply(v, scale, shift):
    rows = v.shape[1]
    box = v[:-2] + v[1:-1] + v[2:]
    box = box + pltpu.roll(box, 1, 1) + pltpu.roll(box, rows - 1, 1)
    box = lane_box(box, 128)
    mid = v[1:-1]
    return scale * (27.0 * mid - box) + shift * mid


def pair_planes(quads, rows_ref):
    parts = []
    for k, t in enumerate(quads):
        halves = []
        for i in (0, 2):
            at = 40 * (2 * k + i // 2)
            rows_ref[at : at + 40] = t[i] + t[i + 1]
            halves.append(
                rows_ref[pl.ds(at + 4, 16, stride=2)] + rows_ref[pl.ds(at + 5, 16, stride=2)]
            )
        parts.append(jnp.concatenate(halves, axis=1))
    lane, out = iota((256, 128), 0), iota((256, 128), 1)
    pack = ones_where(lane // 2 == out, 0.125)
    return dot(jnp.concatenate(parts, axis=0), pack).reshape(len(quads), 16, 128)


def edge_kernel(own_ref, first_ref, last_ref):
    for k in range(3):
        for p in range(4):
            at = 10 * (4 * k + p)
            first_ref[at : at + 10] = own_ref[k, p, :10]
            last_ref[at : at + 10] = own_ref[k, p, 6:]


def block_kernel(own_ref, before_ref, after_ref, block_ref, face_ref, mate_ref):
    left = lax.axis_index("c") == 0
    none = jnp.zeros((2, 128), F32)
    for k in range(3):
        for p in range(4):
            at = 10 * (4 * k + p)
            block_ref[k, p, 12:28] = own_ref[k, p]
            block_ref[k, p, 2:12] = before_ref[at : at + 10]
            block_ref[k, p, 28:38] = after_ref[at : at + 10]
            block_ref[k, p, :2] = none
            block_ref[k, p, 38:] = none

    def send(at, k, low, high, rows):
        low, high = block_ref[k, low, rows], block_ref[k, high, rows]
        size = low.shape[0]
        face_ref[at : at + size] = jnp.where(left, low, high)
        mate_ref[at : at + size] = jnp.where(left, high, low)

    for k in range(3):
        for p in range(2):
            send(40 * (2 * k + p), k, p, p + 2, slice(0, 40))
        send(240 + 24 * k, k, 2, 1, slice(8, 32))
    send(312, 1, 3, 0, slice(8, 32))
    face_ref[336:] = jnp.zeros((8, 128), F32)


def fine_kernel(
    own_ref, mate_ref, face_ref, iter_ref, field_ref, piece_ref, one_ref, coef_rows, rows_ref
):
    left = lax.axis_index("c") == 0
    face, mate = face_ref[:336], mate_ref[...]
    low, high = jnp.where(left, face, mate), jnp.where(left, mate, face)
    pad = jnp.zeros((1, 8, 128), F32)
    blocks = []
    for k in range(3):
        sides = []
        for t in (low, high):
            far = [t[240 + 24 * k : 264 + 24 * k], t[312:]]
            if k != 1:
                far[1] = jnp.zeros_like(far[1])
            far = [jnp.concatenate([pad, u[None], pad], axis=1) for u in far]
            sides.append([t[80 * k : 80 * k + 80].reshape(2, 40, 128)] + far)
        blocks.append(jnp.concatenate(sides[0][::-1] + [own_ref[k]] + sides[1], axis=0))
    f, a, s = blocks
    coefs = pair_planes([t[4 * p : 4 * p + 4] for t in (a, s) for p in range(3)], coef_rows)
    w = relax_weight(a[1:11], s[1:11], 1.0)
    u = w * f[1:11]
    u = u[1:-1] + w[1:-1] * (f[2:10] - fine_apply(u, a[2:10], s[2:10]))
    iter_ref[...] = u[:, 8:32]
    for k, t in enumerate((f[2:10], a[2:10], s[2:10], w[1:9])):
        field_ref[k] = t[:, 8:32]
    resid = f[4:8] - fine_apply(u[1:7], a[4:8], s[4:8])
    f = pair_planes([resid], rows_ref)
    a, s = coefs[:3], coefs[3:]
    for k, t in enumerate((f[0], a[1], s[1])):
        one_ref[k] = t

    none = jnp.zeros_like(f)
    f = jnp.concatenate([none, f, none], axis=0)
    w = relax_weight(a, s, 0.25)
    v = w * f
    v = v + w * (f - middle_apply(v, a, s))
    resid = f - middle_apply(v, a, s)
    spread = ones_where(iota((128, 128), 1) % 32 == (iota((128, 128), 0) % 64) // 2, 0.125)
    own = ones_where(iota((16, 128), 0) // 2 == iota((16, 128), 1) // 32 + 2)
    mixed = dot(resid.reshape(48, 128), spread).reshape(3, 16, 128)
    rows = [mixed[k] * own for k in range(3)]
    mixed = dot(jnp.concatenate([a[1], s[1]], axis=0), spread).reshape(2, 16, 128)
    rows += [mixed[k] * own for k in range(2)] + [jnp.zeros((1, 128), F32)] * 3
    piece = jnp.concatenate([jnp.sum(t, axis=0, keepdims=True) for t in rows], axis=0)
    piece_ref[...] = jnp.broadcast_to(piece[None], piece_ref.shape)


def middle_apply(v, scale, shift):
    rows = v.shape[1]
    lane = iota((rows, 128), 1)
    row = iota((rows, 128), 0)
    swap = pltpu.roll(v, 64, 2)
    edge = jnp.zeros_like(swap[:1])
    prev = jnp.concatenate([edge, swap[:-1]], axis=0)
    later = jnp.concatenate([swap[1:], edge], axis=0)
    box = v + swap + jnp.where(lane < 64, prev, later)
    box = (
        box
        + jnp.where(row > 0, pltpu.roll(box, 1, 1), 0.0)
        + jnp.where(row < rows - 1, pltpu.roll(box, rows - 1, 1), 0.0)
    )
    box = lane_box(box, 64)
    return 0.25 * scale * (27.0 * v - box) + shift * v


def quarter_row(shape, dim):
    i = iota(shape, dim)
    return 4 * (i % 8) + i // 8


def quarter_mask():
    return ones_where(iota((4, 8, 128), 2) // 32 == iota((4, 8, 128), 0))


def gather_kernel(got_ref, piece_ref, rows_ref, block_ref, sems):
    core = lax.axis_index("c")
    half = got_ref.shape[0] // 2
    rows_ref[: 2 * half] = got_ref[...]

    def column(at, k):
        return rows_ref[pl.ds(at * half + k, half // 8, stride=8)]

    outward = 2 * core
    piece = jnp.concatenate(
        [
            column(core, outward),
            column(core, 1) + column(1 - core, outward),
            column(core, 3),
            column(core, 4),
        ],
        axis=0,
    )
    block_ref[...] = jnp.broadcast_to(piece[None], block_ref.shape)
    size = block_ref.shape[0]
    copies = [
        pltpu.make_async_copy(block_ref, piece_ref.at[pl.ds(size * k, size)], sems.at[k])
        for k in range(piece_ref.shape[0] // size)
    ]
    for copy in copies:
        copy.start()
    for copy in copies:
        copy.wait()


def smooth_kernel(
    own_ref, mate_ref, outer_ref, inner_ref, field_ref, iter_ref, matrix_ref, spread_ref, fine_ref
):
    left = lax.axis_index("c") == 0
    for k in range(3):
        mate, outer, inner = mate_ref[k], outer_ref[:, k], inner_ref[k]
        field_ref[k, 0] = jnp.where(left, outer[0], inner)
        field_ref[k, 1] = jnp.where(left, outer[1], mate)
        field_ref[k, 2] = own_ref[k]
        field_ref[k, 3] = jnp.where(left, mate, outer[0])
        field_ref[k, 4] = jnp.where(left, inner, outer[1])
    f, a, s = (field_ref[k] for k in range(3))
    w = relax_weight(a, s, 0.25)
    field_ref[3] = w
    v = w * f
    iter_ref[...] = v + w * (f - middle_apply(v, a, s))
    matrix_ref[...] = box_matrix()
    lane, out = iota((128, 128), 0), iota((128, 128), 1)
    spread_ref[...] = ones_where(lane % 32 == (out % 64) // 2).astype(jnp.bfloat16)
    lane, out = iota((128, 256), 0), iota((128, 256), 1)
    fine_ref[...] = ones_where(lane == out // 2).astype(jnp.bfloat16)


def box_matrix():
    lane, out = iota((384, 256), 0) % 128, iota((384, 256), 1)
    group, to = lane // 32, out % 128 // 32
    near = jnp.abs(lane % 32 - out % 32) <= 1
    same = (out < 128) & (jnp.abs(group - to) <= 1)
    wrap = (out >= 128) & (jnp.abs(group - to) == 3)
    return ones_where(near & (same | wrap)).astype(jnp.bfloat16)


def coarse_box(v, matrix):
    rows = (v[:-2] + v[1:-1] + v[2:]).reshape(-1, 128)
    both = lax.dot_general(
        jnp.concatenate(split(rows), axis=1),
        matrix,
        (((1,), (0,)), ((), ())),
        preferred_element_type=F32,
    )
    box, wrap = (both[:, k : k + 128].reshape(-1, 8, 128) for k in (0, 128))
    lane, row = iota((8, 128), 1), iota((8, 128), 0)
    up = jnp.where((lane < 32) & (row > 0), pltpu.roll(wrap, 1, 1), 0.0)
    down = jnp.where((lane >= 96) & (row < 7), pltpu.roll(wrap, 7, 1), 0.0)
    return box + up + down


def total(plane):
    return jnp.sum(jnp.sum(plane, axis=0, keepdims=True), axis=1, keepdims=True)


def solve_coarse(q_ref, a_ref, d_ref, inverse_ref, w_ref, y_ref, at, matrix):
    planes = a_ref.shape[0]
    chunk = 16 if planes % 16 == 0 else 2
    starts = range(0, planes, chunk)
    none = jnp.zeros((2, 8, 128), F32)
    for ref in (q_ref, inverse_ref, w_ref):
        ref[:2] = none
        ref[planes + 2 :] = none
    for i in starts:
        own, padded = slice(i, i + chunk), slice(i + 2, i + chunk + 2)
        inverse_ref[padded] = 1.0 / (d_ref[own] - a_ref[own])

    span = 8 if planes % 8 == 0 else 2

    def product(ref):
        for i in range(0, planes, span):
            own, wide = slice(i, i + span), slice(i + 1, i + span + 3)
            z = ref[wide] * inverse_ref[wide]
            y_ref[own] = d_ref[own] * z[1:-1] - a_ref[own] * coarse_box(z, matrix)

    product(q_ref)
    solution = jnp.zeros((5, 8, 128), F32)
    for step in range(COARSE):
        upper = lower = jnp.zeros((8, 128), F32)
        for i in starts:
            own, padded = slice(i, i + chunk), slice(i + 2, i + chunk + 2)
            w, q = y_ref[own], q_ref[padded]
            if step > 0:
                old = w_ref[padded]
                w, q = old - alpha * w, q - alpha * old
                q_ref[padded] = q
            w_ref[padded] = w
            upper = upper + jnp.sum(w * q, axis=0)
            lower = lower + jnp.sum(w * w, axis=0)
        alpha = (total(upper) / total(lower))[None]
        if step < COARSE - 1:
            product(w_ref)
        solution = solution + alpha * q_ref[pl.ds(at, 5)]
    return solution * inverse_ref[pl.ds(at, 5)]


def chip_order(ny, nx):
    rows = [0]
    while len(rows) < ny:
        step = ny // (2 * len(rows))
        rows = rows + [r + step for r in rows]
    return [nx * r + x for r in rows for x in range(nx)]


def last_kernel(
    got_ref, mate_ref, matrix_ref, spread_ref, double_ref, field_ref, middle_ref, fine_ref, iter_ref, out_ref,
    q_ref, a_ref, d_ref, inverse_ref, w_ref, y_ref, middle_rows, fine_rows,
):
    nx = lax.axis_size("x")
    chip = lax.axis_index("y") * nx + lax.axis_index("x")
    core = lax.axis_index("c")
    rank = lax.axis_index("z")
    planes = 2 * got_ref.shape[0]

    got, mate = got_ref[...], mate_ref[...]
    order = chip_order(lax.axis_size("y"), nx)
    place = [order.index(chip) for chip in range(len(order))]
    halves = []
    for half in (jnp.where(core == 0, got, mate), jnp.where(core == 0, mate, got)):
        halves.append(jnp.concatenate([half[i : i + 1] for i in place], axis=0))
        place = [len(order) - 1 - i for i in place]

    def part(half, k):
        return halves[half][:, 8 * k : 8 * k + 8]

    def pairs(first, second):
        return jnp.concatenate([first[:, None], second[:, None]], axis=1).reshape(planes, 8, 128)

    edge = jnp.zeros_like(part(0, 0)[:1])
    q_ref[2 : planes + 2] = pairs(
        part(0, 1) + jnp.concatenate([edge, part(1, 0)[:-1]], axis=0),
        part(1, 1) + jnp.concatenate([part(0, 0)[1:], edge], axis=0),
    )
    a = 0.0625 * pairs(part(0, 2), part(1, 2))
    a_ref[...] = a
    d_ref[...] = 27.0 * a + pairs(part(0, 3), part(1, 3))
    near = solve_coarse(
        q_ref, a_ref, d_ref, inverse_ref, w_ref, y_ref, chip * 2 + core, matrix_ref[...]
    )

    mask = quarter_mask()
    stack = jnp.concatenate([(near[p][None] * mask).reshape(32, 128) for p in range(5)], axis=0)
    mixed = dot(stack, spread_ref[...])
    size = (middle_rows.shape[0] - 16) // 5
    edge = jnp.zeros((4, 128), F32)
    window = []
    for p in range(5):
        at = size * p
        middle_rows[at : at + 4] = edge
        middle_rows[at + size - 4 : at + size] = edge
        for k in range(4):
            t = mixed[32 * p + 8 * k : 32 * p + 8 * k + 8]
            for i in (4, 5):
                middle_rows[pl.ds(at + 2 * k + i, 8, stride=8)] = t
        window.append(middle_rows[pl.ds(pl.multiple_of(at + rank * 8, 8), 16)][None])
    v = middle_ref[...] + jnp.concatenate(window, axis=0)
    f, a, s, w = (field_ref[k] for k in range(4))
    for _ in range(2):
        v = v + w * (f - middle_apply(v, a, s))

    mixed = dot(v[1:4].reshape(48, 128), double_ref[...])
    halves = [mixed[:16, 128:], mixed[16:32, :128], mixed[16:32, 128:], mixed[32:, :128]]
    refined = []
    for p, t in enumerate(halves):
        for i in range(2):
            fine_rows[pl.ds(24 * p + i, 12, stride=2)] = t[2:14]
        refined += [fine_rows[24 * p : 24 * p + 24][None]] * 2
    refined = jnp.concatenate(refined, axis=0)

    f, a, s, w = (fine_ref[k] for k in range(4))
    u = iter_ref[...] + jnp.where(a > 0.25, refined, 0.0)
    for i in (1, 2):
        j = 8 - i
        u = u[1:-1] + w[i:j] * (f[i:j] - fine_apply(u, a[i:j], s[i:j]))
    out_ref[...] = u[:, 4:20]


def call(kernel, outs, *args, scratch=()):
    return pl.pallas_call(
        kernel,
        out_shape=[
            jax.ShapeDtypeStruct(*(out if isinstance(out[0], tuple) else (out, F32)))
            for out in outs
        ],
        in_specs=[pl.BlockSpec(memory_space=pltpu.VMEM)] * len(args),
        out_specs=[pl.BlockSpec(memory_space=pltpu.VMEM)] * len(outs),
        scratch_shapes=[pltpu.VMEM(shape, F32) for shape in scratch],
        compiler_params=pltpu.CompilerParams(vmem_limit_bytes=24 * 2**20),
    )(*args)


def shards(source, row_scale, shift_field):
    ny, nx, nz = lax.axis_size("y"), lax.axis_size("x"), lax.axis_size("z")
    chips = ny * nx
    first = lax.axis_index("c") == 0

    own = jnp.stack([source, row_scale, shift_field])
    head, tail = call(edge_kernel, [(120, 128), (120, 128)], own)
    up = [(i, i + 1) for i in range(nz - 1)]
    down = [(i + 1, i) for i in range(nz - 1)]
    before = lax.ppermute(tail, "z", up)
    after = lax.ppermute(head, "z", down)
    own, face, mate = call(
        block_kernel, [(3, 4, 40, 128), (344, 128), (336, 128)], own, before, after
    )
    facing = []
    for i in range(chips - 1):
        facing += [(2 * i + 1, 2 * i + 2), (2 * i + 2, 2 * i + 1)]
    swap = [(0, 1), (1, 0)]
    face = lax.ppermute(face, ("y", "x", "c"), facing)
    mate = lax.ppermute(mate, "c", swap)
    fine_iter, fine_fields, sent, one = call(
        fine_kernel,
        [(8, 24, 128), (4, 8, 24, 128), (2 * nz, 8, 128), (3, 16, 128)],
        own, mate, face,
        scratch=[(12 * 40 + 16, 128), (2 * 40 + 16, 128)],
    )

    got = lax.all_to_all(sent, ("c", "z"), 0, 0).reshape(16 * nz, 128)
    size = 4 if chips % 4 == 0 else 1
    sent = pl.pallas_call(
        gather_kernel,
        out_shape=jax.ShapeDtypeStruct((chips, 32, 128), F32),
        in_specs=[pl.BlockSpec(memory_space=pltpu.VMEM)],
        out_specs=pl.BlockSpec(memory_space=pl.ANY),
        scratch_shapes=[
            pltpu.VMEM((16 * nz + 16, 128), F32),
            pltpu.VMEM((size, 32, 128), F32),
            pltpu.SemaphoreType.DMA((chips // size,)),
        ],
        compiler_params=pltpu.CompilerParams(vmem_limit_bytes=24 * 2**20),
    )(got)
    one, sent = lax.optimization_barrier((one, sent))
    evens = [2 * chip for chip in chip_order(ny, nx)]
    odds = [i + 1 for i in reversed(evens)]
    half = lax.all_to_all(
        sent, ("y", "x", "c"), 0, 0, axis_index_groups=[evens, odds]
    )

    mate = lax.ppermute(one, "c", swap)
    pairs = jnp.stack([jnp.where(first, one, mate), jnp.where(first, mate, one)])
    ring = []
    for i in range(chips - 1):
        ring += [(2 * i, 2 * i + 2), (2 * i + 3, 2 * i + 1)]
    outer = lax.ppermute(pairs, ("y", "x", "c"), ring)
    inner = lax.ppermute(one, ("y", "x", "c"), [(j, i) for i, j in ring])
    half, outer, inner = lax.optimization_barrier((half, outer, inner))
    half_mate = lax.ppermute(half, "c", swap)
    fields, middle_iter, *matrices = call(
        smooth_kernel,
        [(4, 5, 16, 128), (5, 16, 128)]
        + [(shape, jnp.bfloat16) for shape in ((384, 256), (128, 128), (128, 256))],
        one, mate, outer, inner,
    )
    (result,) = call(
        last_kernel, [source.shape],
        half, half_mate, *matrices, fields, middle_iter, fine_fields, fine_iter,
        scratch=[(2 * chips + 4, 8, 128)] + [(2 * chips, 8, 128)] * 2
        + [(2 * chips + 4, 8, 128)] * 2 + [(2 * chips, 8, 128)]
        + [(5 * (8 * nz + 8) + 16, 128), (4 * 24 + 16, 128)],
    )
    return result


def solution(mesh):
    ny, nx = (8, 4) if mesh.devices.shape[0] == 64 else (mesh.devices.shape[0] // 2, 1)
    nz = mesh.devices.shape[1]
    split = Mesh(mesh.devices.reshape(ny, nx, 2, nz), ("y", "x", "c", "z"))
    spec = P(("y", "x", "c"), "z", None)
    return jax.shard_map(
        shards, mesh=split, in_specs=(spec, spec, spec), out_specs=spec, check_vma=False
    )
```

```python
import jax
import jax.numpy as jnp
from jax import lax
from jax.experimental import pallas as pl
from jax.experimental.pallas import tpu as pltpu
from jax.sharding import Mesh, PartitionSpec as P

COARSE = 4
DAMPING = 0.8
F32 = jnp.float32


def split(a):
    high = a.astype(jnp.bfloat16)
    rest = a - high.astype(F32)
    middle = rest.astype(jnp.bfloat16)
    low = (rest - middle.astype(F32)).astype(jnp.bfloat16)
    return [high, middle, low]


def dot(a, b):
    parts = lax.dot_general(
        jnp.concatenate(split(a), axis=0),
        b.astype(jnp.bfloat16),
        (((1,), (0,)), ((), ())),
        preferred_element_type=F32,
    )
    n = a.shape[0]
    return parts[:n] + parts[n : 2 * n] + parts[2 * n :]


def iota(shape, dim):
    return lax.broadcasted_iota(jnp.int32, shape, dim)


def ones_where(cond, value=1.0):
    return jnp.where(cond, jnp.float32(value), jnp.float32(0.0))


def lane_box(v, period):
    axis = v.ndim - 1
    lane = iota(v.shape[-2:], 1) % period
    below = jnp.where(lane > 0, pltpu.roll(v, 1, axis), 0.0)
    above = jnp.where(lane < period - 1, pltpu.roll(v, 127, axis), 0.0)
    return v + below + above


def relax_weight(scale, shift, level_scale):
    inside = scale > 0.25
    diag = jnp.where(inside, 26.0 * level_scale * scale + shift, 1.0)
    return jnp.where(inside, DAMPING / diag, 0.0)


def fine_apply(v, scale, shift):
    rows = v.shape[1]
    box = v[:-2] + v[1:-1] + v[2:]
    box = box + pltpu.roll(box, 1, 1) + pltpu.roll(box, rows - 1, 1)
    box = lane_box(box, 128)
    mid = v[1:-1]
    return scale * (27.0 * mid - box) + shift * mid


def pair_planes(quads, rows_ref):
    parts = []
    for k, t in enumerate(quads):
        halves = []
        for i in (0, 2):
            at = 40 * (2 * k + i // 2)
            rows_ref[at : at + 40] = t[i] + t[i + 1]
            halves.append(
                rows_ref[pl.ds(at + 4, 16, stride=2)] + rows_ref[pl.ds(at + 5, 16, stride=2)]
            )
        parts.append(jnp.concatenate(halves, axis=1))
    lane, out = iota((256, 128), 0), iota((256, 128), 1)
    pack = ones_where(lane // 2 == out, 0.125)
    return dot(jnp.concatenate(parts, axis=0), pack).reshape(len(quads), 16, 128)


def edge_kernel(own_ref, first_ref, last_ref):
    for k in range(3):
        for p in range(4):
            at = 10 * (4 * k + p)
            first_ref[at : at + 10] = own_ref[k, p, :10]
            last_ref[at : at + 10] = own_ref[k, p, 6:]


def block_kernel(own_ref, before_ref, after_ref, block_ref, face_ref, mate_ref):
    left = lax.axis_index("c") == 0
    none = jnp.zeros((2, 128), F32)
    for k in range(3):
        for p in range(4):
            at = 10 * (4 * k + p)
            block_ref[k, p, 12:28] = own_ref[k, p]
            block_ref[k, p, 2:12] = before_ref[at : at + 10]
            block_ref[k, p, 28:38] = after_ref[at : at + 10]
            block_ref[k, p, :2] = none
            block_ref[k, p, 38:] = none

    def send(at, k, low, high, rows):
        low, high = block_ref[k, low, rows], block_ref[k, high, rows]
        size = low.shape[0]
        face_ref[at : at + size] = jnp.where(left, low, high)
        mate_ref[at : at + size] = jnp.where(left, high, low)

    for k in range(3):
        for p in range(2):
            send(40 * (2 * k + p), k, p, p + 2, slice(0, 40))
        send(240 + 24 * k, k, 2, 1, slice(8, 32))
    send(312, 1, 3, 0, slice(8, 32))
    face_ref[336:] = jnp.zeros((8, 128), F32)


def fine_kernel(
    own_ref, mate_ref, face_ref, iter_ref, field_ref, piece_ref, one_ref, coef_rows, rows_ref
):
    left = lax.axis_index("c") == 0
    face, mate = face_ref[:336], mate_ref[...]
    low, high = jnp.where(left, face, mate), jnp.where(left, mate, face)
    pad = jnp.zeros((1, 8, 128), F32)
    blocks = []
    for k in range(3):
        sides = []
        for t in (low, high):
            far = [t[240 + 24 * k : 264 + 24 * k], t[312:]]
            if k != 1:
                far[1] = jnp.zeros_like(far[1])
            far = [jnp.concatenate([pad, u[None], pad], axis=1) for u in far]
            sides.append([t[80 * k : 80 * k + 80].reshape(2, 40, 128)] + far)
        blocks.append(jnp.concatenate(sides[0][::-1] + [own_ref[k]] + sides[1], axis=0))
    f, a, s = blocks
    coefs = pair_planes([t[4 * p : 4 * p + 4] for t in (a, s) for p in range(3)], coef_rows)
    w = relax_weight(a[1:11], s[1:11], 1.0)
    u = w * f[1:11]
    u = u[1:-1] + w[1:-1] * (f[2:10] - fine_apply(u, a[2:10], s[2:10]))
    iter_ref[...] = u[:, 8:32]
    for k, t in enumerate((f[2:10], a[2:10], s[2:10], w[1:9])):
        field_ref[k] = t[:, 8:32]
    resid = f[4:8] - fine_apply(u[1:7], a[4:8], s[4:8])
    f = pair_planes([resid], rows_ref)
    a, s = coefs[:3], coefs[3:]
    for k, t in enumerate((f[0], a[1], s[1])):
        one_ref[k] = t

    none = jnp.zeros_like(f)
    f = jnp.concatenate([none, f, none], axis=0)
    w = relax_weight(a, s, 0.25)
    v = w * f
    v = v + w * (f - middle_apply(v, a, s))
    resid = f - middle_apply(v, a, s)
    spread = ones_where(iota((128, 128), 1) % 32 == (iota((128, 128), 0) % 64) // 2, 0.125)
    own = ones_where(iota((16, 128), 0) // 2 == iota((16, 128), 1) // 32 + 2)
    mixed = dot(resid.reshape(48, 128), spread).reshape(3, 16, 128)
    rows = [mixed[k] * own for k in range(3)]
    mixed = dot(jnp.concatenate([a[1], s[1]], axis=0), spread).reshape(2, 16, 128)
    rows += [mixed[k] * own for k in range(2)] + [jnp.zeros((1, 128), F32)] * 3
    piece = jnp.concatenate([jnp.sum(t, axis=0, keepdims=True) for t in rows], axis=0)
    piece_ref[...] = jnp.broadcast_to(piece[None], piece_ref.shape)


def middle_apply(v, scale, shift):
    rows = v.shape[1]
    lane = iota((rows, 128), 1)
    row = iota((rows, 128), 0)
    swap = pltpu.roll(v, 64, 2)
    edge = jnp.zeros_like(swap[:1])
    prev = jnp.concatenate([edge, swap[:-1]], axis=0)
    later = jnp.concatenate([swap[1:], edge], axis=0)
    box = v + swap + jnp.where(lane < 64, prev, later)
    box = (
        box
        + jnp.where(row > 0, pltpu.roll(box, 1, 1), 0.0)
        + jnp.where(row < rows - 1, pltpu.roll(box, rows - 1, 1), 0.0)
    )
    box = lane_box(box, 64)
    return 0.25 * scale * (27.0 * v - box) + shift * v


def quarter_row(shape, dim):
    i = iota(shape, dim)
    return 4 * (i % 8) + i // 8


def quarter_mask():
    return ones_where(iota((4, 8, 128), 2) // 32 == iota((4, 8, 128), 0))


def gather_kernel(got_ref, piece_ref, rows_ref, block_ref, sems):
    core = lax.axis_index("c")
    half = got_ref.shape[0] // 2
    rows_ref[: 2 * half] = got_ref[...]

    def column(at, k):
        return rows_ref[pl.ds(at * half + k, half // 8, stride=8)]

    outward = 2 * core
    piece = jnp.concatenate(
        [
            column(core, outward),
            column(core, 1) + column(1 - core, outward),
            column(core, 3),
            column(core, 4),
        ],
        axis=0,
    )
    block_ref[...] = jnp.broadcast_to(piece[None], block_ref.shape)
    size = block_ref.shape[0]
    copies = [
        pltpu.make_async_copy(block_ref, piece_ref.at[pl.ds(size * k, size)], sems.at[k])
        for k in range(piece_ref.shape[0] // size)
    ]
    for copy in copies:
        copy.start()
    for copy in copies:
        copy.wait()


def smooth_kernel(
    own_ref, mate_ref, outer_ref, inner_ref, field_ref, iter_ref, matrix_ref, spread_ref, fine_ref
):
    left = lax.axis_index("c") == 0
    for k in range(3):
        mate, outer, inner = mate_ref[k], outer_ref[:, k], inner_ref[k]
        field_ref[k, 0] = jnp.where(left, outer[0], inner)
        field_ref[k, 1] = jnp.where(left, outer[1], mate)
        field_ref[k, 2] = own_ref[k]
        field_ref[k, 3] = jnp.where(left, mate, outer[0])
        field_ref[k, 4] = jnp.where(left, inner, outer[1])
    f, a, s = (field_ref[k] for k in range(3))
    w = relax_weight(a, s, 0.25)
    field_ref[3] = w
    v = w * f
    iter_ref[...] = v + w * (f - middle_apply(v, a, s))
    matrix_ref[...] = box_matrix()
    lane, out = iota((128, 128), 0), iota((128, 128), 1)
    spread_ref[...] = ones_where(lane % 32 == (out % 64) // 2).astype(jnp.bfloat16)
    lane, out = iota((128, 256), 0), iota((128, 256), 1)
    fine_ref[...] = ones_where(lane == out // 2).astype(jnp.bfloat16)


def box_matrix():
    lane, out = iota((384, 256), 0) % 128, iota((384, 256), 1)
    group, to = lane // 32, out % 128 // 32
    near = jnp.abs(lane % 32 - out % 32) <= 1
    same = (out < 128) & (jnp.abs(group - to) <= 1)
    wrap = (out >= 128) & (jnp.abs(group - to) == 3)
    return ones_where(near & (same | wrap)).astype(jnp.bfloat16)


def coarse_box(v, matrix):
    rows = (v[:-2] + v[1:-1] + v[2:]).reshape(-1, 128)
    both = lax.dot_general(
        jnp.concatenate(split(rows), axis=1),
        matrix,
        (((1,), (0,)), ((), ())),
        preferred_element_type=F32,
    )
    box, wrap = (both[:, k : k + 128].reshape(-1, 8, 128) for k in (0, 128))
    lane, row = iota((8, 128), 1), iota((8, 128), 0)
    up = jnp.where((lane < 32) & (row > 0), pltpu.roll(wrap, 1, 1), 0.0)
    down = jnp.where((lane >= 96) & (row < 7), pltpu.roll(wrap, 7, 1), 0.0)
    return box + up + down


def total(plane):
    return jnp.sum(jnp.sum(plane, axis=0, keepdims=True), axis=1, keepdims=True)


def solve_coarse(q_ref, a_ref, d_ref, inverse_ref, w_ref, y_ref, at, matrix):
    planes = a_ref.shape[0]
    chunk = 16 if planes % 16 == 0 else 2
    starts = range(0, planes, chunk)
    none = jnp.zeros((2, 8, 128), F32)
    for ref in (q_ref, inverse_ref, w_ref):
        ref[:2] = none
        ref[planes + 2 :] = none
    for i in starts:
        own, padded = slice(i, i + chunk), slice(i + 2, i + chunk + 2)
        inverse_ref[padded] = 1.0 / (d_ref[own] - a_ref[own])

    span = 16 if planes % 16 == 0 else 2

    def product(ref):
        for i in range(0, planes, span):
            own, wide = slice(i, i + span), slice(i + 1, i + span + 3)
            z = ref[wide] * inverse_ref[wide]
            y_ref[own] = d_ref[own] * z[1:-1] - a_ref[own] * coarse_box(z, matrix)

    product(q_ref)
    solution = jnp.zeros((5, 8, 128), F32)
    for step in range(COARSE):
        upper = lower = jnp.zeros((8, 128), F32)
        for i in starts:
            own, padded = slice(i, i + chunk), slice(i + 2, i + chunk + 2)
            w, q = y_ref[own], q_ref[padded]
            if step > 0:
                old = w_ref[padded]
                w, q = old - alpha * w, q - alpha * old
                q_ref[padded] = q
            w_ref[padded] = w
            upper = upper + jnp.sum(w * q, axis=0)
            lower = lower + jnp.sum(w * w, axis=0)
        alpha = (total(upper) / total(lower))[None]
        if step < COARSE - 1:
            product(w_ref)
        solution = solution + alpha * q_ref[pl.ds(at, 5)]
    return solution * inverse_ref[pl.ds(at, 5)]


def chip_order(ny, nx):
    rows = [0]
    while len(rows) < ny:
        step = ny // (2 * len(rows))
        rows = rows + [r + step for r in rows]
    return [nx * r + x for r in rows for x in range(nx)]


def last_kernel(
    got_ref, mate_ref, matrix_ref, spread_ref, double_ref, field_ref, middle_ref, fine_ref, iter_ref, out_ref,
    q_ref, a_ref, d_ref, inverse_ref, w_ref, y_ref, middle_rows, fine_rows,
):
    nx = lax.axis_size("x")
    chip = lax.axis_index("y") * nx + lax.axis_index("x")
    core = lax.axis_index("c")
    rank = lax.axis_index("z")
    planes = 2 * got_ref.shape[0]

    got, mate = got_ref[...], mate_ref[...]
    order = chip_order(lax.axis_size("y"), nx)
    place = [order.index(chip) for chip in range(len(order))]
    halves = []
    for half in (jnp.where(core == 0, got, mate), jnp.where(core == 0, mate, got)):
        halves.append(jnp.concatenate([half[i : i + 1] for i in place], axis=0))
        place = [len(order) - 1 - i for i in place]

    def part(half, k):
        return halves[half][:, 8 * k : 8 * k + 8]

    def pairs(first, second):
        return jnp.concatenate([first[:, None], second[:, None]], axis=1).reshape(planes, 8, 128)

    edge = jnp.zeros_like(part(0, 0)[:1])
    q_ref[2 : planes + 2] = pairs(
        part(0, 1) + jnp.concatenate([edge, part(1, 0)[:-1]], axis=0),
        part(1, 1) + jnp.concatenate([part(0, 0)[1:], edge], axis=0),
    )
    a = 0.0625 * pairs(part(0, 2), part(1, 2))
    a_ref[...] = a
    d_ref[...] = 27.0 * a + pairs(part(0, 3), part(1, 3))
    near = solve_coarse(
        q_ref, a_ref, d_ref, inverse_ref, w_ref, y_ref, chip * 2 + core, matrix_ref[...]
    )

    mask = quarter_mask()
    stack = jnp.concatenate([(near[p][None] * mask).reshape(32, 128) for p in range(5)], axis=0)
    mixed = dot(stack, spread_ref[...])
    size = (middle_rows.shape[0] - 16) // 5
    edge = jnp.zeros((4, 128), F32)
    window = []
    for p in range(5):
        at = size * p
        middle_rows[at : at + 4] = edge
        middle_rows[at + size - 4 : at + size] = edge
        for k in range(4):
            t = mixed[32 * p + 8 * k : 32 * p + 8 * k + 8]
            for i in (4, 5):
                middle_rows[pl.ds(at + 2 * k + i, 8, stride=8)] = t
        window.append(middle_rows[pl.ds(pl.multiple_of(at + rank * 8, 8), 16)][None])
    v = middle_ref[...] + jnp.concatenate(window, axis=0)
    f, a, s, w = (field_ref[k] for k in range(4))
    for _ in range(2):
        v = v + w * (f - middle_apply(v, a, s))

    mixed = dot(v[1:4].reshape(48, 128), double_ref[...])
    halves = [mixed[:16, 128:], mixed[16:32, :128], mixed[16:32, 128:], mixed[32:, :128]]
    refined = []
    for p, t in enumerate(halves):
        for i in range(2):
            fine_rows[pl.ds(24 * p + i, 12, stride=2)] = t[2:14]
        refined += [fine_rows[24 * p : 24 * p + 24][None]] * 2
    refined = jnp.concatenate(refined, axis=0)

    f, a, s, w = (fine_ref[k] for k in range(4))
    u = iter_ref[...] + jnp.where(a > 0.25, refined, 0.0)
    for i in (1, 2):
        j = 8 - i
        u = u[1:-1] + w[i:j] * (f[i:j] - fine_apply(u, a[i:j], s[i:j]))
    out_ref[...] = u[:, 4:20]


def call(kernel, outs, *args, scratch=()):
    return pl.pallas_call(
        kernel,
        out_shape=[
            jax.ShapeDtypeStruct(*(out if isinstance(out[0], tuple) else (out, F32)))
            for out in outs
        ],
        in_specs=[pl.BlockSpec(memory_space=pltpu.VMEM)] * len(args),
        out_specs=[pl.BlockSpec(memory_space=pltpu.VMEM)] * len(outs),
        scratch_shapes=[pltpu.VMEM(shape, F32) for shape in scratch],
        compiler_params=pltpu.CompilerParams(vmem_limit_bytes=24 * 2**20),
    )(*args)


def shards(source, row_scale, shift_field):
    ny, nx, nz = lax.axis_size("y"), lax.axis_size("x"), lax.axis_size("z")
    chips = ny * nx
    first = lax.axis_index("c") == 0

    own = jnp.stack([source, row_scale, shift_field])
    head, tail = call(edge_kernel, [(120, 128), (120, 128)], own)
    up = [(i, i + 1) for i in range(nz - 1)]
    down = [(i + 1, i) for i in range(nz - 1)]
    before = lax.ppermute(tail, "z", up)
    after = lax.ppermute(head, "z", down)
    own, face, mate = call(
        block_kernel, [(3, 4, 40, 128), (344, 128), (336, 128)], own, before, after
    )
    facing = []
    for i in range(chips - 1):
        facing += [(2 * i + 1, 2 * i + 2), (2 * i + 2, 2 * i + 1)]
    swap = [(0, 1), (1, 0)]
    face = lax.ppermute(face, ("y", "x", "c"), facing)
    mate = lax.ppermute(mate, "c", swap)
    fine_iter, fine_fields, sent, one = call(
        fine_kernel,
        [(8, 24, 128), (4, 8, 24, 128), (2 * nz, 8, 128), (3, 16, 128)],
        own, mate, face,
        scratch=[(12 * 40 + 16, 128), (2 * 40 + 16, 128)],
    )

    got = lax.all_to_all(sent, ("c", "z"), 0, 0).reshape(16 * nz, 128)
    size = 4 if chips % 4 == 0 else 1
    sent = pl.pallas_call(
        gather_kernel,
        out_shape=jax.ShapeDtypeStruct((chips, 32, 128), F32),
        in_specs=[pl.BlockSpec(memory_space=pltpu.VMEM)],
        out_specs=pl.BlockSpec(memory_space=pl.ANY),
        scratch_shapes=[
            pltpu.VMEM((16 * nz + 16, 128), F32),
            pltpu.VMEM((size, 32, 128), F32),
            pltpu.SemaphoreType.DMA((chips // size,)),
        ],
        compiler_params=pltpu.CompilerParams(vmem_limit_bytes=24 * 2**20),
    )(got)
    one, sent = lax.optimization_barrier((one, sent))
    evens = [2 * chip for chip in chip_order(ny, nx)]
    odds = [i + 1 for i in reversed(evens)]
    half = lax.all_to_all(
        sent, ("y", "x", "c"), 0, 0, axis_index_groups=[evens, odds]
    )

    mate = lax.ppermute(one, "c", swap)
    pairs = jnp.stack([jnp.where(first, one, mate), jnp.where(first, mate, one)])
    ring = []
    for i in range(chips - 1):
        ring += [(2 * i, 2 * i + 2), (2 * i + 3, 2 * i + 1)]
    outer = lax.ppermute(pairs, ("y", "x", "c"), ring)
    inner = lax.ppermute(one, ("y", "x", "c"), [(j, i) for i, j in ring])
    half, outer, inner = lax.optimization_barrier((half, outer, inner))
    half_mate = lax.ppermute(half, "c", swap)
    fields, middle_iter, *matrices = call(
        smooth_kernel,
        [(4, 5, 16, 128), (5, 16, 128)]
        + [(shape, jnp.bfloat16) for shape in ((384, 256), (128, 128), (128, 256))],
        one, mate, outer, inner,
    )
    (result,) = call(
        last_kernel, [source.shape],
        half, half_mate, *matrices, fields, middle_iter, fine_fields, fine_iter,
        scratch=[(2 * chips + 4, 8, 128)] + [(2 * chips, 8, 128)] * 2
        + [(2 * chips + 4, 8, 128)] * 2 + [(2 * chips, 8, 128)]
        + [(5 * (8 * nz + 8) + 16, 128), (4 * 24 + 16, 128)],
    )
    return result


def solution(mesh):
    ny, nx = (8, 4) if mesh.devices.shape[0] == 64 else (mesh.devices.shape[0] // 2, 1)
    nz = mesh.devices.shape[1]
    split = Mesh(mesh.devices.reshape(ny, nx, 2, nz), ("y", "x", "c", "z"))
    spec = P(("y", "x", "c"), "z", None)
    return jax.shard_map(
        shards, mesh=split, in_specs=(spec, spec, spec), out_specs=spec, check_vma=False
    )
```
